32 devices in a mesh: gx: 4 (over y, core), gy: 8 (over z, x).
Axes of the slice: x: 2, y: 2, z: 4, core: 2. Of those that a mesh axis runs over, the one named last changes fastest.
Arguments:
- source_mass: float32 [4, 1024, 1024], P(None, 'gx', 'gy'), may hold values from 0.1 to 2
- target_density: float32 [4, 1024, 1024], P(None, 'gx', 'gy'), may hold values from 0.25 to 4
- potential: float32 [4, 1024, 1024], P(None, 'gx', 'gy'), may hold values from -6 to 6
- dest_device: int32 [4, 8, 128, 4], P('gx', 'gy'), may hold values from 0 to 31, all different within a row; in each aligned block of 128 rows (0 to 127, 128 to 255, ..., all dimensions but the last counted through in order) at most 24 rows name the same one
- dest_tile: int32 [4, 8, 128, 4], P('gx', 'gy'), may hold values from 0 to 127
- mass_counts: int32 [4, 8, 128, 4], P('gx', 'gy'), may hold values from 1 to 8
- reach: float32 [4], replicated, may hold values from 2 to 8192
Outputs:
- pushed: float32 [4, 1024, 1024], P(None, 'gx', 'gy')
- potential_next: float32 [4, 1024, 1024], P(None, 'gx', 'gy')
The draws below stay inside these ranges and needn't reach their ends.
Inputs may be any that keep to these rules, and one draw needn't show every extreme that they name: `dest_device`: within one block's 128 x 4 entries no destination block is named more than 24 times, and in some blocks one is named exactly 24 times; the 4 entries of one source tile name different blocks.
All inputs are finite; a program needn't handle non-finite values.
Results may differ from the reference program's by a relative error of at most 0.0001.
Values sent between devices are 32-bit elements; how exact they have to be, the bound alone decides.
No kernel may reach another device: no remote copies, remote signals or barrier semaphores. Data moves between devices by JAX's collectives and lax.ppermute only.
A program may use at most 64 MiB of HBM per device.

```python
import math
import jax
import jax.numpy as jnp
import numpy as np
from jax import lax

NZ = 4
CX = 256
CY = 128
TS = 16
K = 4
TILES_DEV = 128
SLOTS = 24
NX = 1024
NY = 1024
N_GX = 4
N_GY = 8


def draw_reach(key, part):
    key_order = jax.random.fold_in(key, 11)
    key_short = jax.random.fold_in(key, 12)
    key_long = jax.random.fold_in(key, 13)
    order = jax.random.permutation(key_order, NZ)
    slow = order < NZ // 2
    short_reach = jnp.exp(jax.random.uniform(key_short, (NZ,), jnp.float32, jnp.log(2.0), jnp.log(40.0)))
    long_reach = jnp.exp(jax.random.uniform(key_long, (NZ,), jnp.float32, jnp.log(0.5 * NX), jnp.log(8.0 * NX)))
    return jnp.where(slow, long_reach, short_reach).astype(jnp.float32)


def touch_ends(result, own_key, low, top_value):
    longest = result.shape.index(max(result.shape))
    spots = []
    for shift in (0, 1):
        where = [jax.random.randint(jax.random.fold_in(own_key, axis), (), 0, length) for axis, length in enumerate(result.shape)]
        where[longest] = (where[longest] + shift) % result.shape[longest]
        spots.append(tuple(where))
    return result.at[spots[0]].set(low).at[spots[1]].set(top_value)


def levels(own_key, dims, cuts, smallest, top_value):
    loudness = 1.0
    for position, parts in cuts:
        heights = jax.random.uniform(jax.random.fold_in(jax.random.fold_in(own_key, 6), position), (parts,), jnp.float32, smallest / len(cuts), top_value / len(cuts))
        loudness = loudness * jnp.repeat(jnp.exp(heights), dims[position] // parts).reshape((-1,) + (1,) * (len(dims) - 1 - position))
    return loudness


def shared_out(key, own, number, rows, count, top, most, slope):
    sequence = jax.random.permutation(key, count)
    crowded, common = load_shares(count, rows * top, most, slope, True), load_shares(count, rows * top, most, slope, False)
    places = jnp.arange(count)

    def named(sizes, offset_by):
        used = int((sizes > 0).sum())
        fixed = max(1, used // 4)
        moved = fixed + (places - fixed + offset_by * (used - fixed)) % max(1, count - fixed)
        return jnp.zeros((count,), jnp.int32).at[sequence[jnp.where(places < fixed, places, moved)]].set(jnp.asarray(sizes, jnp.int32))

    sizes = jnp.where(number % 4 == 0, named(crowded, number // 4), named(common, number - number // 4 - 1))
    mixed = jax.random.permutation(jax.random.fold_in(own, 3), count)
    giver, receiver = mixed[0:count // 2 * 2:2], mixed[1:count // 2 * 2:2]
    margin = jnp.minimum(sizes[giver] - 1, most - sizes[receiver]) // 2
    margin = jnp.where((giver == sequence[0]) | (receiver == sequence[0]) | (sizes[receiver] == 0), 0, jnp.maximum(margin, 0))
    moved = jax.random.randint(jax.random.fold_in(own, 4), (count // 2,), 0, 1 << 20) % (margin + 1)
    sizes = sizes.at[giver].add(-moved).at[receiver].add(moved)
    items = jnp.searchsorted(jnp.cumsum(sizes), jnp.arange(rows * top), side="right").astype(jnp.int32)
    listing = items.reshape(top, rows).T
    listing = listing[jax.random.permutation(jax.random.fold_in(own, 1), rows)]
    offset_by = jax.random.randint(jax.random.fold_in(own, 2), (rows, 1), 0, top)
    return jnp.take_along_axis(listing, (jnp.arange(top)[None, :] + offset_by) % top, axis=1)


def load_shares(amount, total, most, lean, full):
    loads = [(1 << 20) // math.isqrt(standing ** lean) + 1 for standing in range(1, amount + 1)]
    largest = most if full else min(most, max(-(-total // amount), total * loads[0] // sum(loads)))
    least = 1 if total - largest >= amount - 1 else 0
    holding, rest = [largest] + [least] * (amount - 1), total - largest - least * (amount - 1)
    while rest > 0:
        movable = [i for i in range(1, amount) if holding[i] < largest] or [i for i in range(1, amount) if holding[i] < most]
        whole, remaining = sum([loads[i] for i in movable]), rest
        for i in movable:
            extra = min(most - holding[i], max(1, remaining * loads[i] // whole), rest)
            holding[i] = holding[i] + extra
            rest = rest - extra
    return np.array(holding)


def normal_values(rng, extent, width, most, pieces=(), dtype=jnp.bfloat16):
    entries = jax.random.normal(rng, extent, jnp.float32) * width
    if len(pieces) > 0:
        entries = levels(rng, extent, pieces, -0.22, 0.18) * entries
    return jnp.clip(entries, min=-most, max=most).astype(dtype)


def setup_inputs(seed: int = 0) -> dict:
    key_list = jax.random.split(jax.random.key(seed), 8)
    source_mass = jnp.clip(jnp.exp(math.log(2.0) - 2.9957323 * jax.random.uniform(key_list[0], (NZ, NX, NY), jnp.float32) ** levels(key_list[0], (NZ, NX, NY), ((1, 4), (2, 8)), -0.2, 0.2)), 0.1, 2.0)
    target_density = jnp.clip(jnp.exp(math.log(4.0) - 2.7725887 * jax.random.uniform(key_list[1], (NZ, NX, NY), jnp.float32) ** levels(key_list[1], (NZ, NX, NY), ((1, 4), (2, 8)), -0.2, 0.2)), 0.25, 4.0)
    potential = normal_values(key_list[2], (NZ, NX, NY), 1.0, 6.0, ((1, 4), (2, 8)), jnp.float32)
    dest_device_keys = jax.random.split(jax.random.fold_in(key_list[3], 1), N_GX * N_GY * TILES_DEV // TILES_DEV)
    dest_device_turns = jax.random.permutation(jax.random.fold_in(key_list[3], 3), N_GX * N_GY * TILES_DEV // TILES_DEV)
    dest_device = jax.vmap(lambda own, number: shared_out(jax.random.fold_in(key_list[3], 2), own, number, TILES_DEV, N_GX * N_GY, K, SLOTS, 2))(dest_device_keys, dest_device_turns).reshape((N_GX, N_GY, TILES_DEV, K))
    dest_tile = touch_ends(jax.random.randint(key_list[4], (N_GX, N_GY, TILES_DEV, K), 0, TILES_DEV), jax.random.fold_in(key_list[4], 1), 0, TILES_DEV - 1).astype(jnp.int32)
    mass_counts = touch_ends(jax.random.randint(key_list[5], (N_GX, N_GY, TILES_DEV, K), 1, 9), jax.random.fold_in(key_list[5], 1), 1, 8).astype(jnp.int32)
    reach = draw_reach(jax.random.fold_in(key_list[7], 71), 0)
    return {"source_mass": source_mass, "target_density": target_density, "potential": potential, "dest_device": dest_device, "dest_tile": dest_tile, "mass_counts": mass_counts, "reach": reach}


def line_pass(lines, decay):
    scale = (1.0 - decay) ** 2

    def ahead(carry, value):
        fresh = value + decay * carry
        return fresh, fresh

    def behind(carry, value):
        fresh = scale * value + decay * carry
        return fresh, fresh

    _, forward = lax.scan(ahead, jnp.zeros_like(lines[0]), lines)
    _, backward = lax.scan(behind, jnp.zeros_like(lines[0]), forward, reverse=True)
    return backward


def reference(source_mass, target_density, potential, dest_device, dest_tile, mass_counts, reach):
    tiles_x = CX // TS
    tiles_y = CY // TS
    total_tiles = N_GX * N_GY * TILES_DEV
    tiles = source_mass.reshape(NZ, N_GX, tiles_x, TS, N_GY, tiles_y, TS)
    tiles = tiles.transpose(1, 4, 2, 5, 0, 3, 6).reshape(total_tiles, NZ * TS * TS)
    counts = mass_counts.astype(jnp.float32)
    shares = (counts / jnp.sum(counts, axis=-1, keepdims=True)).reshape(total_tiles, K)
    target_index = (dest_device * TILES_DEV + dest_tile).reshape(total_tiles, K).astype(jnp.int32)
    pushed_tiles = jnp.zeros_like(tiles)
    for entry in range(K):
        pushed_tiles = pushed_tiles + jax.ops.segment_sum(tiles * shares[:, entry:entry + 1], target_index[:, entry], num_segments=total_tiles)
    pushed = pushed_tiles.reshape(N_GX, N_GY, tiles_x, tiles_y, NZ, TS, TS)
    pushed = pushed.transpose(4, 0, 2, 5, 1, 3, 6).reshape(NZ, NX, NY)
    mismatch = target_density - pushed
    decay = (1.0 - 1.0 / reach)[:, None]
    smoothed_x = line_pass(mismatch.transpose(1, 0, 2), decay).transpose(1, 0, 2)
    correction = line_pass(smoothed_x.transpose(2, 0, 1), decay).transpose(1, 2, 0)
    return pushed, potential + correction
```

```python
import functools

import jax
import jax.numpy as jnp
from jax import lax
from jax.experimental import pallas as pl
from jax.experimental.pallas import tpu as pltpu
from jax.sharding import Mesh
from jax.sharding import PartitionSpec as P

TS = 16
SUB = 8
LANES = 128
F32 = jnp.float32
BF16 = jnp.bfloat16
VMEM_LIMIT = 48 * 1024 * 1024


def split(x):
    high = x.astype(BF16)
    return high, (x - high.astype(F32)).astype(BF16)


def mm(a, b):
    return jnp.dot(a, b, preferred_element_type=F32)


def mm_t(a, b):
    return lax.dot_general(a, b, (((0,), (0,)), ((), ())), preferred_element_type=F32)


def dot3(a, b):
    a_high, a_low = split(a)
    b_high, b_low = split(b)
    return mm(a_high, b_high) + mm(a_high, b_low) + mm(a_low, b_high)


def swap_blocks(x):
    rows = x.shape[0]
    x = x.reshape(rows // SUB, SUB, LANES)
    sub = lax.broadcasted_iota(jnp.int32, x.shape, 1)
    block = lax.broadcasted_iota(jnp.int32, x.shape, 2) // TS
    for k in (4, 2, 1):
        up = pltpu.roll(pltpu.roll(x, SUB - k, 1), TS * k, 2)
        down = up if 2 * k == SUB else pltpu.roll(pltpu.roll(x, k, 1), LANES - TS * k, 2)
        moved = jnp.where((sub & k) == 0, up, down)
        x = jnp.where((sub & k) == (block & k), x, moved)
    return x.reshape(rows, LANES)


def tile_columns(tiled, planes, tiles_x):
    grouped = tiled.reshape(planes, tiles_x, 2, SUB, LANES)
    columns = [grouped[z, :, h].reshape(tiles_x * SUB, LANES) for z in range(planes) for h in range(2)]
    return jnp.concatenate(columns, axis=1)


def tile_rows(columns, planes, tiles_x):
    parts = [
        columns[:, i * LANES:(i + 1) * LANES].reshape(1, tiles_x, 1, SUB, LANES) for i in range(2 * planes)
    ]
    planes_of = [jnp.concatenate(parts[2 * z:2 * z + 2], axis=2) for z in range(planes)]
    return jnp.concatenate(planes_of, axis=0).reshape(planes * tiles_x * TS, LANES)


def route_rows(names, tiles, shares, wanted):
    fanout, count = names.shape
    member = jnp.zeros(wanted.shape, F32)
    weight = jnp.zeros(wanted.shape, F32)
    label = jnp.zeros(wanted.shape, F32)
    for k in range(fanout):
        hit = names[k:k + 1, :] == wanted
        member = member + jnp.where(hit, 1.0, 0.0)
        weight = weight + jnp.where(hit, shares[k:k + 1, :], 0.0)
        label = label + jnp.where(hit, tiles[k:k + 1, :], 0.0)
    before = lax.broadcasted_iota(jnp.int32, (count, count), 0) < lax.broadcasted_iota(
        jnp.int32, (count, count), 1
    )
    rank = mm(member.astype(BF16), jnp.where(before, 1.0, 0.0).astype(BF16))
    return jnp.where(member > 0.0, rank, 2.0 * count), weight, label


def slots_of(rank, weight, label, capacity):
    slot = lax.broadcasted_iota(jnp.int32, (capacity, rank.shape[1]), 0).astype(F32)
    chosen = rank == slot
    picked = jnp.where(chosen, weight, 0.0)
    labels = jnp.sum(jnp.where(chosen, label, 0.0), axis=1, keepdims=True)
    return picked, labels


def place_labels(board, labels, first):
    lane = lax.broadcasted_iota(jnp.int32, board.shape, 1)
    for g in range(labels.shape[0] // SUB):
        board = jnp.where(lane == first + g, labels[g * SUB:(g + 1) * SUB], board)
    return board


def read_labels(board, first, capacity):
    lane = lax.broadcasted_iota(jnp.int32, (SUB, LANES), 1).astype(F32)
    rows = [
        jnp.where(board[:, first + g:first + g + 1] == lane, 1.0, 0.0) for g in range(capacity // SUB)
    ]
    return jnp.concatenate(rows, axis=0)


def start_kernel(capacity, columns, depth, planes_a, source, names_in, tiles_in, counts_in, wanted, ring_out,
                 pack_out, picked):
    planes, cells_x, _ = source.shape
    tiles_x = cells_x // TS
    tile_count, fanout = names_in.shape
    names = names_in[...].astype(F32).T
    tiles = tiles_in[...].astype(F32).T
    counts = counts_in[...].astype(F32).T
    shares = counts / jnp.sum(counts, axis=0, keepdims=True)
    half = planes_a * cells_x
    ring_out[:half, :] = swap_blocks(source[:planes_a].reshape(half, LANES))
    ring_out[half:, :] = jnp.zeros((ring_out.shape[0] - half, LANES), F32)
    ring_out[half:half + fanout, :] = names
    ring_out[half + SUB:half + SUB + fanout, :] = tiles
    ring_out[half + 2 * SUB:half + 2 * SUB + fanout, :] = shares
    rank, weight, label = route_rows(names, tiles, shares, wanted[...])
    for j in range(columns):
        board = jnp.zeros((SUB, LANES), F32)
        for r in range(depth):
            n = j * depth + r
            rows, labels = slots_of(rank[n:n + 1], weight[n:n + 1], label[n:n + 1], capacity)
            picked[n * capacity:(n + 1) * capacity, :] = rows
            board = place_labels(board, labels, r * (capacity // SUB))
        pack_out[j, depth * capacity:, :] = jnp.zeros((SUB, pack_out.shape[2]), F32)
        pack_out[j, depth * capacity:, :LANES] = board
    rest = planes - planes_a
    cells = swap_blocks(source[planes_a:].reshape(rest * cells_x, LANES))
    packed = dot3(picked[...], tile_columns(cells, rest, tiles_x))
    pack_out[:, :depth * capacity, :] = packed.reshape(columns, depth * capacity, packed.shape[1])


def forward_kernel(capacity, columns, depth, planes_a, fanout, wanted, *refs):
    rings, pack_out, picked = refs[:depth], refs[depth], refs[depth + 1]
    half = rings[0].shape[0] - 3 * SUB
    tiles_x = half // planes_a // TS
    boards = [jnp.zeros((SUB, LANES), F32) for _ in range(columns)]
    for s in range(depth):
        ring = rings[s]
        names = ring[half:half + fanout, :]
        tiles = ring[half + SUB:half + SUB + fanout, :]
        shares = ring[half + 2 * SUB:half + 2 * SUB + fanout, :]
        rank, weight, label = route_rows(names, tiles, shares, wanted[...])
        for j in range(columns):
            rows, labels = slots_of(rank[j:j + 1], weight[j:j + 1], label[j:j + 1], capacity)
            picked[j * capacity:(j + 1) * capacity, :] = rows
            boards[j] = place_labels(boards[j], labels, s * (capacity // SUB))
        packed = dot3(picked[...], tile_columns(ring[:half, :], planes_a, tiles_x))
        pack_out[:, s * capacity:(s + 1) * capacity, :] = packed.reshape(columns, capacity, packed.shape[1])
    for j in range(columns):
        pack_out[j, depth * capacity:, :] = jnp.zeros((SUB, pack_out.shape[2]), F32)
        pack_out[j, depth * capacity:, :LANES] = boards[j]


def gather_sum(arrived, capacity, groups):
    columns, rows, _ = arrived.shape
    total = rows - SUB
    heads, cells = [], []
    for j in range(columns):
        board = arrived[j, total:, :LANES]
        for g in groups:
            heads.append(read_labels(board, g * (capacity // SUB), capacity))
            cells.append(arrived[j, g * capacity:(g + 1) * capacity, :])
    head = jnp.concatenate(heads, axis=0).astype(BF16)
    high, low = split(jnp.concatenate(cells, axis=0))
    return mm_t(head, high) + mm_t(head, low)


def partial_kernel(capacity, depth, arrived, *outs):
    for r in range(depth):
        outs[r][...] = gather_sum(arrived, capacity, [r])


def pushed_kernel(capacity, depth, planes_a, arrived, ring_sum, own_sum, pushed_out):
    planes, cells_x, _ = pushed_out.shape
    tiles_x = cells_x // TS
    first = gather_sum(arrived, capacity, list(range(depth)))
    rows = swap_blocks(tile_rows(first, planes_a, tiles_x))
    pushed_out[:planes_a] = rows.reshape(planes_a, cells_x, LANES)
    rest = planes - planes_a
    rows = swap_blocks(tile_rows(ring_sum[...] + own_sum[...], rest, tiles_x))
    pushed_out[planes_a:] = rows.reshape(rest, cells_x, LANES)


def call(body, out_shape, scratch=()):
    return pl.pallas_call(
        body,
        out_shape=out_shape,
        scratch_shapes=list(scratch),
        compiler_params=pltpu.CompilerParams(vmem_limit_bytes=VMEM_LIMIT),
    )


def line_tables(reach, length):
    decay = 1.0 - 1.0 / reach
    logs = jnp.log(decay)[:, None, None]
    rows = lax.broadcasted_iota(F32, (1, length, length), 1)
    cols = lax.broadcasted_iota(F32, (1, length, length), 2)
    spacing = rows - cols
    lower = jnp.where(spacing >= 0.0, jnp.exp(jnp.maximum(spacing, 0.0) * logs), 0.0)
    place = lax.broadcasted_iota(F32, (1, length), 1)
    rise = jnp.exp((place + 1.0) * logs[:, :, 0])
    fall = jnp.exp((length - place) * logs[:, :, 0])
    across = jnp.exp(length * logs[:, :, 0])
    scale = ((1.0 - decay) ** 2)[:, None, None]
    both = scale * jnp.einsum("zki,zkj->zij", lower, lower, precision=lax.Precision.HIGHEST)
    bend = scale[:, :, 0] * jnp.einsum("zki,zk->zi", lower, rise, precision=lax.Precision.HIGHEST)
    return lower[:, -1, :], both, bend, fall, across


def entering(ends, across, position, count, reverse):
    total = jnp.zeros_like(ends[0])
    for k in range(count):
        at = count - 1 - k if reverse else k
        reached = at > position if reverse else at < position
        total = jnp.where(reached, across * total + ends[at], total)
    return total


def neighbours(across, ends, starts, gain, position, count):
    forward = entering(ends, across, position, count, False)
    running = jnp.zeros_like(ends[0])
    full = []
    for k in range(count):
        full.append(starts[k] + gain * running)
        running = across * running + ends[k]
    return forward, entering(jnp.stack(full), across, position, count, True)


def per_device(source_mass, target_density, potential, dest_device, dest_tile, mass_counts, reach):
    planes, cells_x, cells_y = source_mass.shape
    tile_count, fanout = dest_device.shape[2:]
    grid_x, depth, inner = lax.axis_size("gx"), lax.axis_size("z"), lax.axis_size("x")
    columns = grid_x * inner
    device_count = columns * depth
    capacity = max(2, 3 * fanout * tile_count // (2 * device_count))
    capacity = -(-capacity // SUB) * SUB
    rows = depth * capacity + SUB
    planes_a = planes // 2
    tile_cells = 2 * LANES
    at_gx, at_z, at_x = lax.axis_index("gx"), lax.axis_index("z"), lax.axis_index("x")

    column = jnp.arange(columns, dtype=jnp.int32)
    level = (at_z - jnp.arange(depth, dtype=jnp.int32)) % depth
    block = (column // inner)[:, None] * (depth * inner) + level[None, :] * inner + (column % inner)[:, None]
    wanted_b = jnp.broadcast_to(block.reshape(-1, 1).astype(F32), (columns * depth, LANES))
    wanted_a = jnp.broadcast_to(block[:, :1].astype(F32), (columns, LANES))

    ring, packed_b = call(
        functools.partial(start_kernel, capacity, columns, depth, planes_a),
        (
            jax.ShapeDtypeStruct((planes_a * cells_x + 3 * SUB, LANES), F32),
            jax.ShapeDtypeStruct((columns, rows, (planes - planes_a) * tile_cells), F32),
        ),
        [pltpu.VMEM((columns * depth * capacity, tile_count), F32)],
    )(
        source_mass,
        dest_device.reshape(tile_count, fanout),
        dest_tile.reshape(tile_count, fanout),
        mass_counts.reshape(tile_count, fanout),
        wanted_b,
    )
    onward = [(i, (i + 1) % depth) for i in range(depth)]
    rings = [ring]
    for _ in range(depth - 1):
        rings.append(lax.ppermute(rings[-1], "z", onward))
    arrived_b = lax.all_to_all(packed_b, ("gx", "x"), 0, 0, tiled=True)
    packed_a = call(
        functools.partial(forward_kernel, capacity, columns, depth, planes_a, fanout),
        jax.ShapeDtypeStruct((columns, rows, planes_a * tile_cells), F32),
        [pltpu.VMEM((columns * capacity, tile_count), F32)],
    )(wanted_a, *rings)
    arrived_a = lax.all_to_all(packed_a, ("gx", "x"), 0, 0, tiled=True)
    sums = call(
        functools.partial(partial_kernel, capacity, depth),
        tuple(
            jax.ShapeDtypeStruct((tile_count, (planes - planes_a) * tile_cells), F32) for _ in range(depth)
        ),
    )(arrived_b)
    moving = sums[1 % depth]
    for r in range(2, depth + 1):
        moving = lax.ppermute(moving, "z", onward)
        if r < depth:
            moving = moving + sums[r]
    if depth == 1:
        moving = jnp.zeros_like(sums[0])
    pushed = call(
        functools.partial(pushed_kernel, capacity, depth, planes_a),
        jax.ShapeDtypeStruct(source_mass.shape, F32),
    )(arrived_a, moving, sums[0])

    last_x, both_x, bend_x, fall_x, across_x = line_tables(reach, cells_x)
    last_y, both_y, bend_y, fall_y, across_y = line_tables(reach, cells_y)
    high = lax.Precision.HIGHEST
    mismatch = target_density - pushed
    ends = jnp.einsum("zx,zxy->zy", last_x, mismatch, precision=high)
    base = jnp.einsum("zij,zjy->ziy", both_x, mismatch, precision=high)
    packed = jnp.stack([ends, base[:, 0, :]])
    packed = lax.all_gather(packed, "gx")
    forward, backward = neighbours(across_x, packed[:, 0], packed[:, 1], bend_x[:, :1], at_gx, grid_x)
    smoothed = base + bend_x[:, :, None] * forward[:, None, :] + fall_x[:, :, None] * backward[:, None, :]
    ends = jnp.einsum("zy,zxy->zx", last_y, smoothed, precision=high)
    base = jnp.einsum("zij,zxj->zxi", both_y, smoothed, precision=high)
    packed = jnp.stack([ends, base[:, :, 0]])
    everyone = depth * inner
    packed = lax.all_to_all(jnp.broadcast_to(packed[None], (everyone,) + packed.shape), ("z", "x"), 0, 0, tiled=True)
    forward, backward = neighbours(
        across_y, packed[:, 0], packed[:, 1], bend_y[:, :1], at_z * inner + at_x, everyone
    )
    correction = base + forward[:, :, None] * bend_y[:, None, :] + backward[:, :, None] * fall_y[:, None, :]
    return pushed, potential + correction


def solution(mesh):
    grid_x, grid_y = mesh.shape["gx"], mesh.shape["gy"]
    inner = grid_x // 2
    if inner < 1 or grid_y % inner:
        inner = 1
    split_mesh = Mesh(mesh.devices.reshape(grid_x, grid_y // inner, inner), ("gx", "z", "x"))
    field = P(None, "gx", ("z", "x"))
    table = P("gx", ("z", "x"), None, None)
    return jax.shard_map(
        per_device,
        mesh=split_mesh,
        in_specs=(field, field, field, table, table, table, P()),
        out_specs=(field, field),
        check_vma=False,
    )
```

```python
import functools

import jax
import jax.numpy as jnp
from jax import lax
from jax.experimental import pallas as pl
from jax.experimental.pallas import tpu as pltpu
from jax.sharding import Mesh
from jax.sharding import PartitionSpec as P

TS = 16
SUB = 8
LANES = 128
F32 = jnp.float32
BF16 = jnp.bfloat16
BYTES_A_MICRO = 3_690_000
VMEM_LIMIT = 48 * 1024 * 1024


def split(x):
    high = x.astype(BF16)
    return high, (x - high.astype(F32)).astype(BF16)


def mm(a, b):
    return jnp.dot(a, b, preferred_element_type=F32)


def mm_t(a, b):
    return lax.dot_general(a, b, (((0,), (0,)), ((), ())), preferred_element_type=F32)


def dot3(a, b):
    a_high, a_low = split(a)
    b_high, b_low = split(b)
    return mm(a_high, b_high) + mm(a_high, b_low) + mm(a_low, b_high)


def swap_blocks(x):
    rows = x.shape[0]
    x = x.reshape(rows // SUB, SUB, LANES)
    sub = lax.broadcasted_iota(jnp.int32, x.shape, 1)
    block = lax.broadcasted_iota(jnp.int32, x.shape, 2) // TS
    for k in (4, 2, 1):
        up = pltpu.roll(pltpu.roll(x, SUB - k, 1), TS * k, 2)
        down = up if 2 * k == SUB else pltpu.roll(pltpu.roll(x, k, 1), LANES - TS * k, 2)
        moved = jnp.where((sub & k) == 0, up, down)
        x = jnp.where((sub & k) == (block & k), x, moved)
    return x.reshape(rows, LANES)


def tile_columns(tiled, planes, tiles_x):
    grouped = tiled.reshape(planes, tiles_x, 2, SUB, LANES)
    columns = [grouped[z, :, h].reshape(tiles_x * SUB, LANES) for z in range(planes) for h in range(2)]
    return jnp.concatenate(columns, axis=1)


def tile_rows(columns, planes, tiles_x):
    parts = [
        columns[:, i * LANES:(i + 1) * LANES].reshape(1, tiles_x, 1, SUB, LANES) for i in range(2 * planes)
    ]
    planes_of = [jnp.concatenate(parts[2 * z:2 * z + 2], axis=2) for z in range(planes)]
    return jnp.concatenate(planes_of, axis=0).reshape(planes * tiles_x * TS, LANES)


def route_rows(names, tiles, shares, wanted):
    fanout, count = names.shape
    member = jnp.zeros(wanted.shape, F32)
    weight = jnp.zeros(wanted.shape, F32)
    label = jnp.zeros(wanted.shape, F32)
    for k in range(fanout):
        hit = names[k:k + 1, :] == wanted
        member = member + jnp.where(hit, 1.0, 0.0)
        weight = weight + jnp.where(hit, shares[k:k + 1, :], 0.0)
        label = label + jnp.where(hit, tiles[k:k + 1, :], 0.0)
    return member, weight, label


def ranked(member):
    count = member.shape[1]
    before = lax.broadcasted_iota(jnp.int32, (count, count), 0) < lax.broadcasted_iota(
        jnp.int32, (count, count), 1
    )
    rank = mm(member.astype(BF16), jnp.where(before, 1.0, 0.0).astype(BF16))
    return jnp.where(member > 0.0, rank, 2.0 * count)


def slots_of(rank, weight, label, capacity):
    slot = lax.broadcasted_iota(jnp.int32, (capacity, rank.shape[1]), 0).astype(F32)
    chosen = rank == slot
    picked = jnp.where(chosen, weight, 0.0)
    labels = jnp.sum(jnp.where(chosen, label, 0.0), axis=1, keepdims=True)
    return picked, labels


def place_labels(board, labels, first):
    lane = lax.broadcasted_iota(jnp.int32, board.shape, 1)
    for g in range(labels.shape[0] // SUB):
        board = jnp.where(lane == first + g, labels[g * SUB:(g + 1) * SUB], board)
    return board


def read_labels(board, first, capacity):
    lane = lax.broadcasted_iota(jnp.int32, (SUB, LANES), 1).astype(F32)
    rows = [
        jnp.where(board[:, first + g:first + g + 1] == lane, 1.0, 0.0) for g in range(capacity // SUB)
    ]
    return jnp.concatenate(rows, axis=0)


def turned_by(at, steps, size):
    at = at + steps
    return jnp.where(at >= size, at - size, at)


def columns_wanted(shape, depth, inner, level, steps):
    row = lax.broadcasted_iota(jnp.int32, shape, 0)
    column, steps = (row // depth, row % depth) if steps is None else (row, steps)
    level = turned_by(level, depth - steps, depth)
    return (column // inner * (depth * inner) + level * inner + column % inner).astype(F32)


def ring_kernel(planes_a, source, routes, ring, tiled):
    planes, cells_x, _ = source.shape
    half = planes_a * cells_x
    fanout = routes.shape[1]
    ring[:half, :] = swap_blocks(source[:planes_a].reshape(half, LANES))
    ring[half:, :] = jnp.zeros((3 * SUB, LANES), F32)
    ring[half:half + fanout, :] = routes[0]
    ring[half + SUB:half + SUB + fanout, :] = routes[1]
    ring[half + 2 * SUB:half + 2 * SUB + fanout, :] = routes[2] / jnp.sum(routes[2], axis=0, keepdims=True)
    tiled[...] = swap_blocks(source[planes_a:].reshape(tiled.shape[0], LANES))


def start_kernel(capacity, columns, depth, inner, planes_a, fanout, at, ring, tiled, pack_out, picked):
    cells_x = (ring.shape[0] - 3 * SUB) // planes_a
    rest = tiled.shape[0] // cells_x
    names, tiles, shares = routing(ring, fanout)
    wanted = columns_wanted((columns * depth, LANES), depth, inner, at[1], None)
    member, weight, label = route_rows(names, tiles, shares, wanted)
    rank = ranked(member)
    for j in range(columns):
        board = jnp.zeros((SUB, LANES), F32)
        for r in range(depth):
            n = j * depth + r
            rows, labels = slots_of(rank[n:n + 1], weight[n:n + 1], label[n:n + 1], capacity)
            picked[n * capacity:(n + 1) * capacity, :] = rows
            board = place_labels(board, labels, r * (capacity // SUB))
        pack_out[j, depth * capacity:, :] = jnp.zeros((SUB, pack_out.shape[2]), F32)
        pack_out[j, depth * capacity:, :LANES] = board
    packed = dot3(picked[...], tile_columns(tiled[...], rest, cells_x // TS))
    pack_out[:, :depth * capacity, :] = packed.reshape(columns, depth * capacity, packed.shape[1])


def routing(ring, fanout):
    first = ring.shape[0] - 3 * SUB
    return [ring[first + k * SUB:first + k * SUB + fanout, :] for k in range(3)]


def forward_kernel(capacity, columns, depth, inner, planes_a, fanout, at, *refs):
    rings, edges, (pack_out, picked) = refs[:depth], refs[depth:-2], refs[-2:]
    half = rings[0].shape[0] - 3 * SUB
    tiles_x = half // planes_a // TS
    boards = [jnp.zeros((SUB, LANES), F32) for _ in range(columns)]
    wanted = columns_wanted((columns, LANES), depth, inner, at[1], 0)
    for s in range(depth):
        member, weight, label = route_rows(*routing(rings[s], fanout), wanted)
        rank = ranked(member)
        for j in range(columns):
            rows, labels = slots_of(rank[j:j + 1], weight[j:j + 1], label[j:j + 1], capacity)
            picked[j * capacity:(j + 1) * capacity, :] = rows
            boards[j] = place_labels(boards[j], labels, s * (capacity // SUB))
        packed = dot3(picked[...], tile_columns(rings[s][:half, :], planes_a, tiles_x))
        pack_out[:, s * capacity:(s + 1) * capacity, :] = packed.reshape(columns, capacity, packed.shape[1])
    value = edges[0][...]
    for part in edges[1:]:
        value = value + part[...]
    for i in range(value.shape[1] // SUB):
        first = (1 + i) * LANES
        pack_out[:, depth * capacity:, first:first + LANES] = value[:, i * SUB:(i + 1) * SUB, :]
    for j in range(columns):
        pack_out[j, depth * capacity:, :LANES] = boards[j]


def gather_sum(arrived, capacity, groups):
    columns, rows, _ = arrived.shape
    total = rows - SUB
    heads, cells = [], []
    for j in range(columns):
        board = arrived[j, total:, :LANES]
        for g in groups:
            heads.append(read_labels(board, g * (capacity // SUB), capacity))
            cells.append(arrived[j, g * capacity:(g + 1) * capacity, :])
    head = jnp.concatenate(heads, axis=0).astype(BF16)
    high, low = split(jnp.concatenate(cells, axis=0))
    return mm_t(head, high) + mm_t(head, low)


def partial_kernel(capacity, arrived, *outs):
    for r, out in enumerate(outs):
        out[...] = gather_sum(arrived, capacity, [r])


def edge_sums(proj, weight, label, tiles_x, tiles_y, logs, part):
    label = label.astype(jnp.int32)
    tile_x, tile_y = label // tiles_y, label % tiles_y
    place, other, size = (tile_y, tile_x, tiles_x) if part == 0 else (tile_x, tile_y, tiles_y)
    per = tiles_y if part == 0 else tiles_x
    blocks = weight.shape[0]
    proj = proj[:, part * LANES:(part + 1) * LANES]
    owner = lax.broadcasted_iota(jnp.int32, proj.shape, 1) // TS
    row = lax.broadcasted_iota(jnp.int32, (per, weight.shape[1]), 0)
    here = [place[n:n + 1] == row for n in range(blocks)]
    planes = len(logs)
    left, right = [], []
    for kind in range(2):
        gap = (size - 1 - other if kind == 0 else other).astype(F32)
        for z in range(planes):
            value = weight * jnp.exp(gap * (TS * logs[z]))
            left.append(
                jnp.concatenate([jnp.where(here[n], value[n:n + 1], 0.0) for n in range(blocks)], axis=0)
            )
            right.append(jnp.where(owner == kind * planes + z, proj, 0.0))
    a_high, a_low = split(jnp.concatenate(left, axis=1))
    b_high, b_low = split(jnp.concatenate(right, axis=0))
    both = mm(a_high, jnp.concatenate([b_high, b_low], axis=1))
    total = both[:, :LANES] + both[:, LANES:] + mm(a_low, b_high)
    return total.reshape(blocks, per, LANES)


def line_carries(ends, starts, across, first):
    forward, full, running = [], [], jnp.zeros_like(ends[0])
    for end, start in zip(ends, starts):
        forward.append(running)
        full.append(start + first * running)
        running = across * running + end
    backward, running = [], jnp.zeros_like(ends[0])
    for start in full[::-1]:
        backward.append(running)
        running = across * running + start
    return forward, backward[::-1]


def end_start(both, gain, back):
    half = both.shape[1] // 2
    end = both[:, :half]
    return end, gain[:half] * both[:, half:] - back[:half] * end


def edge_kernel(grid_x, depth, inner, planes, fanout, at, logs_in, target, table, lines, coef, both_x, ring, tiled,
                earlier, later, *refs):
    del earlier, later
    outs, carries = refs[:-1], refs[-1]
    _, cells_x, cells_y = target.shape
    tiles_x, tiles_y = cells_x // TS, cells_y // TS
    half = ring.shape[0] - 3 * SUB
    planes_a = half // cells_x
    logs = [logs_in[z] for z in range(planes)]
    names, tiles, shares = routing(ring, fanout)
    cells = [tile_columns(ring[:half, :], planes_a, tiles_x), tile_columns(tiled[...], planes - planes_a, tiles_x)]
    proj = dot3(jnp.concatenate(cells, axis=1), table[...])
    cells = swap_blocks(target[...].reshape(planes * cells_x, LANES))
    own = dot3(tile_columns(cells, planes, tiles_x), table[...])
    tile_count = names.shape[1]
    along = depth * inner
    blocks = grid_x * along
    wanted = lax.broadcasted_iota(jnp.int32, (blocks, tile_count), 0).astype(F32)
    _, weight, label = route_rows(names, tiles, shares, wanted)
    mine = lax.broadcasted_iota(jnp.int32, (1, tile_count), 1).astype(F32)
    one = jnp.ones((1, tile_count), F32)
    here = at[0] * along + at[1] * inner + at[2]
    edges = []
    for part in range(2):
        sums = edge_sums(proj, weight, label, tiles_x, tiles_y, logs, part)
        plus = edge_sums(own, one, mine, tiles_x, tiles_y, logs, part)
        is_here = lax.broadcasted_iota(jnp.int32, sums.shape, 0) == here
        sums = jnp.where(is_here, plus, 0.0) - sums
        edges.append(swap_blocks(sums.reshape(-1, LANES)).reshape(blocks, sums.shape[1] // SUB, SUB, LANES))
    gain, across_x, first_x, back_x, across_y, first_y, back_y = [coef[i][:, :1] for i in range(7)]

    ends, starts = zip(*[
        end_start(edges[0][p * along:(p + 1) * along, 0], gain, back_x) for p in range(grid_x)
    ])
    forward, backward = line_carries(ends, starts, across_x[:planes], first_x[:planes])
    for p in range(grid_x):
        rows = jnp.concatenate([forward[p], backward[p]], axis=1).reshape(depth, inner, SUB, LANES)
        carries[:, p * inner:(p + 1) * inner, :SUB, :] = rows

    side = jnp.concatenate([edges[1][:, i] for i in range(edges[1].shape[1])], axis=2)
    flat = side.reshape(blocks * SUB, cells_x)
    local = jnp.zeros_like(flat)
    for z in range(planes):
        local = local + dot3(masked(flat, planes, z), both_x[z])
    local = local.reshape(side.shape)
    ends = jnp.sum(side * lines[0], axis=2, keepdims=True)
    starts = jnp.sum(side * lines[1], axis=2, keepdims=True)
    forward, backward = line_carries(
        [ends[p * along:(p + 1) * along] for p in range(grid_x)],
        [starts[p * along:(p + 1) * along] for p in range(grid_x)],
        across_x,
        first_x,
    )
    smooth = [
        local[p * along:(p + 1) * along] + forward[p] * lines[2] + backward[p] * lines[3] for p in range(grid_x)
    ]
    smooth = jnp.stack(smooth)
    ends, starts = zip(*[end_start(smooth[:, q], gain, back_y) for q in range(along)])
    forward, backward = line_carries(ends, starts, across_y[:planes], first_y[:planes])
    for q in range(along):
        rows = jnp.concatenate([forward[q], backward[q]], axis=1)
        for p in range(grid_x):
            for i in range(cells_x // LANES):
                carries[q // inner, p * inner + q % inner, (1 + i) * SUB:(2 + i) * SUB, :] = (
                    rows[p, :, i * LANES:(i + 1) * LANES]
                )
    for o, out in enumerate(outs):
        out[...] = carries[turned_by(at[1], o, depth)]


def masked(rows, planes, z):
    row = lax.broadcasted_iota(jnp.int32, rows.shape, 0)
    return jnp.where(row % planes == z, rows, 0.0)


def outer(a, b):
    a_high, a_low = split(a)
    b_high, b_low = split(b)
    return mm_t(a_high, b_high) + mm_t(a_high, b_low) + mm_t(a_low, b_high)


def base_kernel(target, potential, both_x, both_y, out):
    for z in range(target.shape[0]):
        out[z] = potential[z] + dot3(dot3(both_x[z], target[z]), both_y[z])


def solve(pushed, before, both_x, both_y):
    return before - dot3(dot3(both_x, pushed), both_y)


def near_kernel(capacity, depth, arrived, base, both_x, both_y, curve_x, curve_y, pushed_out, next_out, rest_out):
    planes, planes_a = base.shape[0], pushed_out.shape[0]
    cells_x = pushed_out.shape[1]
    columns, rows, width = arrived.shape
    carries = arrived[0, rows - SUB:, :]
    for j in range(1, columns):
        carries = carries + arrived[j, rows - SUB:, :]
    carry_x, carry_y = carries[:, LANES:2 * LANES], carries[:, 2 * LANES:2 * LANES + cells_x]
    total = gather_sum(arrived, capacity, list(range(depth)))
    pushed = swap_blocks(tile_rows(total, planes_a, cells_x // TS)).reshape(planes_a, cells_x, LANES)
    pushed_out[...] = pushed
    for z in range(planes):
        left = jnp.concatenate([masked(curve_x[...], planes, z), masked(carry_y, planes, z)], axis=0)
        right = jnp.concatenate([dot3(carry_x, both_y[z]), curve_y[...]], axis=0)
        before = base[z] + outer(left, right)
        if z < planes_a:
            next_out[z] = solve(pushed[z], before, both_x[z], both_y[z])
        else:
            rest_out[z - planes_a] = before


def far_kernel(first, pushed_in, next_in, base, both_x, both_y, *refs):
    del pushed_in, next_in
    sums, (pushed_out, next_out) = refs[:-2], refs[-2:]
    count, cells_x, _ = pushed_out.shape
    total = sums[0][...]
    for part in sums[1:]:
        total = total + part[...]
    pushed = swap_blocks(tile_rows(total, count, cells_x // TS)).reshape(count, cells_x, LANES)
    for z in range(count):
        pushed_out[z] = pushed[z]
        next_out[z] = solve(pushed[z], base[z], both_x[first + z], both_y[first + z])


def call(micros, body, out_shape, in_specs=None, scratch=(), **extra):
    if in_specs is not None:
        extra["in_specs"] = in_specs
    return pl.pallas_call(
        body,
        out_shape=out_shape,
        scratch_shapes=list(scratch),
        compiler_params=pltpu.CompilerParams(vmem_limit_bytes=VMEM_LIMIT),
        cost_estimate=pl.CostEstimate(flops=0, bytes_accessed=int(micros * BYTES_A_MICRO), transcendentals=0),
        **extra,
    )


def table_kernel(planes, decay_in, logs_in, earlier, table, lines, coef, curve_x, curve_y, both_x, both_y):
    del earlier
    row = lax.broadcasted_iota(jnp.int32, (2 * planes, LANES), 0)
    decay, rate = jnp.zeros(row.shape, F32), jnp.zeros(row.shape, F32)
    for z in range(planes):
        decay = jnp.where(row % planes == z, decay_in[z], decay)
        rate = jnp.where(row % planes == z, logs_in[z], rate)
    gain = (1.0 - decay) / (1.0 + decay)
    coef[0] = gain
    for i, (curve, both) in enumerate(((curve_x, both_x), (curve_y, both_y))):
        length = curve.shape[1]
        across = jnp.exp(length * rate)
        coef[1 + 3 * i] = across
        coef[2 + 3 * i] = gain * decay * (1.0 - across * across)
        coef[3 + 3 * i] = gain * decay * across
        slope, width, turn = rate[:, :1], gain[:, :1], (gain * decay)[:, :1]
        place = lax.broadcasted_iota(jnp.int32, curve.shape, 1).astype(F32)
        risen = jnp.exp(place * slope) - jnp.exp((2.0 * length - place) * slope)
        fall = jnp.exp((length - place) * slope)
        bend = turn * risen
        curve[...] = jnp.where(lax.broadcasted_iota(jnp.int32, curve.shape, 0) < planes, bend, fall)
        if i == 0:
            lines[0] = jnp.exp((length - 1.0 - place) * slope)
            lines[1] = width * risen
            lines[2] = bend
            lines[3] = fall
        rows = lax.broadcasted_iota(jnp.int32, (length, length), 0).astype(F32)
        cols = lax.broadcasted_iota(jnp.int32, (length, length), 1).astype(F32)
        apart, down = jnp.abs(rows - cols), length - rows[:, :1]
        for z in range(planes):
            log = logs_in[z]
            both[z] = width[z:z + 1] * (jnp.exp(apart * log) - jnp.exp(down * log) * fall[z:z + 1])
    cells = TS * TS
    shape = (cells, table.shape[1])
    row, col = lax.broadcasted_iota(jnp.int32, shape, 0), lax.broadcasted_iota(jnp.int32, shape, 1)
    along_y, kind = col // (2 * planes * TS) == 1, col // (planes * TS) % 2
    owner, cell = col // TS % planes, col % TS
    at_x, at_y = row // TS, row % TS
    summed, kept = jnp.where(along_y, at_y, at_x), jnp.where(along_y, at_x, at_y)
    steps = jnp.where(kind == 0, TS - 1 - summed, summed).astype(F32)
    for z in range(planes):
        power = jnp.exp(steps * logs_in[z])
        table[z * cells:(z + 1) * cells, :] = jnp.where((owner == z) & (kept == cell), power, 0.0)


def per_device(source_mass, target_density, potential, dest_device, dest_tile, mass_counts, reach):
    planes, cells_x, cells_y = source_mass.shape
    tile_count, fanout = dest_device.shape[2:]
    tiles_x, tiles_y = cells_x // TS, cells_y // TS
    grid_x, depth, inner = lax.axis_size("gx"), lax.axis_size("z"), lax.axis_size("x")
    columns = grid_x * inner
    device_count = columns * depth
    capacity = max(2, 3 * fanout * tile_count // (2 * device_count))
    capacity = -(-capacity // SUB) * SUB
    rows = depth * capacity + SUB
    planes_a = planes // 2
    rest = planes - planes_a
    tile_cells = 2 * LANES
    at = jnp.stack([lax.axis_index("gx"), lax.axis_index("z"), lax.axis_index("x")])
    scalars, near = pl.BlockSpec(memory_space=pltpu.SMEM), pl.BlockSpec(memory_space=pltpu.VMEM)
    far = pl.BlockSpec(memory_space=pl.ANY)

    def array(*shape):
        return jax.ShapeDtypeStruct(shape, F32)

    def turn(x, axis, steps):
        size = lax.axis_size(axis)
        return lax.ppermute(x, axis, [(i, (i + steps) % size) for i in range(size)])

    routes = jnp.stack([x.reshape(tile_count, fanout).T for x in (dest_device, dest_tile, mass_counts)])
    ring, tiled = call(
        0.8, functools.partial(ring_kernel, planes_a),
        [array(planes_a * cells_x + 3 * SUB, LANES), array(rest * cells_x, LANES)],
    )(source_mass, routes.astype(F32))
    packed_b = call(
        2.7, functools.partial(start_kernel, capacity, columns, depth, inner, planes_a, fanout),
        array(columns, rows, rest * tile_cells),
        [scalars] + [near] * 2,
        [pltpu.VMEM((columns * depth * capacity, tile_count), F32)],
    )(at, ring, tiled)
    arrived_b = lax.all_to_all(packed_b, ("gx", "x"), 0, 0, tiled=True)
    rings = [ring] + [None] * (depth - 1)
    for s in range(1, depth // 2 + 1):
        rings[s] = turn(rings[s - 1], "z", 1)
        if s < depth - s:
            rings[depth - s] = turn(rings[(depth - s + 1) % depth], "z", -1)

    decay = 1.0 - 1.0 / reach
    logs = jnp.log(decay)
    eight = 2 * planes
    table, lines, coef, curve_x, curve_y, both_x, both_y = call(
        1.2, functools.partial(table_kernel, planes),
        [
            array(planes * TS * TS, 4 * planes * TS), array(4, eight, cells_x), array(7, eight, LANES),
            array(eight, cells_x), array(eight, cells_y), array(planes, cells_x, cells_x),
            array(planes, cells_y, cells_y),
        ],
        [scalars] * 2 + [far],
    )(decay, logs, packed_b)
    edge_rows = tiles_x + tiles_y
    edges = call(
        4.7, functools.partial(edge_kernel, grid_x, depth, inner, planes, fanout),
        [array(columns, edge_rows, LANES)] * depth,
        [scalars] * 2 + [near] * 7 + [far] * 2,
        [pltpu.VMEM((depth, columns, edge_rows, LANES), F32)],
    )(at, logs, target_density, table, lines, coef, both_x, ring, tiled, rings[1], rings[-1])
    edges = [edges[0]] + [turn(edges[o], "z", o) for o in range(1, depth)]
    packed_a = call(
        1.9, functools.partial(forward_kernel, capacity, columns, depth, inner, planes_a, fanout),
        array(columns, rows, planes_a * tile_cells),
        [scalars] + [near] * (depth + len(edges)),
        [pltpu.VMEM((columns * capacity, tile_count), F32)],
    )(at, *rings, *edges)
    arrived_a = lax.all_to_all(packed_a, ("gx", "x"), 0, 0, tiled=True)
    sums = call(1.4, functools.partial(partial_kernel, capacity), [array(tile_count, rest * tile_cells)] * depth)(arrived_b)
    moving = [sums[0]] + [turn(sums[r], "z", -r) for r in range(1, depth)]
    base = call(1.3, base_kernel, array(*potential.shape))(target_density, potential, both_x, both_y)
    field = (planes_a, cells_x, cells_y)
    shapes = [array(*source_mass.shape), array(*potential.shape)]
    part = pl.BlockSpec(field, lambda i: (0, 0, 0))
    *outs, base = call(
        3.9, functools.partial(near_kernel, capacity, depth), shapes + [array(rest, cells_x, cells_y)], [near] * 6,
        out_specs=[part, part, near], grid=(1,),
    )(arrived_a, base, both_x, both_y, curve_x, curve_y)
    part = pl.BlockSpec(field, lambda i: (1, 0, 0))
    outs = call(
        1.7, functools.partial(far_kernel, planes_a), shapes, [far, far] + [near] * (3 + depth),
        out_specs=[part, part], grid=(1,), input_output_aliases={0: 0, 1: 1},
    )(*outs, base, both_x, both_y, *moving)
    return tuple(outs)


def solution(mesh):
    grid_x, grid_y = mesh.shape["gx"], mesh.shape["gy"]
    inner = grid_x // 2
    if inner < 1 or grid_y % inner:
        inner = 1
    depth = grid_y // inner
    split_mesh = Mesh(mesh.devices.reshape(grid_x, depth, inner), ("gx", "z", "x"))
    field = P(None, "gx", ("z", "x"))
    table = P("gx", ("z", "x"), None, None)
    return jax.shard_map(
        per_device,
        mesh=split_mesh,
        in_specs=(field, field, field, table, table, table, P()),
        out_specs=(field, field),
        check_vma=False,
    )
```

```python
import functools

import jax
import jax.numpy as jnp
from jax import lax
from jax.experimental import pallas as pl
from jax.experimental.pallas import tpu as pltpu
from jax.sharding import Mesh
from jax.sharding import PartitionSpec as P

TS = 16
MXU = 256
SUB = 8
LANES = 128
F32 = jnp.float32
BF16 = jnp.bfloat16
FLOPS_A_MICRO = 1_100_000_000
COST = {'ring': 0.8, 'start': 2.5, 'table': 20, 'edge': 60, 'partial': 1.4, 'sum': 1.2, 'near': 3.5, 'far': 1.6, 'base': 1, 'pack': 1.8, 'early': 1.8}
FLAG = {'edge': ('A1', 'packB'), 'table': ('ring',), 'rs2': True}
VMEM_LIMIT = 48 * 1024 * 1024


def split(x):
    high = x.astype(BF16)
    return high, (x - high.astype(F32)).astype(BF16)


def mm(a, b):
    return jnp.dot(a, b, preferred_element_type=F32)


def mm_t(a, b):
    return lax.dot_general(a, b, (((0,), (0,)), ((), ())), preferred_element_type=F32)


def beside(*parts):
    return jnp.concatenate(parts, axis=1)


def stacked(*parts):
    return jnp.concatenate(parts, axis=0)


def dot3(a, b):
    a_high, a_low = split(a)
    b_high, b_low = split(b)
    deep, wide = a.shape[1], b.shape[1]
    if 2 * deep <= MXU and 2 * wide <= MXU:
        both = mm(beside(a_high, a_low), stacked(beside(b_high, b_low), beside(b_high, jnp.zeros_like(b_low))))
        return both[:, :wide] + both[:, wide:]
    if 2 * wide <= MXU:
        both = mm(a_high, beside(b_high, b_low))
        return both[:, :wide] + both[:, wide:] + mm(a_low, b_high)
    if 2 * deep <= MXU:
        return mm(beside(a_high, a_low), stacked(b_high, b_high)) + mm(a_high, b_low)
    rows = a.shape[0]
    both = mm(stacked(a_high, a_low), b_high)
    return both[:rows] + both[rows:] + mm(a_high, b_low)


def swap_blocks(x):
    rows = x.shape[0]
    x = x.reshape(rows // SUB, SUB, LANES)
    sub = lax.broadcasted_iota(jnp.int32, x.shape, 1)
    block = lax.broadcasted_iota(jnp.int32, x.shape, 2) // TS
    for k in (4, 2, 1):
        up = pltpu.roll(pltpu.roll(x, SUB - k, 1), TS * k, 2)
        down = up if 2 * k == SUB else pltpu.roll(pltpu.roll(x, k, 1), LANES - TS * k, 2)
        moved = jnp.where((sub & k) == 0, up, down)
        x = jnp.where((sub & k) == (block & k), x, moved)
    return x.reshape(rows, LANES)


def tile_columns(tiled, planes, tiles_x):
    grouped = tiled.reshape(planes, tiles_x, 2, SUB, LANES)
    columns = [grouped[z, :, h].reshape(tiles_x * SUB, LANES) for z in range(planes) for h in range(2)]
    return jnp.concatenate(columns, axis=1)


def tile_rows(columns, planes, tiles_x):
    parts = [
        columns[:, i * LANES:(i + 1) * LANES].reshape(1, tiles_x, 1, SUB, LANES) for i in range(2 * planes)
    ]
    planes_of = [jnp.concatenate(parts[2 * z:2 * z + 2], axis=2) for z in range(planes)]
    return jnp.concatenate(planes_of, axis=0).reshape(planes * tiles_x * TS, LANES)


def route_rows(names, tiles, shares, wanted):
    fanout, count = names.shape
    member = jnp.zeros(wanted.shape, F32)
    weight = jnp.zeros(wanted.shape, F32)
    label = jnp.zeros(wanted.shape, F32)
    for k in range(fanout):
        hit = names[k:k + 1, :] == wanted
        member = member + jnp.where(hit, 1.0, 0.0)
        weight = weight + jnp.where(hit, shares[k:k + 1, :], 0.0)
        label = label + jnp.where(hit, tiles[k:k + 1, :], 0.0)
    return member, weight, label


def ranked(member):
    count = member.shape[1]
    before = lax.broadcasted_iota(jnp.int32, (count, count), 0) < lax.broadcasted_iota(
        jnp.int32, (count, count), 1
    )
    rank = mm(member.astype(BF16), jnp.where(before, 1.0, 0.0).astype(BF16))
    return jnp.where(member > 0.0, rank, 2.0 * count)


def slots_of(rank, weight, label, capacity):
    slot = lax.broadcasted_iota(jnp.int32, (capacity, rank.shape[1]), 0).astype(F32)
    chosen = rank == slot
    picked = jnp.where(chosen, weight, 0.0)
    labels = jnp.sum(jnp.where(chosen, label, 0.0), axis=1, keepdims=True)
    return picked, labels


def place_labels(board, labels, first):
    lane = lax.broadcasted_iota(jnp.int32, board.shape, 1)
    for g in range(labels.shape[0] // SUB):
        board = jnp.where(lane == first + g, labels[g * SUB:(g + 1) * SUB], board)
    return board


def read_labels(board, first, capacity):
    lane = lax.broadcasted_iota(jnp.int32, (SUB, LANES), 1).astype(F32)
    rows = [
        jnp.where(board[:, first + g:first + g + 1] == lane, 1.0, 0.0) for g in range(capacity // SUB)
    ]
    return jnp.concatenate(rows, axis=0)


def turned_by(at, steps, size):
    at = at + steps
    return jnp.where(at >= size, at - size, at)


def columns_wanted(shape, depth, inner, level, steps):
    row = lax.broadcasted_iota(jnp.int32, shape, 0)
    column, steps = (row // depth, row % depth) if steps is None else (row, steps)
    level = turned_by(level, depth - steps, depth)
    return (column // inner * (depth * inner) + level * inner + column % inner).astype(F32)


def ring_kernel(planes_a, source, routes, ring, tiled):
    planes, cells_x, _ = source.shape
    half = planes_a * cells_x
    fanout = routes.shape[1]
    ring[:half, :] = swap_blocks(source[:planes_a].reshape(half, LANES))
    ring[half:, :] = jnp.zeros((3 * SUB, LANES), F32)
    ring[half:half + fanout, :] = routes[0]
    ring[half + SUB:half + SUB + fanout, :] = routes[1]
    ring[half + 2 * SUB:half + 2 * SUB + fanout, :] = routes[2] / jnp.sum(routes[2], axis=0, keepdims=True)
    tiled[...] = swap_blocks(source[planes_a:].reshape(tiled.shape[0], LANES))


def start_kernel(capacity, columns, depth, inner, planes_a, fanout, at, ring, tiled, pack_out, picked):
    cells_x = (ring.shape[0] - 3 * SUB) // planes_a
    rest = tiled.shape[0] // cells_x
    names, tiles, shares = routing(ring, fanout)
    wanted = columns_wanted((columns * depth, LANES), depth, inner, at[1], None)
    member, weight, label = route_rows(names, tiles, shares, wanted)
    rank = ranked(member)
    for j in range(columns):
        board = jnp.zeros((SUB, LANES), F32)
        for r in range(depth):
            n = j * depth + r
            rows, labels = slots_of(rank[n:n + 1], weight[n:n + 1], label[n:n + 1], capacity)
            picked[n * capacity:(n + 1) * capacity, :] = rows
            board = place_labels(board, labels, r * (capacity // SUB))
        pack_out[j, depth * capacity:, :] = jnp.zeros((SUB, pack_out.shape[2]), F32)
        pack_out[j, depth * capacity:, :LANES] = board
    packed = dot3(picked[...], tile_columns(tiled[...], rest, cells_x // TS))
    pack_out[:, :depth * capacity, :] = packed.reshape(columns, depth * capacity, packed.shape[1])


def routing(ring, fanout):
    first = ring.shape[0] - 3 * SUB
    return [ring[first + k * SUB:first + k * SUB + fanout, :] for k in range(3)]


def forward_kernel(capacity, columns, depth, inner, planes_a, fanout, count, at, *refs):
    rings, edges, (pack_out, picked) = refs[:count], refs[count:-2], refs[-2:]
    half = rings[0].shape[0] - 3 * SUB
    tiles_x = half // planes_a // TS
    boards = [jnp.zeros((SUB, LANES), F32) for _ in range(columns)]
    wanted = columns_wanted((columns, LANES), depth, inner, at[1], 0)
    for s, ring in enumerate(rings):
        member, weight, label = route_rows(*routing(ring, fanout), wanted)
        rank = ranked(member)
        for j in range(columns):
            rows, labels = slots_of(rank[j:j + 1], weight[j:j + 1], label[j:j + 1], capacity)
            picked[j * capacity:(j + 1) * capacity, :] = rows
            boards[j] = place_labels(boards[j], labels, s * (capacity // SUB))
        packed = dot3(picked[...], tile_columns(ring[:half, :], planes_a, tiles_x))
        pack_out[:, s * capacity:(s + 1) * capacity, :] = packed.reshape(columns, capacity, packed.shape[1])
    if edges:
        value = edges[0][...]
        for part in edges[1:]:
            value = value + part[...]
        for i in range(value.shape[1] // SUB):
            first = (1 + i) * LANES
            pack_out[:, count * capacity:, first:first + LANES] = value[:, i * SUB:(i + 1) * SUB, :]
    else:
        pack_out[:, count * capacity:, :] = jnp.zeros((columns, SUB, pack_out.shape[2]), F32)
    for j in range(columns):
        pack_out[j, count * capacity:, :LANES] = boards[j]


def gather_sum(arrived, capacity, groups):
    columns, rows, _ = arrived.shape
    total = rows - SUB
    heads, cells = [], []
    for j in range(columns):
        board = arrived[j, total:, :LANES]
        for g in groups:
            heads.append(read_labels(board, g * (capacity // SUB), capacity))
            cells.append(arrived[j, g * capacity:(g + 1) * capacity, :])
    head = jnp.concatenate(heads, axis=0).astype(BF16)
    high, low = split(jnp.concatenate(cells, axis=0))
    return mm_t(head, high) + mm_t(head, low)


def partial_kernel(capacity, arrived, *outs):
    for r, out in enumerate(outs):
        out[...] = gather_sum(arrived, capacity, [r])


def edge_sums(proj, weight, label, tiles_x, tiles_y, logs, part):
    label = label.astype(jnp.int32)
    tile_x, tile_y = label // tiles_y, label % tiles_y
    place, other, size = (tile_y, tile_x, tiles_x) if part == 0 else (tile_x, tile_y, tiles_y)
    per = tiles_y if part == 0 else tiles_x
    blocks = weight.shape[0]
    proj = proj[:, part * LANES:(part + 1) * LANES]
    owner = lax.broadcasted_iota(jnp.int32, proj.shape, 1) // TS
    row = lax.broadcasted_iota(jnp.int32, (per, weight.shape[1]), 0)
    here = [place[n:n + 1] == row for n in range(blocks)]
    planes = len(logs)
    left, right = [], []
    for kind in range(2):
        gap = (size - 1 - other if kind == 0 else other).astype(F32)
        for z in range(planes):
            value = weight * jnp.exp(gap * (TS * logs[z]))
            left.append(stacked(*[jnp.where(here[n], value[n:n + 1], 0.0) for n in range(blocks)]))
            right.append(jnp.where(owner == kind * planes + z, proj, 0.0))
    return dot3(beside(*left), stacked(*right)).reshape(blocks, per, LANES)


def own_edges(proj, tiles_x, tiles_y, logs):
    lane = lax.broadcasted_iota(jnp.int32, (SUB, LANES), 1) // TS
    sub = lax.broadcasted_iota(jnp.int32, (SUB, LANES), 0)
    planes = len(logs)
    rate = jnp.zeros((SUB, LANES), F32)
    for z in range(planes):
        rate = jnp.where(lane % planes == z, TS * logs[z], rate)
    to_end = lane < planes
    near = jnp.exp(jnp.where(to_end, tiles_y - 1 - sub, sub).astype(F32) * rate)
    along_x, along_y = jnp.zeros((SUB, LANES), F32), []
    for i in range(tiles_x):
        rows = proj[i * tiles_y:(i + 1) * tiles_y]
        steps = jnp.where(to_end, tiles_x - 1 - i, i).astype(F32)
        along_x = along_x + rows[:, :LANES] * jnp.exp(steps * rate)
        along_y.append(jnp.sum(rows[:, LANES:] * near, axis=0, keepdims=True))
    return along_x[None], stacked(*along_y)[None]


def line_carries(ends, starts, across, first):
    forward, full, running = [], [], jnp.zeros_like(ends[0])
    for end, start in zip(ends, starts):
        forward.append(running)
        full.append(start + first * running)
        running = across * running + end
    backward, running = [], jnp.zeros_like(ends[0])
    for start in full[::-1]:
        backward.append(running)
        running = across * running + start
    return forward, backward[::-1]


def end_start(both, gain, back):
    half = both.shape[1] // 2
    end = both[:, :half]
    return end, gain[:half] * both[:, half:] - back[:half] * end


def edge_kernel(grid_x, depth, inner, planes, fanout, at, logs_in, target, table, lines, coef, both_x, ring, tiled,
                *refs):
    outs, carries = refs[:-1], refs[-1]
    _, cells_x, cells_y = target.shape
    tiles_x, tiles_y = cells_x // TS, cells_y // TS
    half = ring.shape[0] - 3 * SUB
    planes_a = half // cells_x
    logs = [logs_in[z] for z in range(planes)]
    names, tiles, shares = routing(ring, fanout)
    cells = [tile_columns(ring[:half, :], planes_a, tiles_x), tile_columns(tiled[...], planes - planes_a, tiles_x)]
    cells = beside(*cells)
    own_cells = tile_columns(swap_blocks(target[...].reshape(planes * cells_x, LANES)), planes, tiles_x)
    proj = dot3(stacked(cells, own_cells), table[...])
    own = own_edges(proj[cells.shape[0]:], tiles_x, tiles_y, logs)
    proj = proj[:cells.shape[0]]
    tile_count = names.shape[1]
    along = depth * inner
    blocks = grid_x * along
    wanted = lax.broadcasted_iota(jnp.int32, (blocks, tile_count), 0).astype(F32)
    _, weight, label = route_rows(names, tiles, shares, wanted)
    here = at[0] * along + at[1] * inner + at[2]
    edges = []
    for part in range(2):
        sums = edge_sums(proj, weight, label, tiles_x, tiles_y, logs, part)
        is_here = lax.broadcasted_iota(jnp.int32, sums.shape, 0) == here
        sums = jnp.where(is_here, own[part], 0.0) - sums
        edges.append(swap_blocks(sums.reshape(-1, LANES)).reshape(blocks, sums.shape[1] // SUB, SUB, LANES))
    gain, across_x, first_x, back_x, across_y, first_y, back_y = [coef[i][:, :1] for i in range(7)]

    ends, starts = zip(*[
        end_start(edges[0][p * along:(p + 1) * along, 0], gain, back_x) for p in range(grid_x)
    ])
    forward, backward = line_carries(ends, starts, across_x[:planes], first_x[:planes])
    for p in range(grid_x):
        rows = jnp.concatenate([forward[p], backward[p]], axis=1).reshape(depth, inner, SUB, LANES)
        carries[:, p * inner:(p + 1) * inner, :SUB, :] = rows

    side = jnp.concatenate([edges[1][:, i] for i in range(edges[1].shape[1])], axis=2)
    flat = side.reshape(blocks * SUB, cells_x)
    local = jnp.zeros_like(flat)
    for z in range(planes):
        local = local + dot3(masked(flat, planes, z), both_x[z])
    local = local.reshape(side.shape)
    ends = jnp.sum(side * lines[0], axis=2, keepdims=True)
    starts = jnp.sum(side * lines[1], axis=2, keepdims=True)
    forward, backward = line_carries(
        [ends[p * along:(p + 1) * along] for p in range(grid_x)],
        [starts[p * along:(p + 1) * along] for p in range(grid_x)],
        across_x,
        first_x,
    )
    smooth = [
        local[p * along:(p + 1) * along] + forward[p] * lines[2] + backward[p] * lines[3] for p in range(grid_x)
    ]
    smooth = jnp.stack(smooth)
    ends, starts = zip(*[end_start(smooth[:, q], gain, back_y) for q in range(along)])
    forward, backward = line_carries(ends, starts, across_y[:planes], first_y[:planes])
    for q in range(along):
        rows = jnp.concatenate([forward[q], backward[q]], axis=1)
        for p in range(grid_x):
            for i in range(cells_x // LANES):
                carries[q // inner, p * inner + q % inner, (1 + i) * SUB:(2 + i) * SUB, :] = (
                    rows[p, :, i * LANES:(i + 1) * LANES]
                )
    for o, out in enumerate(outs):
        out[...] = carries[turned_by(at[1], o, depth)]


def masked(rows, planes, z):
    row = lax.broadcasted_iota(jnp.int32, rows.shape, 0)
    return jnp.where(row % planes == z, rows, 0.0)


def outer(a, b):
    a_high, a_low = split(a)
    b_high, b_low = split(b)
    return mm_t(stacked(a_high, a_high, a_low), stacked(b_high, b_low, b_high))


def base_kernel(target, potential, both_x, both_y, out):
    for z in range(target.shape[0]):
        out[z] = potential[z] + dot3(dot3(both_x[z], target[z]), both_y[z])


def solve(pushed, before, both_x, both_y):
    return before - dot3(dot3(both_x, pushed), both_y)


def sum_kernel(capacity, count, arrived, out):
    out[...] = gather_sum(arrived, capacity, list(range(count)))


def near_kernel(capacity, count, arrived, base, both_x, both_y, curve_x, curve_y, *refs):
    earlier, (pushed_out, next_out, rest_out) = refs[:-3], refs[-3:]
    planes, planes_a = base.shape[0], pushed_out.shape[0]
    cells_x = pushed_out.shape[1]
    columns, rows, width = arrived.shape
    carries = arrived[0, rows - SUB:, :]
    for j in range(1, columns):
        carries = carries + arrived[j, rows - SUB:, :]
    carry_x, carry_y = carries[:, LANES:2 * LANES], carries[:, 2 * LANES:2 * LANES + cells_x]
    total = gather_sum(arrived, capacity, list(range(count)))
    for part in earlier:
        total = total + part[...]
    pushed = swap_blocks(tile_rows(total, planes_a, cells_x // TS)).reshape(planes_a, cells_x, LANES)
    pushed_out[...] = pushed
    for z in range(planes):
        left = jnp.concatenate([masked(curve_x[...], planes, z), masked(carry_y, planes, z)], axis=0)
        right = jnp.concatenate([dot3(carry_x, both_y[z]), curve_y[...]], axis=0)
        before = base[z] + outer(left, right)
        if z < planes_a:
            next_out[z] = solve(pushed[z], before, both_x[z], both_y[z])
        else:
            rest_out[z - planes_a] = before


def far_kernel(first, pushed_in, next_in, base, both_x, both_y, *refs):
    del pushed_in, next_in
    sums, (pushed_out, next_out) = refs[:-2], refs[-2:]
    count, cells_x, _ = pushed_out.shape
    total = sums[0][...]
    for part in sums[1:]:
        total = total + part[...]
    pushed = swap_blocks(tile_rows(total, count, cells_x // TS)).reshape(count, cells_x, LANES)
    for z in range(count):
        pushed_out[z] = pushed[z]
        next_out[z] = solve(pushed[z], base[z], both_x[first + z], both_y[first + z])


def call(name, body, out_shape, in_specs=None, scratch=(), wait=(), **extra):
    def run(*args):
        count, unread = len(args), len(wait)

        def kernel(*refs):
            body(*refs[:count], *refs[count + unread:])

        near = pl.BlockSpec(memory_space=pltpu.VMEM)
        specs = [near] * count if in_specs is None else list(in_specs)
        return pl.pallas_call(
            kernel,
            out_shape=out_shape,
            in_specs=specs + [pl.BlockSpec(memory_space=pl.ANY)] * unread,
            scratch_shapes=list(scratch),
            compiler_params=pltpu.CompilerParams(vmem_limit_bytes=VMEM_LIMIT),
            cost_estimate=pl.CostEstimate(
                flops=int(COST[name] * FLOPS_A_MICRO), bytes_accessed=0, transcendentals=0
            ),
            **extra,
        )(*args, *wait)

    return run


def table_kernel(planes, decay_in, logs_in, table, lines, coef, curve_x, curve_y, both_x, both_y):
    row = lax.broadcasted_iota(jnp.int32, (2 * planes, LANES), 0)
    decay, rate = jnp.zeros(row.shape, F32), jnp.zeros(row.shape, F32)
    for z in range(planes):
        decay = jnp.where(row % planes == z, decay_in[z], decay)
        rate = jnp.where(row % planes == z, logs_in[z], rate)
    gain = (1.0 - decay) / (1.0 + decay)
    coef[0] = gain
    for i, (curve, both) in enumerate(((curve_x, both_x), (curve_y, both_y))):
        length = curve.shape[1]
        across = jnp.exp(length * rate)
        coef[1 + 3 * i] = across
        coef[2 + 3 * i] = gain * decay * (1.0 - across * across)
        coef[3 + 3 * i] = gain * decay * across
        slope, width, turn = rate[:, :1], gain[:, :1], (gain * decay)[:, :1]
        place = lax.broadcasted_iota(jnp.int32, curve.shape, 1).astype(F32)
        risen = jnp.exp(place * slope) - jnp.exp((2.0 * length - place) * slope)
        fall = jnp.exp((length - place) * slope)
        bend = turn * risen
        curve[...] = jnp.where(lax.broadcasted_iota(jnp.int32, curve.shape, 0) < planes, bend, fall)
        if i == 0:
            lines[0] = jnp.exp((length - 1.0 - place) * slope)
            lines[1] = width * risen
            lines[2] = bend
            lines[3] = fall
        rows = lax.broadcasted_iota(jnp.int32, (length, length), 0).astype(F32)
        cols = lax.broadcasted_iota(jnp.int32, (length, length), 1).astype(F32)
        apart, down = jnp.abs(rows - cols), length - rows[:, :1]
        for z in range(planes):
            log = logs_in[z]
            both[z] = width[z:z + 1] * (jnp.exp(apart * log) - jnp.exp(down * log) * fall[z:z + 1])
    cells = TS * TS
    shape = (cells, table.shape[1])
    row, col = lax.broadcasted_iota(jnp.int32, shape, 0), lax.broadcasted_iota(jnp.int32, shape, 1)
    along_y, kind = col // (2 * planes * TS) == 1, col // (planes * TS) % 2
    owner, cell = col // TS % planes, col % TS
    at_x, at_y = row // TS, row % TS
    summed, kept = jnp.where(along_y, at_y, at_x), jnp.where(along_y, at_x, at_y)
    steps = jnp.where(kind == 0, TS - 1 - summed, summed).astype(F32)
    for z in range(planes):
        power = jnp.exp(steps * logs_in[z])
        table[z * cells:(z + 1) * cells, :] = jnp.where((owner == z) & (kept == cell), power, 0.0)


def per_device(source_mass, target_density, potential, dest_device, dest_tile, mass_counts, reach):
    planes, cells_x, cells_y = source_mass.shape
    tile_count, fanout = dest_device.shape[2:]
    tiles_x, tiles_y = cells_x // TS, cells_y // TS
    grid_x, depth, inner = lax.axis_size("gx"), lax.axis_size("z"), lax.axis_size("x")
    columns = grid_x * inner
    device_count = columns * depth
    capacity = max(2, 3 * fanout * tile_count // (2 * device_count))
    capacity = -(-capacity // SUB) * SUB
    rows = depth * capacity + SUB
    planes_a = planes // 2
    rest = planes - planes_a
    tile_cells = 2 * LANES
    at = jnp.stack([lax.axis_index("gx"), lax.axis_index("z"), lax.axis_index("x")])
    scalars, near = pl.BlockSpec(memory_space=pltpu.SMEM), pl.BlockSpec(memory_space=pltpu.VMEM)
    far = pl.BlockSpec(memory_space=pl.ANY)

    def array(*shape):
        return jax.ShapeDtypeStruct(shape, F32)

    def turn(x, axis, steps):
        size = lax.axis_size(axis)
        return lax.ppermute(x, axis, [(i, (i + steps) % size) for i in range(size)])

    routes = jnp.stack([x.reshape(tile_count, fanout).T for x in (dest_device, dest_tile, mass_counts)])
    ring, tiled = call(
        "ring", functools.partial(ring_kernel, planes_a),
        [array(planes_a * cells_x + 3 * SUB, LANES), array(rest * cells_x, LANES)],
    )(source_mass, routes.astype(F32))
    rings = [ring] + [None] * (depth - 1)
    for s in range(1, depth // 2 + 1):
        rings[s] = turn(rings[s - 1], "z", 1)
        if s < depth - s:
            rings[depth - s] = turn(rings[(depth - s + 1) % depth], "z", -1)
    have = {"A1": rings[1], "A3": rings[-1], "ring": ring}

    def wait_of(name):
        return [have[x] for x in FLAG.get(name, ())]

    packed_b = call(
        "start", functools.partial(start_kernel, capacity, columns, depth, inner, planes_a, fanout),
        array(columns, rows, rest * tile_cells),
        [scalars] + [near] * 2,
        [pltpu.VMEM((columns * depth * capacity, tile_count), F32)],
        wait_of("start"),
    )(at, ring, tiled)
    arrived_b = lax.all_to_all(packed_b, ("gx", "x"), 0, 0, tiled=True)
    have["B"] = arrived_b
    have["packB"] = packed_b
    decay = 1.0 - 1.0 / reach
    logs = jnp.log(decay)
    eight = 2 * planes
    table, lines, coef, curve_x, curve_y, both_x, both_y = call(
        "table", functools.partial(table_kernel, planes),
        [
            array(planes * TS * TS, 4 * planes * TS), array(4, eight, cells_x), array(7, eight, LANES),
            array(eight, cells_x), array(eight, cells_y), array(planes, cells_x, cells_x),
            array(planes, cells_y, cells_y),
        ],
        [scalars] * 2,
        (),
        wait_of("table"),
    )(decay, logs)
    edge_rows = tiles_x + tiles_y
    edges = call(
        "edge", functools.partial(edge_kernel, grid_x, depth, inner, planes, fanout),
        [array(columns, edge_rows, LANES)] * depth,
        [scalars] * 2 + [near] * 7,
        [pltpu.VMEM((depth, columns, edge_rows, LANES), F32)],
        wait_of("edge"),
    )(at, logs, target_density, table, lines, coef, both_x, ring, tiled)
    have["edge"] = edges[0]
    edges = [edges[0]] + [turn(edges[o], "z", o) for o in range(1, depth)]
    sums = call(
        "partial", functools.partial(partial_kernel, capacity), [array(tile_count, rest * tile_cells)] * depth,
        None, (), wait_of("partial"),
    )(arrived_b)
    have["sums"] = sums[1]
    if FLAG.get("rs2"):
        moving = [sums[0], turn(sums[1] + turn(sums[2], "z", -1), "z", -1), turn(sums[3], "z", 1)]
    else:
        moving = [sums[0]] + [turn(sums[r], "z", -r) for r in range(1, depth)]
    last = depth // 2
    groups = [[s for s in range(depth) if s != last], [last]] if FLAG.get("split") else [list(range(depth))]
    arrived_a = []
    for group in groups:
        more = edges if group is groups[-1] else []
        rows = len(group) * capacity + SUB
        name = "pack" if more else "early"
        packed_a = call(
            name,
            functools.partial(forward_kernel, capacity, columns, depth, inner, planes_a, fanout, len(group)),
            array(columns, rows, planes_a * tile_cells),
            [scalars] + [near] * (len(group) + len(more)),
            [pltpu.VMEM((columns * capacity, tile_count), F32)],
            wait_of(name),
        )(at, *[rings[s] for s in group], *more)
        arrived_a.append(lax.all_to_all(packed_a, ("gx", "x"), 0, 0, tiled=True))
    earlier = [
        call("sum", functools.partial(sum_kernel, capacity, len(group)), array(tile_count, planes_a * tile_cells))(x)
        for group, x in zip(groups[:-1], arrived_a)
    ]
    base = call("base", base_kernel, array(*potential.shape), None, (), wait_of("base"))(
        target_density, potential, both_x, both_y
    )
    field = (planes_a, cells_x, cells_y)
    shapes = [array(*source_mass.shape), array(*potential.shape)]
    part = pl.BlockSpec(field, lambda i: (0, 0, 0))
    *outs, base = call(
        "near", functools.partial(near_kernel, capacity, len(groups[-1])),
        shapes + [array(rest, cells_x, cells_y)], None,
        out_specs=[part, part, near], grid=(1,),
    )(arrived_a[-1], base, both_x, both_y, curve_x, curve_y, *earlier)
    part = pl.BlockSpec(field, lambda i: (1, 0, 0))
    outs = call(
        "far", functools.partial(far_kernel, planes_a), shapes, [far, far] + [near] * (3 + len(moving)),
        out_specs=[part, part], grid=(1,), input_output_aliases={0: 0, 1: 1},
    )(*outs, base, both_x, both_y, *moving)
    return tuple(outs)


def solution(mesh):
    grid_x, grid_y = mesh.shape["gx"], mesh.shape["gy"]
    inner = grid_x // 2
    if inner < 1 or grid_y % inner:
        inner = 1
    depth = grid_y // inner
    split_mesh = Mesh(mesh.devices.reshape(grid_x, depth, inner), ("gx", "z", "x"))
    field = P(None, "gx", ("z", "x"))
    table = P("gx", ("z", "x"), None, None)
    return jax.shard_map(
        per_device,
        mesh=split_mesh,
        in_specs=(field, field, field, table, table, table, P()),
        out_specs=(field, field),
        check_vma=False,
    )
```

```python
import functools

import jax
import jax.numpy as jnp
from jax import lax
from jax.experimental import pallas as pl
from jax.experimental.pallas import tpu as pltpu
from jax.sharding import Mesh
from jax.sharding import PartitionSpec as P

TS = 16
MXU = 256
SUB = 8
LANES = 128
F32 = jnp.float32
BF16 = jnp.bfloat16
FLOPS_A_MICRO = 1_100_000_000
COST = {
    "ring": 0.8, "start": 2.5, "table": 20.0, "edge": 60.0, "partial": 1.4, "base": 1.0, "early": 1.8, "pack": 1.8,
    "near": 3.5, "far": 1.6,
}
VMEM_LIMIT = 20 * 1024 * 1024


def split(x):
    high = x.astype(BF16)
    return high, (x - high.astype(F32)).astype(BF16)


def mm(a, b):
    return jnp.dot(a, b, preferred_element_type=F32)


def mm_t(a, b):
    return lax.dot_general(a, b, (((0,), (0,)), ((), ())), preferred_element_type=F32)


def beside(*parts):
    return jnp.concatenate(parts, axis=1)


def stacked(*parts):
    return jnp.concatenate(parts, axis=0)


def dot3(a, b):
    a_high, a_low = split(a)
    b_high, b_low = split(b)
    deep, wide = a.shape[1], b.shape[1]
    if 2 * deep <= MXU and 2 * wide <= MXU:
        both = mm(beside(a_high, a_low), stacked(beside(b_high, b_low), beside(b_high, jnp.zeros_like(b_low))))
        return both[:, :wide] + both[:, wide:]
    if 2 * wide <= MXU:
        both = mm(a_high, beside(b_high, b_low))
        return both[:, :wide] + both[:, wide:] + mm(a_low, b_high)
    if 2 * deep <= MXU:
        return mm(beside(a_high, a_low), stacked(b_high, b_high)) + mm(a_high, b_low)
    rows = a.shape[0]
    both = mm(stacked(a_high, a_low), b_high)
    return both[:rows] + both[rows:] + mm(a_high, b_low)


def swap_blocks(x):
    rows = x.shape[0]
    x = x.reshape(rows // SUB, SUB, LANES)
    sub = lax.broadcasted_iota(jnp.int32, x.shape, 1)
    block = lax.broadcasted_iota(jnp.int32, x.shape, 2) // TS
    for k in (4, 2, 1):
        up = pltpu.roll(pltpu.roll(x, SUB - k, 1), TS * k, 2)
        down = up if 2 * k == SUB else pltpu.roll(pltpu.roll(x, k, 1), LANES - TS * k, 2)
        moved = jnp.where((sub & k) == 0, up, down)
        x = jnp.where((sub & k) == (block & k), x, moved)
    return x.reshape(rows, LANES)


def tile_columns(tiled, planes, tiles_x):
    grouped = tiled.reshape(planes, tiles_x, 2, SUB, LANES)
    columns = [grouped[z, :, h].reshape(tiles_x * SUB, LANES) for z in range(planes) for h in range(2)]
    return jnp.concatenate(columns, axis=1)


def tile_rows(columns, planes, tiles_x):
    parts = [
        columns[:, i * LANES:(i + 1) * LANES].reshape(1, tiles_x, 1, SUB, LANES) for i in range(2 * planes)
    ]
    planes_of = [jnp.concatenate(parts[2 * z:2 * z + 2], axis=2) for z in range(planes)]
    return jnp.concatenate(planes_of, axis=0).reshape(planes * tiles_x * TS, LANES)


def route_rows(names, tiles, shares, wanted):
    fanout, count = names.shape
    member = jnp.zeros(wanted.shape, F32)
    weight = jnp.zeros(wanted.shape, F32)
    label = jnp.zeros(wanted.shape, F32)
    for k in range(fanout):
        hit = names[k:k + 1, :] == wanted
        member = member + jnp.where(hit, 1.0, 0.0)
        weight = weight + jnp.where(hit, shares[k:k + 1, :], 0.0)
        label = label + jnp.where(hit, tiles[k:k + 1, :], 0.0)
    return member, weight, label


def ranked(member):
    count = member.shape[1]
    before = lax.broadcasted_iota(jnp.int32, (count, count), 0) < lax.broadcasted_iota(
        jnp.int32, (count, count), 1
    )
    rank = mm(member.astype(BF16), jnp.where(before, 1.0, 0.0).astype(BF16))
    return jnp.where(member > 0.0, rank, 2.0 * count)


def slots_of(rank, weight, label, capacity):
    slot = lax.broadcasted_iota(jnp.int32, (capacity, rank.shape[1]), 0).astype(F32)
    chosen = rank == slot
    picked = jnp.where(chosen, weight, 0.0)
    labels = jnp.sum(jnp.where(chosen, label, 0.0), axis=1, keepdims=True)
    return picked, labels


def place_labels(board, labels, first):
    lane = lax.broadcasted_iota(jnp.int32, board.shape, 1)
    for g in range(labels.shape[0] // SUB):
        board = jnp.where(lane == first + g, labels[g * SUB:(g + 1) * SUB], board)
    return board


def read_labels(board, first, capacity):
    lane = lax.broadcasted_iota(jnp.int32, (SUB, LANES), 1).astype(F32)
    rows = [
        jnp.where(board[:, first + g:first + g + 1] == lane, 1.0, 0.0) for g in range(capacity // SUB)
    ]
    return jnp.concatenate(rows, axis=0)


def turned_by(at, steps, size):
    at = at + steps
    return jnp.where(at >= size, at - size, at)


def columns_wanted(shape, depth, inner, level, steps):
    row = lax.broadcasted_iota(jnp.int32, shape, 0)
    column, steps = (row // depth, row % depth) if steps is None else (row, steps)
    level = turned_by(level, depth - steps, depth)
    return (column // inner * (depth * inner) + level * inner + column % inner).astype(F32)


def ring_kernel(planes_a, source, routes, ring, tiled):
    planes, cells_x, _ = source.shape
    half = planes_a * cells_x
    fanout = routes.shape[1]
    ring[:half, :] = swap_blocks(source[:planes_a].reshape(half, LANES))
    ring[half:, :] = jnp.zeros((3 * SUB, LANES), F32)
    ring[half:half + fanout, :] = routes[0]
    ring[half + SUB:half + SUB + fanout, :] = routes[1]
    ring[half + 2 * SUB:half + 2 * SUB + fanout, :] = routes[2] / jnp.sum(routes[2], axis=0, keepdims=True)
    tiled[...] = swap_blocks(source[planes_a:].reshape(tiled.shape[0], LANES))


def start_kernel(capacity, columns, depth, inner, planes_a, fanout, at, ring, tiled, pack_out, picked):
    cells_x = (ring.shape[0] - 3 * SUB) // planes_a
    rest = tiled.shape[0] // cells_x
    names, tiles, shares = routing(ring, fanout)
    wanted = columns_wanted((columns * depth, LANES), depth, inner, at[1], None)
    member, weight, label = route_rows(names, tiles, shares, wanted)
    rank = ranked(member)
    for j in range(columns):
        board = jnp.zeros((SUB, LANES), F32)
        for r in range(depth):
            n = j * depth + r
            rows, labels = slots_of(rank[n:n + 1], weight[n:n + 1], label[n:n + 1], capacity)
            picked[n * capacity:(n + 1) * capacity, :] = rows
            board = place_labels(board, labels, r * (capacity // SUB))
        pack_out[j, pack_out.shape[1] - SUB:, :] = board
    packed = dot3(picked[...], tile_columns(tiled[...], rest, cells_x // TS))
    put(pack_out, packed.reshape(columns, depth * capacity, packed.shape[1]))


def put(out, slots, first=0, size=None):
    count = slots.shape[1]
    size = count if size is None else size
    for c in range(slots.shape[2] // LANES):
        out[:, c * size + first:c * size + first + count, :] = slots[:, :, c * LANES:(c + 1) * LANES]


def routing(ring, fanout):
    first = ring.shape[0] - 3 * SUB
    return [ring[first + k * SUB:first + k * SUB + fanout, :] for k in range(3)]


def pack(capacity, columns, depth, inner, fanout, level, rings, picked, pack_out, boards, first, size):
    wanted = columns_wanted((columns, LANES), depth, inner, level, 0)
    for s, ring in enumerate(rings):
        half = ring.shape[0] - 3 * SUB
        member, weight, label = route_rows(*routing(ring, fanout), wanted)
        rank = ranked(member)
        for j in range(columns):
            rows, labels = slots_of(rank[j:j + 1], weight[j:j + 1], label[j:j + 1], capacity)
            picked[j * capacity:(j + 1) * capacity, :] = rows
            boards[j] = place_labels(boards[j], labels, (first + s) * (capacity // SUB))
        planes = pack_out.shape[1] // size // 2
        cells = tile_columns(ring[:half, :], planes, half // planes // TS)
        packed = dot3(picked[...], cells)
        put(pack_out, packed.reshape(columns, capacity, packed.shape[1]), s * capacity, size)
    return boards


def send(pairs, gone):
    copies = [pltpu.make_async_copy(near, far, gone.at[i]) for i, (near, far) in enumerate(pairs)]
    for copy in copies:
        copy.start()
    for copy in copies:
        copy.wait()


def early_kernel(capacity, columns, depth, inner, fanout, total, at, *refs):
    rings, (far, boards_out, picked, out, gone) = refs[:-5], refs[-5:]
    size = len(rings) * capacity
    boards = [jnp.zeros((SUB, LANES), F32) for _ in range(columns)]
    boards = pack(capacity, columns, depth, inner, fanout, at[1], rings, picked, out, boards, 0, size)
    for j in range(columns):
        boards_out[j] = boards[j]
    send(
        [
            (out.at[:, c * size:(c + 1) * size], far.at[:, c * total:c * total + size])
            for c in range(out.shape[1] // size)
        ],
        gone,
    )


def forward_kernel(capacity, columns, depth, inner, fanout, total, at, far_in, boards_in, ring, *refs):
    edges, (far, picked, out, tail, gone) = refs[:-5], refs[-5:]
    del far_in
    boards = [boards_in[j] for j in range(columns)]
    boards = pack(
        capacity, columns, depth, inner, fanout, at[1], [ring], picked, out, boards, total // capacity - 1, capacity
    )
    for j in range(columns):
        tail[j, :SUB, :] = boards[j]
    value = edges[0][...]
    for part in edges[1:]:
        value = value + part[...]
    tail[:, SUB:, :] = value
    parts = out.shape[1] // capacity
    send(
        [
            (out.at[:, c * capacity:(c + 1) * capacity], far.at[:, (c + 1) * total - capacity:(c + 1) * total])
            for c in range(parts)
        ] + [(tail, far.at[:, parts * total:])],
        gone,
    )


def gather_sum(arrived, capacity, groups, total, parts):
    heads, cells = [], []
    for j in range(arrived.shape[0]):
        board = arrived[j, parts * total:parts * total + SUB, :]
        for g in groups:
            heads.append(read_labels(board, g * (capacity // SUB), capacity))
            first = g * capacity
            cells.append(beside(*[
                arrived[j, c * total + first:c * total + first + capacity, :] for c in range(parts)
            ]))
    head = stacked(*heads).astype(BF16)
    high, low = split(stacked(*cells))
    return mm_t(head, high) + mm_t(head, low)


def partial_kernel(capacity, arrived, *outs):
    for r, out in enumerate(outs):
        out[...] = gather_sum(arrived, capacity, [r], len(outs) * capacity, out.shape[1] // LANES)


def edge_sums(proj, weight, label, tiles_x, tiles_y, logs, part):
    label = label.astype(jnp.int32)
    tile_x, tile_y = label // tiles_y, label % tiles_y
    place, other, size = (tile_y, tile_x, tiles_x) if part == 0 else (tile_x, tile_y, tiles_y)
    per = tiles_y if part == 0 else tiles_x
    blocks = weight.shape[0]
    proj = proj[:, part * LANES:(part + 1) * LANES]
    owner = lax.broadcasted_iota(jnp.int32, proj.shape, 1) // TS
    row = lax.broadcasted_iota(jnp.int32, (per, weight.shape[1]), 0)
    here = [place[n:n + 1] == row for n in range(blocks)]
    planes = len(logs)
    left, right = [], []
    for kind in range(2):
        gap = (size - 1 - other if kind == 0 else other).astype(F32)
        for z in range(planes):
            value = weight * jnp.exp(gap * (TS * logs[z]))
            left.append(stacked(*[jnp.where(here[n], value[n:n + 1], 0.0) for n in range(blocks)]))
            right.append(jnp.where(owner == kind * planes + z, proj, 0.0))
    return dot3(beside(*left), stacked(*right)).reshape(blocks, per, LANES)


def own_edges(proj, tiles_x, tiles_y, logs):
    lane = lax.broadcasted_iota(jnp.int32, (SUB, LANES), 1) // TS
    sub = lax.broadcasted_iota(jnp.int32, (SUB, LANES), 0)
    planes = len(logs)
    rate = jnp.zeros((SUB, LANES), F32)
    for z in range(planes):
        rate = jnp.where(lane % planes == z, TS * logs[z], rate)
    to_end = lane < planes
    near = jnp.exp(jnp.where(to_end, tiles_y - 1 - sub, sub).astype(F32) * rate)
    along_x, along_y = jnp.zeros((SUB, LANES), F32), []
    for i in range(tiles_x):
        rows = proj[i * tiles_y:(i + 1) * tiles_y]
        steps = jnp.where(to_end, tiles_x - 1 - i, i).astype(F32)
        along_x = along_x + rows[:, :LANES] * jnp.exp(steps * rate)
        along_y.append(jnp.sum(rows[:, LANES:] * near, axis=0, keepdims=True))
    return along_x[None], stacked(*along_y)[None]


def line_carries(ends, starts, across, first):
    forward, full, running = [], [], jnp.zeros_like(ends[0])
    for end, start in zip(ends, starts):
        forward.append(running)
        full.append(start + first * running)
        running = across * running + end
    backward, running = [], jnp.zeros_like(ends[0])
    for start in full[::-1]:
        backward.append(running)
        running = across * running + start
    return forward, backward[::-1]


def end_start(both, gain, back):
    half = both.shape[1] // 2
    end = both[:, :half]
    return end, gain[:half] * both[:, half:] - back[:half] * end


def edge_kernel(grid_x, depth, inner, planes, fanout, at, logs_in, target, table, lines, coef, both_x, ring, tiled,
                *refs):
    outs, carries = refs[:-1], refs[-1]
    _, cells_x, cells_y = target.shape
    tiles_x, tiles_y = cells_x // TS, cells_y // TS
    half = ring.shape[0] - 3 * SUB
    planes_a = half // cells_x
    logs = [logs_in[z] for z in range(planes)]
    names, tiles, shares = routing(ring, fanout)
    cells = [tile_columns(ring[:half, :], planes_a, tiles_x), tile_columns(tiled[...], planes - planes_a, tiles_x)]
    cells = beside(*cells)
    own_cells = tile_columns(swap_blocks(target[...].reshape(planes * cells_x, LANES)), planes, tiles_x)
    proj = dot3(stacked(cells, own_cells), table[...])
    own = own_edges(proj[cells.shape[0]:], tiles_x, tiles_y, logs)
    proj = proj[:cells.shape[0]]
    tile_count = names.shape[1]
    along = depth * inner
    blocks = grid_x * along
    wanted = lax.broadcasted_iota(jnp.int32, (blocks, tile_count), 0).astype(F32)
    _, weight, label = route_rows(names, tiles, shares, wanted)
    here = at[0] * along + at[1] * inner + at[2]
    edges = []
    for part in range(2):
        sums = edge_sums(proj, weight, label, tiles_x, tiles_y, logs, part)
        is_here = lax.broadcasted_iota(jnp.int32, sums.shape, 0) == here
        sums = jnp.where(is_here, own[part], 0.0) - sums
        edges.append(swap_blocks(sums.reshape(-1, LANES)).reshape(blocks, sums.shape[1] // SUB, SUB, LANES))
    gain, across_x, first_x, back_x, across_y, first_y, back_y = [coef[i][:, :1] for i in range(7)]

    ends, starts = zip(*[
        end_start(edges[0][p * along:(p + 1) * along, 0], gain, back_x) for p in range(grid_x)
    ])
    forward, backward = line_carries(ends, starts, across_x[:planes], first_x[:planes])
    for p in range(grid_x):
        rows = jnp.concatenate([forward[p], backward[p]], axis=1).reshape(depth, inner, SUB, LANES)
        carries[:, p * inner:(p + 1) * inner, :SUB, :] = rows

    side = jnp.concatenate([edges[1][:, i] for i in range(edges[1].shape[1])], axis=2)
    flat = side.reshape(blocks * SUB, cells_x)
    local = jnp.zeros_like(flat)
    for z in range(planes):
        local = local + dot3(masked(flat, planes, z), both_x[z])
    local = local.reshape(side.shape)
    ends = jnp.sum(side * lines[0], axis=2, keepdims=True)
    starts = jnp.sum(side * lines[1], axis=2, keepdims=True)
    forward, backward = line_carries(
        [ends[p * along:(p + 1) * along] for p in range(grid_x)],
        [starts[p * along:(p + 1) * along] for p in range(grid_x)],
        across_x,
        first_x,
    )
    smooth = [
        local[p * along:(p + 1) * along] + forward[p] * lines[2] + backward[p] * lines[3] for p in range(grid_x)
    ]
    smooth = jnp.stack(smooth)
    ends, starts = zip(*[end_start(smooth[:, q], gain, back_y) for q in range(along)])
    forward, backward = line_carries(ends, starts, across_y[:planes], first_y[:planes])
    for q in range(along):
        rows = jnp.concatenate([forward[q], backward[q]], axis=1)
        for p in range(grid_x):
            for i in range(cells_x // LANES):
                carries[q // inner, p * inner + q % inner, (1 + i) * SUB:(2 + i) * SUB, :] = (
                    rows[p, :, i * LANES:(i + 1) * LANES]
                )
    for o, out in enumerate(outs):
        out[...] = carries[turned_by(at[1], o, depth)]


def masked(rows, planes, z):
    row = lax.broadcasted_iota(jnp.int32, rows.shape, 0)
    return jnp.where(row % planes == z, rows, 0.0)


def outer(a, b):
    a_high, a_low = split(a)
    b_high, b_low = split(b)
    return mm_t(stacked(a_high, a_high, a_low), stacked(b_high, b_low, b_high))


def base_kernel(target, potential, both_x, both_y, out):
    for z in range(target.shape[0]):
        out[z] = potential[z] + dot3(dot3(both_x[z], target[z]), both_y[z])


def solve(pushed, before, both_x, both_y):
    return before - dot3(dot3(both_x, pushed), both_y)


def near_kernel(capacity, depth, arrived, base, both_x, both_y, curve_x, curve_y, pushed_out, next_out, rest_out):
    planes, planes_a = base.shape[0], pushed_out.shape[0]
    cells_x = pushed_out.shape[1]
    total, parts = depth * capacity, 2 * planes_a
    first = parts * total + SUB
    carries = arrived[0, first:, :]
    for j in range(1, arrived.shape[0]):
        carries = carries + arrived[j, first:, :]
    carry_x = carries[:SUB]
    carry_y = beside(*[carries[i:i + SUB] for i in range(SUB, carries.shape[0], SUB)])
    total = gather_sum(arrived, capacity, list(range(depth)), total, parts)
    pushed = swap_blocks(tile_rows(total, planes_a, cells_x // TS)).reshape(planes_a, cells_x, LANES)
    pushed_out[...] = pushed
    for z in range(planes):
        left = jnp.concatenate([masked(curve_x[...], planes, z), masked(carry_y, planes, z)], axis=0)
        right = jnp.concatenate([dot3(carry_x, both_y[z]), curve_y[...]], axis=0)
        before = base[z] + outer(left, right)
        if z < planes_a:
            next_out[z] = solve(pushed[z], before, both_x[z], both_y[z])
        else:
            rest_out[z - planes_a] = before


def far_kernel(first, pushed_in, next_in, base, both_x, both_y, *refs):
    del pushed_in, next_in
    sums, (pushed_out, next_out) = refs[:-2], refs[-2:]
    count, cells_x, _ = pushed_out.shape
    total = sums[0][...]
    for part in sums[1:]:
        total = total + part[...]
    pushed = swap_blocks(tile_rows(total, count, cells_x // TS)).reshape(count, cells_x, LANES)
    for z in range(count):
        pushed_out[z] = pushed[z]
        next_out[z] = solve(pushed[z], base[z], both_x[first + z], both_y[first + z])


def call(name, body, out_shape, in_specs=None, scratch=(), wait=(), **extra):
    def run(*args):
        count, unread = len(args), len(wait)

        def kernel(*refs):
            body(*refs[:count], *refs[count + unread:])

        near = pl.BlockSpec(memory_space=pltpu.VMEM)
        specs = [near] * count if in_specs is None else list(in_specs)
        return pl.pallas_call(
            kernel,
            out_shape=out_shape,
            in_specs=specs + [pl.BlockSpec(memory_space=pl.ANY)] * unread,
            scratch_shapes=list(scratch),
            compiler_params=pltpu.CompilerParams(vmem_limit_bytes=VMEM_LIMIT),
            cost_estimate=pl.CostEstimate(
                flops=int(COST[name] * FLOPS_A_MICRO), bytes_accessed=0, transcendentals=0
            ),
            **extra,
        )(*args, *wait)

    return run


def table_kernel(planes, decay_in, logs_in, table, lines, coef, curve_x, curve_y, both_x, both_y):
    row = lax.broadcasted_iota(jnp.int32, (2 * planes, LANES), 0)
    decay, rate = jnp.zeros(row.shape, F32), jnp.zeros(row.shape, F32)
    for z in range(planes):
        decay = jnp.where(row % planes == z, decay_in[z], decay)
        rate = jnp.where(row % planes == z, logs_in[z], rate)
    gain = (1.0 - decay) / (1.0 + decay)
    coef[0] = gain
    for i, (curve, both) in enumerate(((curve_x, both_x), (curve_y, both_y))):
        length = curve.shape[1]
        across = jnp.exp(length * rate)
        coef[1 + 3 * i] = across
        coef[2 + 3 * i] = gain * decay * (1.0 - across * across)
        coef[3 + 3 * i] = gain * decay * across
        slope, width, turn = rate[:, :1], gain[:, :1], (gain * decay)[:, :1]
        place = lax.broadcasted_iota(jnp.int32, curve.shape, 1).astype(F32)
        risen = jnp.exp(place * slope) - jnp.exp((2.0 * length - place) * slope)
        fall = jnp.exp((length - place) * slope)
        bend = turn * risen
        curve[...] = jnp.where(lax.broadcasted_iota(jnp.int32, curve.shape, 0) < planes, bend, fall)
        if i == 0:
            lines[0] = jnp.exp((length - 1.0 - place) * slope)
            lines[1] = width * risen
            lines[2] = bend
            lines[3] = fall
        rows = lax.broadcasted_iota(jnp.int32, (length, length), 0).astype(F32)
        cols = lax.broadcasted_iota(jnp.int32, (length, length), 1).astype(F32)
        apart, down = jnp.abs(rows - cols), length - rows[:, :1]
        for z in range(planes):
            log = logs_in[z]
            both[z] = width[z:z + 1] * (jnp.exp(apart * log) - jnp.exp(down * log) * fall[z:z + 1])
    cells = TS * TS
    shape = (cells, table.shape[1])
    row, col = lax.broadcasted_iota(jnp.int32, shape, 0), lax.broadcasted_iota(jnp.int32, shape, 1)
    along_y, kind = col // (2 * planes * TS) == 1, col // (planes * TS) % 2
    owner, cell = col // TS % planes, col % TS
    at_x, at_y = row // TS, row % TS
    summed, kept = jnp.where(along_y, at_y, at_x), jnp.where(along_y, at_x, at_y)
    steps = jnp.where(kind == 0, TS - 1 - summed, summed).astype(F32)
    for z in range(planes):
        power = jnp.exp(steps * logs_in[z])
        table[z * cells:(z + 1) * cells, :] = jnp.where((owner == z) & (kept == cell), power, 0.0)


def per_device(source_mass, target_density, potential, dest_device, dest_tile, mass_counts, reach):
    planes, cells_x, cells_y = source_mass.shape
    tile_count, fanout = dest_device.shape[2:]
    tiles_x, tiles_y = cells_x // TS, cells_y // TS
    grid_x, depth, inner = lax.axis_size("gx"), lax.axis_size("z"), lax.axis_size("x")
    columns = grid_x * inner
    device_count = columns * depth
    capacity = max(2, 3 * fanout * tile_count // (2 * device_count))
    capacity = -(-capacity // SUB) * SUB
    slots = depth * capacity
    planes_a = planes // 2
    rest = planes - planes_a
    tile_cells = 2 * LANES
    at = jnp.stack([lax.axis_index("gx"), lax.axis_index("z"), lax.axis_index("x")])
    scalars, near = pl.BlockSpec(memory_space=pltpu.SMEM), pl.BlockSpec(memory_space=pltpu.VMEM)
    far = pl.BlockSpec(memory_space=pl.ANY)

    def array(*shape):
        return jax.ShapeDtypeStruct(shape, F32)

    def turn(x, axis, steps):
        size = lax.axis_size(axis)
        return lax.ppermute(x, axis, [(i, (i + steps) % size) for i in range(size)])

    routes = jnp.stack([x.reshape(tile_count, fanout).T for x in (dest_device, dest_tile, mass_counts)])
    ring, tiled = call(
        "ring", functools.partial(ring_kernel, planes_a),
        [array(planes_a * cells_x + 3 * SUB, LANES), array(rest * cells_x, LANES)],
    )(source_mass, routes.astype(F32))
    rings = [ring] + [None] * (depth - 1)
    for s in range(1, depth // 2 + 1):
        rings[s] = turn(rings[s - 1], "z", 1)
        if s < depth - s:
            rings[depth - s] = turn(rings[(depth - s + 1) % depth], "z", -1)

    packed_b = call(
        "start", functools.partial(start_kernel, capacity, columns, depth, inner, planes_a, fanout),
        array(columns, 2 * rest * slots + SUB, LANES),
        [scalars] + [near] * 2,
        [pltpu.VMEM((columns * depth * capacity, tile_count), F32)],
    )(at, ring, tiled)
    arrived_b = lax.all_to_all(packed_b, ("gx", "x"), 0, 0, tiled=True)
    decay = 1.0 - 1.0 / reach
    logs = jnp.log(decay)
    eight = 2 * planes
    table, lines, coef, curve_x, curve_y, both_x, both_y = call(
        "table", functools.partial(table_kernel, planes),
        [
            array(planes * TS * TS, 4 * planes * TS), array(4, eight, cells_x), array(7, eight, LANES),
            array(eight, cells_x), array(eight, cells_y), array(planes, cells_x, cells_x),
            array(planes, cells_y, cells_y),
        ],
        [scalars] * 2,
        (),
        [ring],
    )(decay, logs)
    edge_rows = tiles_x + tiles_y
    edges = call(
        "edge", functools.partial(edge_kernel, grid_x, depth, inner, planes, fanout),
        [array(columns, edge_rows, LANES)] * depth,
        [scalars] * 2 + [near] * 7,
        [pltpu.VMEM((depth, columns, edge_rows, LANES), F32)],
        [rings[1], packed_b],
    )(at, logs, target_density, table, lines, coef, both_x, ring, tiled)
    edges = [edges[0]] + [turn(edges[o], "z", o) for o in range(1, depth)]
    sums = call(
        "partial", functools.partial(partial_kernel, capacity), [array(tile_count, rest * tile_cells)] * depth,
        None, (),
    )(arrived_b)
    moving = {r: sums[r] for r in range(depth)}
    for r in range(depth // 2, 0, -1):
        moving[r - 1] = turn(moving[r], "z", -1) if r == 1 else moving[r - 1] + turn(moving[r], "z", -1)
    moving = [sums[0], moving[0]]
    if depth > 2:
        more = sums[depth // 2 + 1]
        for r in range(depth // 2 + 1, depth):
            more = turn(more, "z", 1)
            if r < depth - 1:
                more = more + sums[r + 1]
        moving.append(more)
    last = depth // 2
    order = [s for s in range(depth) if s != last]
    parts = 2 * planes_a
    packed_a, boards = call(
        "early", functools.partial(early_kernel, capacity, columns, depth, inner, fanout, slots),
        [array(columns, parts * slots + SUB + edge_rows, LANES), array(columns, SUB, LANES)],
        [scalars] + [near] * len(order),
        [
            pltpu.VMEM((columns * capacity, tile_count), F32),
            pltpu.VMEM((columns, parts * (slots - capacity), LANES), F32),
            pltpu.SemaphoreType.DMA((parts,)),
        ],
        out_specs=[far, near],
    )(at, *[rings[s] for s in order])
    packed_a = call(
        "pack", functools.partial(forward_kernel, capacity, columns, depth, inner, fanout, slots),
        array(*packed_a.shape), [scalars, far] + [near] * (2 + len(edges)),
        [
            pltpu.VMEM((columns * capacity, tile_count), F32), pltpu.VMEM((columns, parts * capacity, LANES), F32),
            pltpu.VMEM((columns, SUB + edge_rows, LANES), F32), pltpu.SemaphoreType.DMA((parts + 1,)),
        ],
        out_specs=far, input_output_aliases={1: 0},
    )(at, packed_a, boards, rings[last], *edges)
    arrived_a = lax.all_to_all(packed_a, ("gx", "x"), 0, 0, tiled=True)
    base = call("base", base_kernel, array(*potential.shape))(
        target_density, potential, both_x, both_y
    )
    field = (planes_a, cells_x, cells_y)
    shapes = [array(*source_mass.shape), array(*potential.shape)]
    part = pl.BlockSpec(field, lambda i: (0, 0, 0))
    *outs, base = call(
        "near", functools.partial(near_kernel, capacity, depth),
        shapes + [array(rest, cells_x, cells_y)], None,
        out_specs=[part, part, near], grid=(1,),
    )(arrived_a, base, both_x, both_y, curve_x, curve_y)
    part = pl.BlockSpec(field, lambda i: (1, 0, 0))
    outs = call(
        "far", functools.partial(far_kernel, planes_a), shapes, [far, far] + [near] * (3 + len(moving)),
        out_specs=[part, part], grid=(1,), input_output_aliases={0: 0, 1: 1},
    )(*outs, base, both_x, both_y, *moving)
    return tuple(outs)


def solution(mesh):
    grid_x, grid_y = mesh.shape["gx"], mesh.shape["gy"]
    inner = grid_x // 2
    if inner < 1 or grid_y % inner:
        inner = 1
    depth = grid_y // inner
    split_mesh = Mesh(mesh.devices.reshape(grid_x, depth, inner), ("gx", "z", "x"))
    field = P(None, "gx", ("z", "x"))
    table = P("gx", ("z", "x"), None, None)
    return jax.shard_map(
        per_device,
        mesh=split_mesh,
        in_specs=(field, field, field, table, table, table, P()),
        out_specs=(field, field),
        check_vma=False,
    )
```

```python
import functools

import jax
import jax.numpy as jnp
from jax import lax
from jax.experimental import pallas as pl
from jax.experimental.pallas import tpu as pltpu
from jax.sharding import Mesh
from jax.sharding import PartitionSpec as P

TS = 16
MXU = 256
SUB = 8
LANES = 128
F32 = jnp.float32
BF16 = jnp.bfloat16
FLOPS_A_MICRO = 1_100_000_000
COST = {
    "ring": 0.8, "start": 2.5, "table": 20.0, "edge": 60.0, "partial": 1.4, "base": 1.0, "early": 1.8, "pack": 1.8,
    "near": 3.5, "far": 1.6,
}
VMEM_LIMIT = 20 * 1024 * 1024


def split(x):
    high = x.astype(BF16)
    return high, (x - high.astype(F32)).astype(BF16)


def mm(a, b):
    return jnp.dot(a, b, preferred_element_type=F32)


def mm_t(a, b):
    return lax.dot_general(a, b, (((0,), (0,)), ((), ())), preferred_element_type=F32)


def beside(*parts):
    return jnp.concatenate(parts, axis=1)


def stacked(*parts):
    return jnp.concatenate(parts, axis=0)


def dot3(a, b):
    a_high, a_low = split(a)
    b_high, b_low = split(b)
    deep, wide = a.shape[1], b.shape[1]
    if 2 * deep <= MXU and 2 * wide <= MXU:
        both = mm(beside(a_high, a_low), stacked(beside(b_high, b_low), beside(b_high, jnp.zeros_like(b_low))))
        return both[:, :wide] + both[:, wide:]
    if 2 * wide <= MXU:
        both = mm(a_high, beside(b_high, b_low))
        return both[:, :wide] + both[:, wide:] + mm(a_low, b_high)
    if 2 * deep <= MXU:
        return mm(beside(a_high, a_low), stacked(b_high, b_high)) + mm(a_high, b_low)
    rows = a.shape[0]
    both = mm(stacked(a_high, a_low), b_high)
    return both[:rows] + both[rows:] + mm(a_high, b_low)


def swap_blocks(x):
    rows = x.shape[0]
    x = x.reshape(rows // SUB, SUB, LANES)
    sub = lax.broadcasted_iota(jnp.int32, x.shape, 1)
    block = lax.broadcasted_iota(jnp.int32, x.shape, 2) // TS
    for k in (4, 2, 1):
        up = pltpu.roll(pltpu.roll(x, SUB - k, 1), TS * k, 2)
        down = up if 2 * k == SUB else pltpu.roll(pltpu.roll(x, k, 1), LANES - TS * k, 2)
        moved = jnp.where((sub & k) == 0, up, down)
        x = jnp.where((sub & k) == (block & k), x, moved)
    return x.reshape(rows, LANES)


def tile_columns(tiled, planes, tiles_x):
    grouped = tiled.reshape(planes, tiles_x, 2, SUB, LANES)
    columns = [grouped[z, :, h].reshape(tiles_x * SUB, LANES) for z in range(planes) for h in range(2)]
    return jnp.concatenate(columns, axis=1)


def tile_rows(columns, planes, tiles_x):
    parts = [
        columns[:, i * LANES:(i + 1) * LANES].reshape(1, tiles_x, 1, SUB, LANES) for i in range(2 * planes)
    ]
    planes_of = [jnp.concatenate(parts[2 * z:2 * z + 2], axis=2) for z in range(planes)]
    return jnp.concatenate(planes_of, axis=0).reshape(planes * tiles_x * TS, LANES)


def route_rows(names, tiles, shares, wanted):
    fanout, count = names.shape
    member = jnp.zeros(wanted.shape, F32)
    weight = jnp.zeros(wanted.shape, F32)
    label = jnp.zeros(wanted.shape, F32)
    for k in range(fanout):
        hit = names[k:k + 1, :] == wanted
        member = member + jnp.where(hit, 1.0, 0.0)
        weight = weight + jnp.where(hit, shares[k:k + 1, :], 0.0)
        label = label + jnp.where(hit, tiles[k:k + 1, :], 0.0)
    return member, weight, label


def ranked(member):
    count = member.shape[1]
    before = lax.broadcasted_iota(jnp.int32, (count, count), 0) < lax.broadcasted_iota(
        jnp.int32, (count, count), 1
    )
    rank = mm(member.astype(BF16), jnp.where(before, 1.0, 0.0).astype(BF16))
    return jnp.where(member > 0.0, rank, 2.0 * count)


def slots_of(rank, weight, label, capacity):
    slot = lax.broadcasted_iota(jnp.int32, (capacity, rank.shape[1]), 0).astype(F32)
    chosen = rank == slot
    return jnp.where(chosen, weight, 0.0), jnp.where(chosen, label, 0.0)


def in_all_lanes(rows):
    return mm(rows.astype(BF16), jnp.ones((rows.shape[1], LANES), BF16))


def place_labels(board, labels, first):
    lane = lax.broadcasted_iota(jnp.int32, board.shape, 1)
    for g in range(labels.shape[0] // SUB):
        board = jnp.where(lane == first + g, labels[g * SUB:(g + 1) * SUB], board)
    return board


def read_labels(board, first, capacity):
    lane = lax.broadcasted_iota(jnp.int32, (SUB, LANES), 1).astype(F32)
    rows = [
        jnp.where(board[:, first + g:first + g + 1] == lane, 1.0, 0.0) for g in range(capacity // SUB)
    ]
    return jnp.concatenate(rows, axis=0)


def turned_by(at, steps, size):
    at = at + steps
    return jnp.where(at >= size, at - size, at)


def columns_wanted(shape, depth, inner, level, steps):
    row = lax.broadcasted_iota(jnp.int32, shape, 0)
    column, steps = (row // depth, row % depth) if steps is None else (row, steps)
    level = turned_by(level, depth - steps, depth)
    return (column // inner * (depth * inner) + level * inner + column % inner).astype(F32)


def ring_kernel(planes_a, source, routes, ring, tiled):
    planes, cells_x, _ = source.shape
    half = planes_a * cells_x
    fanout = routes.shape[1]
    ring[:half, :] = swap_blocks(source[:planes_a].reshape(half, LANES))
    ring[half:, :] = jnp.zeros((3 * SUB, LANES), F32)
    ring[half:half + fanout, :] = routes[0]
    ring[half + SUB:half + SUB + fanout, :] = routes[1]
    ring[half + 2 * SUB:half + 2 * SUB + fanout, :] = routes[2] / jnp.sum(routes[2], axis=0, keepdims=True)
    tiled[...] = swap_blocks(source[planes_a:].reshape(tiled.shape[0], LANES))


def start_kernel(capacity, columns, depth, inner, planes_a, fanout, at, ring, tiled, pack_out, picked):
    cells_x = (ring.shape[0] - 3 * SUB) // planes_a
    rest = tiled.shape[0] // cells_x
    names, tiles, shares = routing(ring, fanout)
    wanted = columns_wanted((columns * depth, LANES), depth, inner, at[1], None)
    member, weight, label = route_rows(names, tiles, shares, wanted)
    rank = ranked(member)
    named = []
    for n in range(columns * depth):
        rows, labels = slots_of(rank[n:n + 1], weight[n:n + 1], label[n:n + 1], capacity)
        picked[n * capacity:(n + 1) * capacity, :] = rows
        named.append(labels)
    named = in_all_lanes(stacked(*named))
    slots = depth * capacity
    for j in range(columns):
        board = jnp.zeros((SUB, LANES), F32)
        pack_out[j, pack_out.shape[1] - SUB:, :] = place_labels(board, named[j * slots:(j + 1) * slots], 0)
    packed = dot3(picked[...], tile_columns(tiled[...], rest, cells_x // TS))
    put(pack_out, packed.reshape(columns, depth * capacity, packed.shape[1]))


def put(out, slots, first=0, size=None):
    count = slots.shape[1]
    size = count if size is None else size
    for c in range(slots.shape[2] // LANES):
        out[:, c * size + first:c * size + first + count, :] = slots[:, :, c * LANES:(c + 1) * LANES]


def routing(ring, fanout):
    first = ring.shape[0] - 3 * SUB
    return [ring[first + k * SUB:first + k * SUB + fanout, :] for k in range(3)]


def pack(capacity, columns, depth, inner, fanout, level, rings, picked, pack_out, boards, first, size):
    wanted = columns_wanted((columns, LANES), depth, inner, level, 0)
    for s, ring in enumerate(rings):
        half = ring.shape[0] - 3 * SUB
        member, weight, label = route_rows(*routing(ring, fanout), wanted)
        rank = ranked(member)
        named = []
        for j in range(columns):
            rows, labels = slots_of(rank[j:j + 1], weight[j:j + 1], label[j:j + 1], capacity)
            picked[j * capacity:(j + 1) * capacity, :] = rows
            named.append(labels)
        named = in_all_lanes(stacked(*named))
        for j in range(columns):
            labels = named[j * capacity:(j + 1) * capacity]
            boards[j] = place_labels(boards[j], labels, (first + s) * (capacity // SUB))
        planes = pack_out.shape[1] // size // 2
        cells = tile_columns(ring[:half, :], planes, half // planes // TS)
        packed = dot3(picked[...], cells)
        put(pack_out, packed.reshape(columns, capacity, packed.shape[1]), s * capacity, size)
    return boards


def send(pairs, gone):
    copies = [pltpu.make_async_copy(near, far, gone.at[i]) for i, (near, far) in enumerate(pairs)]
    for copy in copies:
        copy.start()
    for copy in copies:
        copy.wait()


def early_kernel(capacity, columns, depth, inner, fanout, total, at, *refs):
    rings, (far, boards_out, picked, out, gone) = refs[:-5], refs[-5:]
    size = len(rings) * capacity
    boards = [jnp.zeros((SUB, LANES), F32) for _ in range(columns)]
    boards = pack(capacity, columns, depth, inner, fanout, at[1], rings, picked, out, boards, 0, size)
    for j in range(columns):
        boards_out[j] = boards[j]
    send(
        [
            (out.at[:, c * size:(c + 1) * size], far.at[:, c * total:c * total + size])
            for c in range(out.shape[1] // size)
        ],
        gone,
    )


def forward_kernel(capacity, columns, depth, inner, fanout, total, at, far_in, boards_in, ring, *refs):
    edges, (far, picked, out, tail, gone) = refs[:-5], refs[-5:]
    del far_in
    boards = [boards_in[j] for j in range(columns)]
    boards = pack(
        capacity, columns, depth, inner, fanout, at[1], [ring], picked, out, boards, total // capacity - 1, capacity
    )
    for j in range(columns):
        tail[j, :SUB, :] = boards[j]
    value = edges[0][...]
    for part in edges[1:]:
        value = value + part[...]
    tail[:, SUB:, :] = value
    parts = out.shape[1] // capacity
    send(
        [
            (out.at[:, c * capacity:(c + 1) * capacity], far.at[:, (c + 1) * total - capacity:(c + 1) * total])
            for c in range(parts)
        ] + [(tail, far.at[:, parts * total:])],
        gone,
    )


def gather_sum(arrived, capacity, groups, total, parts):
    heads, cells = [], []
    for j in range(arrived.shape[0]):
        board = arrived[j, parts * total:parts * total + SUB, :]
        for g in groups:
            heads.append(read_labels(board, g * (capacity // SUB), capacity))
            first = g * capacity
            cells.append(beside(*[
                arrived[j, c * total + first:c * total + first + capacity, :] for c in range(parts)
            ]))
    head = stacked(*heads).astype(BF16)
    high, low = split(stacked(*cells))
    return mm_t(head, high) + mm_t(head, low)


def partial_kernel(capacity, depth, groups, far, *refs):
    outs, (boards, cells, here) = refs[:-3], refs[-3:]
    slots, parts = depth * capacity, outs[0].shape[1] // LANES
    pairs = [(far.at[:, parts * slots:parts * slots + SUB], boards)]
    for i, r in enumerate(groups):
        for c in range(parts):
            first = c * slots + r * capacity
            pairs.append((far.at[:, first:first + capacity], cells.at[i, c]))
    copies = [pltpu.make_async_copy(a, b, here.at[i]) for i, (a, b) in enumerate(pairs)]
    for copy in copies:
        copy.start()
    copies[0].wait()
    for i, (r, out) in enumerate(zip(groups, outs)):
        for copy in copies[1 + i * parts:1 + (i + 1) * parts]:
            copy.wait()
        heads, values = [], []
        for j in range(boards.shape[0]):
            heads.append(read_labels(boards[j], r * (capacity // SUB), capacity))
            values.append(beside(*[cells[i, c, j] for c in range(parts)]))
        head = stacked(*heads).astype(BF16)
        high, low = split(stacked(*values))
        out[...] = mm_t(head, high) + mm_t(head, low)


def edge_sums(proj, weight, label, tiles_x, tiles_y, logs, part):
    label = label.astype(jnp.int32)
    tile_x, tile_y = label // tiles_y, label % tiles_y
    place, other, size = (tile_y, tile_x, tiles_x) if part == 0 else (tile_x, tile_y, tiles_y)
    per = tiles_y if part == 0 else tiles_x
    blocks = weight.shape[0]
    proj = proj[:, part * LANES:(part + 1) * LANES]
    owner = lax.broadcasted_iota(jnp.int32, proj.shape, 1) // TS
    row = lax.broadcasted_iota(jnp.int32, (per, weight.shape[1]), 0)
    here = [place[n:n + 1] == row for n in range(blocks)]
    planes = len(logs)
    left, right = [], []
    for kind in range(2):
        gap = (size - 1 - other if kind == 0 else other).astype(F32)
        for z in range(planes):
            value = weight * jnp.exp(gap * (TS * logs[z]))
            left.append(stacked(*[jnp.where(here[n], value[n:n + 1], 0.0) for n in range(blocks)]))
            right.append(jnp.where(owner == kind * planes + z, proj, 0.0))
    return dot3(beside(*left), stacked(*right)).reshape(blocks, per, LANES)


def own_edges(proj, tiles_x, tiles_y, logs):
    lane = lax.broadcasted_iota(jnp.int32, (SUB, LANES), 1) // TS
    sub = lax.broadcasted_iota(jnp.int32, (SUB, LANES), 0)
    planes = len(logs)
    rate = jnp.zeros((SUB, LANES), F32)
    for z in range(planes):
        rate = jnp.where(lane % planes == z, TS * logs[z], rate)
    to_end = lane < planes
    near = jnp.exp(jnp.where(to_end, tiles_y - 1 - sub, sub).astype(F32) * rate)
    along_x, along_y = jnp.zeros((SUB, LANES), F32), []
    for i in range(tiles_x):
        rows = proj[i * tiles_y:(i + 1) * tiles_y]
        steps = jnp.where(to_end, tiles_x - 1 - i, i).astype(F32)
        along_x = along_x + rows[:, :LANES] * jnp.exp(steps * rate)
        along_y.append(jnp.sum(rows[:, LANES:] * near, axis=0, keepdims=True))
    return along_x[None], stacked(*along_y)[None]


def line_carries(ends, starts, across, first):
    forward, full, running = [], [], jnp.zeros_like(ends[0])
    for end, start in zip(ends, starts):
        forward.append(running)
        full.append(start + first * running)
        running = across * running + end
    backward, running = [], jnp.zeros_like(ends[0])
    for start in full[::-1]:
        backward.append(running)
        running = across * running + start
    return forward, backward[::-1]


def end_start(both, gain, back):
    half = both.shape[1] // 2
    end = both[:, :half]
    return end, gain[:half] * both[:, half:] - back[:half] * end


def edge_kernel(grid_x, depth, inner, planes, fanout, at, logs_in, target, table, lines, coef, both_x, ring, tiled,
                *refs):
    outs, carries = refs[:-1], refs[-1]
    _, cells_x, cells_y = target.shape
    tiles_x, tiles_y = cells_x // TS, cells_y // TS
    half = ring.shape[0] - 3 * SUB
    planes_a = half // cells_x
    logs = [logs_in[z] for z in range(planes)]
    names, tiles, shares = routing(ring, fanout)
    cells = [tile_columns(ring[:half, :], planes_a, tiles_x), tile_columns(tiled[...], planes - planes_a, tiles_x)]
    cells = beside(*cells)
    own_cells = tile_columns(swap_blocks(target[...].reshape(planes * cells_x, LANES)), planes, tiles_x)
    proj = dot3(stacked(cells, own_cells), table[...])
    own = own_edges(proj[cells.shape[0]:], tiles_x, tiles_y, logs)
    proj = proj[:cells.shape[0]]
    tile_count = names.shape[1]
    along = depth * inner
    blocks = grid_x * along
    wanted = lax.broadcasted_iota(jnp.int32, (blocks, tile_count), 0).astype(F32)
    _, weight, label = route_rows(names, tiles, shares, wanted)
    here = at[0] * along + at[1] * inner + at[2]
    edges = []
    for part in range(2):
        sums = edge_sums(proj, weight, label, tiles_x, tiles_y, logs, part)
        is_here = lax.broadcasted_iota(jnp.int32, sums.shape, 0) == here
        sums = jnp.where(is_here, own[part], 0.0) - sums
        edges.append(swap_blocks(sums.reshape(-1, LANES)).reshape(blocks, sums.shape[1] // SUB, SUB, LANES))
    gain, across_x, first_x, back_x, across_y, first_y, back_y = [coef[i][:, :1] for i in range(7)]

    ends, starts = zip(*[
        end_start(edges[0][p * along:(p + 1) * along, 0], gain, back_x) for p in range(grid_x)
    ])
    forward, backward = line_carries(ends, starts, across_x[:planes], first_x[:planes])
    for p in range(grid_x):
        rows = jnp.concatenate([forward[p], backward[p]], axis=1).reshape(depth, inner, SUB, LANES)
        carries[:, p * inner:(p + 1) * inner, :SUB, :] = rows

    side = jnp.concatenate([edges[1][:, i] for i in range(edges[1].shape[1])], axis=2)
    flat = side.reshape(blocks * SUB, cells_x)
    local = jnp.zeros_like(flat)
    for z in range(planes):
        local = local + dot3(masked(flat, planes, z), both_x[z])
    local = local.reshape(side.shape)
    ends = jnp.sum(side * lines[0], axis=2, keepdims=True)
    starts = jnp.sum(side * lines[1], axis=2, keepdims=True)
    forward, backward = line_carries(
        [ends[p * along:(p + 1) * along] for p in range(grid_x)],
        [starts[p * along:(p + 1) * along] for p in range(grid_x)],
        across_x,
        first_x,
    )
    smooth = [
        local[p * along:(p + 1) * along] + forward[p] * lines[2] + backward[p] * lines[3] for p in range(grid_x)
    ]
    smooth = jnp.stack(smooth)
    ends, starts = zip(*[end_start(smooth[:, q], gain, back_y) for q in range(along)])
    forward, backward = line_carries(ends, starts, across_y[:planes], first_y[:planes])
    for q in range(along):
        rows = jnp.concatenate([forward[q], backward[q]], axis=1)
        for p in range(grid_x):
            for i in range(cells_x // LANES):
                carries[q // inner, p * inner + q % inner, (1 + i) * SUB:(2 + i) * SUB, :] = (
                    rows[p, :, i * LANES:(i + 1) * LANES]
                )
    for o, out in enumerate(outs):
        out[...] = carries[turned_by(at[1], o, depth)]


def masked(rows, planes, z):
    row = lax.broadcasted_iota(jnp.int32, rows.shape, 0)
    return jnp.where(row % planes == z, rows, 0.0)


def outer(a, b):
    a_high, a_low = split(a)
    b_high, b_low = split(b)
    return mm_t(stacked(a_high, a_high, a_low), stacked(b_high, b_low, b_high))


def base_kernel(target, potential, both_x, both_y, out):
    for z in range(target.shape[0]):
        out[z] = potential[z] + dot3(dot3(both_x[z], target[z]), both_y[z])


def solve(pushed, before, both_x, both_y):
    return before - dot3(dot3(both_x, pushed), both_y)


def out_copies(near, far, gone, planes, first):
    return [
        pltpu.make_async_copy(near.at[z], far.at[first + z], gone.at[z]) for z in range(planes)
    ]


def near_kernel(capacity, depth, arrived, base_far, both_x, both_y, curve_x, curve_y, pushed_far, next_far, rest_out,
                pushed_out, next_out, pushed_gone, next_gone, base, base_here):
    del base_far
    fetched = pltpu.make_async_copy(next_far, base, base_here)
    fetched.start()
    planes, planes_a = base.shape[0], pushed_out.shape[0]
    cells_x = pushed_out.shape[1]
    total, parts = depth * capacity, 2 * planes_a
    first = parts * total + SUB
    carries = arrived[0, first:, :]
    for j in range(1, arrived.shape[0]):
        carries = carries + arrived[j, first:, :]
    carry_x = carries[:SUB]
    carry_y = beside(*[carries[i:i + SUB] for i in range(SUB, carries.shape[0], SUB)])
    total = gather_sum(arrived, capacity, list(range(depth)), total, parts)
    pushed_out[...] = swap_blocks(tile_rows(total, planes_a, cells_x // TS)).reshape(planes_a, cells_x, LANES)
    copies = out_copies(pushed_out, pushed_far, pushed_gone, planes_a, 0)
    copies += out_copies(next_out, next_far, next_gone, planes_a, 0)
    for copy in copies[:planes_a]:
        copy.start()
    fetched.wait()
    for z in range(planes):
        left = stacked(masked(curve_x[...], planes, z), masked(carry_y, planes, z))
        right = stacked(dot3(carry_x, both_y[z]), curve_y[...])
        before = base[z] + outer(left, right)
        if z < planes_a:
            next_out[z] = solve(pushed_out[z], before, both_x[z], both_y[z])
            copies[planes_a + z].start()
        else:
            rest_out[z - planes_a] = before
    for copy in copies:
        copy.wait()


def far_kernel(first, pushed_in, next_in, base, both_x, both_y, *refs):
    del pushed_in, next_in
    sums, (pushed_far, next_far, pushed_out, next_out, pushed_gone, next_gone) = refs[:-6], refs[-6:]
    count, cells_x, _ = pushed_out.shape
    total = sums[0][...]
    for part in sums[1:]:
        total = total + part[...]
    pushed_out[...] = swap_blocks(tile_rows(total, count, cells_x // TS)).reshape(count, cells_x, LANES)
    copies = out_copies(pushed_out, pushed_far, pushed_gone, count, first)
    copies += out_copies(next_out, next_far, next_gone, count, first)
    for copy in copies[:count]:
        copy.start()
    for z in range(count):
        next_out[z] = solve(pushed_out[z], base[z], both_x[first + z], both_y[first + z])
        copies[count + z].start()
    for copy in copies:
        copy.wait()


def call(name, body, out_shape, in_specs=None, scratch=(), wait=(), **extra):
    def run(*args):
        count, unread = len(args), len(wait)

        def kernel(*refs):
            body(*refs[:count], *refs[count + unread:])

        near = pl.BlockSpec(memory_space=pltpu.VMEM)
        specs = [near] * count if in_specs is None else list(in_specs)
        return pl.pallas_call(
            kernel,
            out_shape=out_shape,
            in_specs=specs + [pl.BlockSpec(memory_space=pl.ANY)] * unread,
            scratch_shapes=list(scratch),
            compiler_params=pltpu.CompilerParams(vmem_limit_bytes=VMEM_LIMIT),
            cost_estimate=pl.CostEstimate(
                flops=int(COST[name] * FLOPS_A_MICRO), bytes_accessed=0, transcendentals=0
            ),
            **extra,
        )(*args, *wait)

    return run


def table_kernel(planes, decay_in, logs_in, table, lines, coef, curve_x, curve_y, both_x, both_y):
    row = lax.broadcasted_iota(jnp.int32, (2 * planes, LANES), 0)
    decay, rate = jnp.zeros(row.shape, F32), jnp.zeros(row.shape, F32)
    for z in range(planes):
        decay = jnp.where(row % planes == z, decay_in[z], decay)
        rate = jnp.where(row % planes == z, logs_in[z], rate)
    gain = (1.0 - decay) / (1.0 + decay)
    coef[0] = gain
    for i, (curve, both) in enumerate(((curve_x, both_x), (curve_y, both_y))):
        length = curve.shape[1]
        across = jnp.exp(length * rate)
        coef[1 + 3 * i] = across
        coef[2 + 3 * i] = gain * decay * (1.0 - across * across)
        coef[3 + 3 * i] = gain * decay * across
        slope, width, turn = rate[:, :1], gain[:, :1], (gain * decay)[:, :1]
        place = lax.broadcasted_iota(jnp.int32, curve.shape, 1).astype(F32)
        risen = jnp.exp(place * slope) - jnp.exp((2.0 * length - place) * slope)
        fall = jnp.exp((length - place) * slope)
        bend = turn * risen
        curve[...] = jnp.where(lax.broadcasted_iota(jnp.int32, curve.shape, 0) < planes, bend, fall)
        if i == 0:
            lines[0] = jnp.exp((length - 1.0 - place) * slope)
            lines[1] = width * risen
            lines[2] = bend
            lines[3] = fall
        rows = lax.broadcasted_iota(jnp.int32, (length, length), 0).astype(F32)
        cols = lax.broadcasted_iota(jnp.int32, (length, length), 1).astype(F32)
        apart, down = jnp.abs(rows - cols), length - rows[:, :1]
        for z in range(planes):
            log = logs_in[z]
            both[z] = width[z:z + 1] * (jnp.exp(apart * log) - jnp.exp(down * log) * fall[z:z + 1])
    cells = TS * TS
    shape = (cells, table.shape[1])
    row, col = lax.broadcasted_iota(jnp.int32, shape, 0), lax.broadcasted_iota(jnp.int32, shape, 1)
    along_y, kind = col // (2 * planes * TS) == 1, col // (planes * TS) % 2
    owner, cell = col // TS % planes, col % TS
    at_x, at_y = row // TS, row % TS
    summed, kept = jnp.where(along_y, at_y, at_x), jnp.where(along_y, at_x, at_y)
    steps = jnp.where(kind == 0, TS - 1 - summed, summed).astype(F32)
    for z in range(planes):
        power = jnp.exp(steps * logs_in[z])
        table[z * cells:(z + 1) * cells, :] = jnp.where((owner == z) & (kept == cell), power, 0.0)


def per_device(source_mass, target_density, potential, dest_device, dest_tile, mass_counts, reach):
    planes, cells_x, cells_y = source_mass.shape
    tile_count, fanout = dest_device.shape[2:]
    tiles_x, tiles_y = cells_x // TS, cells_y // TS
    grid_x, depth, inner = lax.axis_size("gx"), lax.axis_size("z"), lax.axis_size("x")
    columns = grid_x * inner
    device_count = columns * depth
    capacity = max(2, 3 * fanout * tile_count // (2 * device_count))
    capacity = -(-capacity // SUB) * SUB
    slots = depth * capacity
    planes_a = planes // 2
    rest = planes - planes_a
    tile_cells = 2 * LANES
    at = jnp.stack([lax.axis_index("gx"), lax.axis_index("z"), lax.axis_index("x")])
    scalars, near = pl.BlockSpec(memory_space=pltpu.SMEM), pl.BlockSpec(memory_space=pltpu.VMEM)
    far = pl.BlockSpec(memory_space=pl.ANY)

    def array(*shape):
        return jax.ShapeDtypeStruct(shape, F32)

    def turn(x, axis, steps):
        size = lax.axis_size(axis)
        return lax.ppermute(x, axis, [(i, (i + steps) % size) for i in range(size)])

    routes = jnp.stack([x.reshape(tile_count, fanout).T for x in (dest_device, dest_tile, mass_counts)])
    ring, tiled = call(
        "ring", functools.partial(ring_kernel, planes_a),
        [array(planes_a * cells_x + 3 * SUB, LANES), array(rest * cells_x, LANES)],
    )(source_mass, routes.astype(F32))
    rings = [ring] + [None] * (depth - 1)
    for s in range(1, depth // 2 + 1):
        rings[s] = turn(rings[s - 1], "z", 1)
        if s < depth - s:
            rings[depth - s] = turn(rings[(depth - s + 1) % depth], "z", -1)

    packed_b = call(
        "start", functools.partial(start_kernel, capacity, columns, depth, inner, planes_a, fanout),
        array(columns, 2 * rest * slots + SUB, LANES),
        [scalars] + [near] * 2,
        [pltpu.VMEM((columns * depth * capacity, tile_count), F32)],
    )(at, ring, tiled)
    arrived_b = lax.all_to_all(packed_b, ("gx", "x"), 0, 0, tiled=True)
    decay = 1.0 - 1.0 / reach
    logs = jnp.log(decay)
    eight = 2 * planes
    table, lines, coef, curve_x, curve_y, both_x, both_y = call(
        "table", functools.partial(table_kernel, planes),
        [
            array(planes * TS * TS, 4 * planes * TS), array(4, eight, cells_x), array(7, eight, LANES),
            array(eight, cells_x), array(eight, cells_y), array(planes, cells_x, cells_x),
            array(planes, cells_y, cells_y),
        ],
        [scalars] * 2,
        (),
        [ring],
    )(decay, logs)
    edge_rows = tiles_x + tiles_y
    edges = call(
        "edge", functools.partial(edge_kernel, grid_x, depth, inner, planes, fanout),
        [array(columns, edge_rows, LANES)] * depth,
        [scalars] * 2 + [near] * 7,
        [pltpu.VMEM((depth, columns, edge_rows, LANES), F32)],
        [rings[1], packed_b],
    )(at, logs, target_density, table, lines, coef, both_x, ring, tiled)
    edges = [edges[0]] + [turn(edges[o], "z", o) for o in range(1, depth)]
    sums = {}
    for groups in [[depth // 2], [r for r in range(depth) if r != depth // 2]]:
        parts = 2 * rest
        some = call(
            "partial", functools.partial(partial_kernel, capacity, depth, groups),
            [array(tile_count, rest * tile_cells)] * len(groups),
            [far],
            [
                pltpu.VMEM((columns, SUB, LANES), F32),
                pltpu.VMEM((len(groups), parts, columns, capacity, LANES), F32),
                pltpu.SemaphoreType.DMA((1 + len(groups) * parts,)),
            ],
        )(arrived_b)
        sums.update(zip(groups, some))
    moving = {r: sums[r] for r in range(depth)}
    for r in range(depth // 2, 0, -1):
        moving[r - 1] = turn(moving[r], "z", -1) if r == 1 else moving[r - 1] + turn(moving[r], "z", -1)
    moving = [sums[0], moving[0]]
    if depth > 2:
        more = sums[depth // 2 + 1]
        for r in range(depth // 2 + 1, depth):
            more = turn(more, "z", 1)
            if r < depth - 1:
                more = more + sums[r + 1]
        moving.append(more)
    last = depth // 2
    order = [s for s in range(depth) if s != last]
    parts = 2 * planes_a
    packed_a, boards = call(
        "early", functools.partial(early_kernel, capacity, columns, depth, inner, fanout, slots),
        [array(columns, parts * slots + SUB + edge_rows, LANES), array(columns, SUB, LANES)],
        [scalars] + [near] * len(order),
        [
            pltpu.VMEM((columns * capacity, tile_count), F32),
            pltpu.VMEM((columns, parts * (slots - capacity), LANES), F32),
            pltpu.SemaphoreType.DMA((parts,)),
        ],
        out_specs=[far, near],
    )(at, *[rings[s] for s in order])
    packed_a = call(
        "pack", functools.partial(forward_kernel, capacity, columns, depth, inner, fanout, slots),
        array(*packed_a.shape), [scalars, far] + [near] * (2 + len(edges)),
        [
            pltpu.VMEM((columns * capacity, tile_count), F32), pltpu.VMEM((columns, parts * capacity, LANES), F32),
            pltpu.VMEM((columns, SUB + edge_rows, LANES), F32), pltpu.SemaphoreType.DMA((parts + 1,)),
        ],
        out_specs=far, input_output_aliases={1: 0},
    )(at, packed_a, boards, rings[last], *edges)
    arrived_a = lax.all_to_all(packed_a, ("gx", "x"), 0, 0, tiled=True)
    base = call("base", base_kernel, array(*potential.shape), wait=[sums[0]])(
        target_density, potential, both_x, both_y
    )
    shapes = [array(*source_mass.shape), array(*potential.shape)]

    def staged(count):
        return [pltpu.VMEM((count, cells_x, cells_y), F32)] * 2 + [pltpu.SemaphoreType.DMA((count,))] * 2

    *outs, base = call(
        "near", functools.partial(near_kernel, capacity, depth), shapes + [array(rest, cells_x, cells_y)],
        [near, far] + [near] * 4, staged(planes_a) + [pltpu.VMEM(potential.shape, F32), pltpu.SemaphoreType.DMA],
        out_specs=[far, far, near], input_output_aliases={1: 1},
    )(arrived_a, base, both_x, both_y, curve_x, curve_y)
    outs = call(
        "far", functools.partial(far_kernel, planes_a), shapes, [far, far] + [near] * (3 + len(moving)),
        staged(rest), out_specs=[far, far], input_output_aliases={0: 0, 1: 1},
    )(*outs, base, both_x, both_y, *moving)
    return tuple(outs)


def solution(mesh):
    grid_x, grid_y = mesh.shape["gx"], mesh.shape["gy"]
    inner = grid_x // 2
    if inner < 1 or grid_y % inner:
        inner = 1
    depth = grid_y // inner
    split_mesh = Mesh(mesh.devices.reshape(grid_x, depth, inner), ("gx", "z", "x"))
    field = P(None, "gx", ("z", "x"))
    table = P("gx", ("z", "x"), None, None)
    return jax.shard_map(
        per_device,
        mesh=split_mesh,
        in_specs=(field, field, field, table, table, table, P()),
        out_specs=(field, field),
        check_vma=False,
    )
```

```python
import functools

import jax
import jax.numpy as jnp
from jax import lax
from jax.experimental import pallas as pl
from jax.experimental.pallas import tpu as pltpu
from jax.sharding import Mesh
from jax.sharding import PartitionSpec as P

TS = 16
MXU = 256
CHUNKS = 8
SUB = 8
LANES = 128
F32 = jnp.float32
BF16 = jnp.bfloat16
FLOPS_A_MICRO = 1_100_000_000
COST = {
    "ring": 0.8, "start": 2.5, "table": 20.0, "edge": 60.0, "partial": 1.4, "base": 1.0, "early": 1.8, "pack": 1.8,
    "near": 3.5, "far": 1.6,
}
VMEM_LIMIT = 20 * 1024 * 1024


def split(x):
    high = x.astype(BF16)
    return high, (x - high.astype(F32)).astype(BF16)


def mm(a, b):
    return jnp.dot(a, b, preferred_element_type=F32)


def mm_t(a, b):
    return lax.dot_general(a, b, (((0,), (0,)), ((), ())), preferred_element_type=F32)


def beside(*parts):
    return jnp.concatenate(parts, axis=1)


def stacked(*parts):
    return jnp.concatenate(parts, axis=0)


def dot3(a, b):
    a_high, a_low = split(a)
    b_high, b_low = split(b)
    deep, wide = a.shape[1], b.shape[1]
    if 2 * deep <= MXU and 2 * wide <= MXU:
        both = mm(beside(a_high, a_low), stacked(beside(b_high, b_low), beside(b_high, jnp.zeros_like(b_low))))
        return both[:, :wide] + both[:, wide:]
    if 2 * wide <= MXU:
        both = mm(a_high, beside(b_high, b_low))
        return both[:, :wide] + both[:, wide:] + mm(a_low, b_high)
    if 2 * deep <= MXU:
        return mm(beside(a_high, a_low), stacked(b_high, b_high)) + mm(a_high, b_low)
    rows = a.shape[0]
    both = mm(stacked(a_high, a_low), b_high)
    return both[:rows] + both[rows:] + mm(a_high, b_low)


def swap_blocks(x):
    rows = x.shape[0]
    x = x.reshape(rows // SUB, SUB, LANES)
    sub = lax.broadcasted_iota(jnp.int32, x.shape, 1)
    block = lax.broadcasted_iota(jnp.int32, x.shape, 2) // TS
    for k in (4, 2, 1):
        up = pltpu.roll(pltpu.roll(x, SUB - k, 1), TS * k, 2)
        down = up if 2 * k == SUB else pltpu.roll(pltpu.roll(x, k, 1), LANES - TS * k, 2)
        moved = jnp.where((sub & k) == 0, up, down)
        x = jnp.where((sub & k) == (block & k), x, moved)
    return x.reshape(rows, LANES)


def tile_columns(tiled, planes, tiles_x):
    grouped = tiled.reshape(planes, tiles_x, 2, SUB, LANES)
    columns = [grouped[z, :, h].reshape(tiles_x * SUB, LANES) for z in range(planes) for h in range(2)]
    return jnp.concatenate(columns, axis=1)


def tile_rows(columns, planes, tiles_x):
    parts = [
        columns[:, i * LANES:(i + 1) * LANES].reshape(1, tiles_x, 1, SUB, LANES) for i in range(2 * planes)
    ]
    planes_of = [jnp.concatenate(parts[2 * z:2 * z + 2], axis=2) for z in range(planes)]
    return jnp.concatenate(planes_of, axis=0).reshape(planes * tiles_x * TS, LANES)


def route_rows(names, tiles, shares, wanted):
    fanout, count = names.shape
    member = jnp.zeros(wanted.shape, F32)
    weight = jnp.zeros(wanted.shape, F32)
    label = jnp.zeros(wanted.shape, F32)
    for k in range(fanout):
        hit = names[k:k + 1, :] == wanted
        member = member + jnp.where(hit, 1.0, 0.0)
        weight = weight + jnp.where(hit, shares[k:k + 1, :], 0.0)
        label = label + jnp.where(hit, tiles[k:k + 1, :], 0.0)
    return member, weight, label


def ranked(member):
    count = member.shape[1]
    before = lax.broadcasted_iota(jnp.int32, (count, count), 0) < lax.broadcasted_iota(
        jnp.int32, (count, count), 1
    )
    rank = mm(member.astype(BF16), jnp.where(before, 1.0, 0.0).astype(BF16))
    return jnp.where(member > 0.0, rank, 2.0 * count)


def slots_of(rank, weight, label, capacity):
    slot = lax.broadcasted_iota(jnp.int32, (capacity, rank.shape[1]), 0).astype(F32)
    chosen = rank == slot
    return jnp.where(chosen, weight, 0.0), jnp.where(chosen, label, 0.0)


def in_all_lanes(rows):
    return mm(rows.astype(BF16), jnp.ones((rows.shape[1], LANES), BF16))


def place_labels(board, labels, first):
    lane = lax.broadcasted_iota(jnp.int32, board.shape, 1)
    for g in range(labels.shape[0] // SUB):
        board = jnp.where(lane == first + g, labels[g * SUB:(g + 1) * SUB], board)
    return board


def read_labels(board, first, capacity):
    lane = lax.broadcasted_iota(jnp.int32, (SUB, LANES), 1).astype(F32)
    rows = [
        jnp.where(board[:, first + g:first + g + 1] == lane, 1.0, 0.0) for g in range(capacity // SUB)
    ]
    return jnp.concatenate(rows, axis=0)


def turned_by(at, steps, size):
    at = at + steps
    return jnp.where(at >= size, at - size, at)


def columns_wanted(shape, depth, inner, level, steps):
    row = lax.broadcasted_iota(jnp.int32, shape, 0)
    column, steps = (row // depth, row % depth) if steps is None else (row, steps)
    level = turned_by(level, depth - steps, depth)
    return (column // inner * (depth * inner) + level * inner + column % inner).astype(F32)


def ring_kernel(planes_a, source, routes, ring, tiled):
    planes, cells_x, _ = source.shape
    half = planes_a * cells_x
    fanout = routes.shape[1]
    ring[:half, :] = swap_blocks(source[:planes_a].reshape(half, LANES))
    ring[half:, :] = jnp.zeros((3 * SUB, LANES), F32)
    ring[half:half + fanout, :] = routes[0]
    ring[half + SUB:half + SUB + fanout, :] = routes[1]
    ring[half + 2 * SUB:half + 2 * SUB + fanout, :] = routes[2] / jnp.sum(routes[2], axis=0, keepdims=True)
    tiled[...] = swap_blocks(source[planes_a:].reshape(tiled.shape[0], LANES))


def start_kernel(capacity, columns, depth, inner, planes_a, fanout, at, ring, tiled, far, out, gone):
    cells_x = (ring.shape[0] - 3 * SUB) // planes_a
    rest = tiled.shape[0] // cells_x
    names, tiles, shares = routing(ring, fanout)
    wanted = columns_wanted((columns * depth, LANES), depth, inner, at[1], None)
    member, weight, label = route_rows(names, tiles, shares, wanted)
    rank = ranked(member)
    cells = tile_columns(tiled[...], rest, cells_x // TS)
    slots = depth * capacity
    step = columns // gone.shape[0]
    copies = []
    for first in range(0, columns, step):
        picked, named = [], []
        for n in range(first * depth, (first + step) * depth):
            rows, labels = slots_of(rank[n:n + 1], weight[n:n + 1], label[n:n + 1], capacity)
            picked.append(rows)
            named.append(labels)
        packed = dot3(stacked(*picked), cells)
        named = in_all_lanes(stacked(*named))
        put(out.at[first:first + step], packed.reshape(step, slots, packed.shape[1]))
        for j in range(step):
            board = jnp.zeros((SUB, LANES), F32)
            out[first + j, out.shape[1] - SUB:, :] = place_labels(board, named[j * slots:(j + 1) * slots], 0)
        there = slice(first, first + step)
        copies.append(pltpu.make_async_copy(out.at[there], far.at[there], gone.at[first // step]))
        copies[-1].start()
    for copy in copies:
        copy.wait()


def put(out, slots, first=0, size=None):
    count = slots.shape[1]
    size = count if size is None else size
    for c in range(slots.shape[2] // LANES):
        out[:, c * size + first:c * size + first + count, :] = slots[:, :, c * LANES:(c + 1) * LANES]


def routing(ring, fanout):
    first = ring.shape[0] - 3 * SUB
    return [ring[first + k * SUB:first + k * SUB + fanout, :] for k in range(3)]


def pack(capacity, columns, depth, inner, fanout, level, rings, picked, pack_out, boards, first, size):
    wanted = columns_wanted((columns, LANES), depth, inner, level, 0)
    for s, ring in enumerate(rings):
        half = ring.shape[0] - 3 * SUB
        member, weight, label = route_rows(*routing(ring, fanout), wanted)
        rank = ranked(member)
        named = []
        for j in range(columns):
            rows, labels = slots_of(rank[j:j + 1], weight[j:j + 1], label[j:j + 1], capacity)
            picked[j * capacity:(j + 1) * capacity, :] = rows
            named.append(labels)
        named = in_all_lanes(stacked(*named))
        for j in range(columns):
            labels = named[j * capacity:(j + 1) * capacity]
            boards[j] = place_labels(boards[j], labels, (first + s) * (capacity // SUB))
        planes = pack_out.shape[1] // size // 2
        cells = tile_columns(ring[:half, :], planes, half // planes // TS)
        packed = dot3(picked[...], cells)
        put(pack_out, packed.reshape(columns, capacity, packed.shape[1]), s * capacity, size)
    return boards


def send(pairs, gone):
    copies = [pltpu.make_async_copy(near, far, gone.at[i]) for i, (near, far) in enumerate(pairs)]
    for copy in copies:
        copy.start()
    for copy in copies:
        copy.wait()


def early_kernel(capacity, columns, depth, inner, fanout, total, at, *refs):
    rings, (far, boards_out, picked, out, gone) = refs[:-5], refs[-5:]
    size = len(rings) * capacity
    boards = [jnp.zeros((SUB, LANES), F32) for _ in range(columns)]
    boards = pack(capacity, columns, depth, inner, fanout, at[1], rings, picked, out, boards, 0, size)
    for j in range(columns):
        boards_out[j] = boards[j]
    send(
        [
            (out.at[:, c * size:(c + 1) * size], far.at[:, c * total:c * total + size])
            for c in range(out.shape[1] // size)
        ],
        gone,
    )


def forward_kernel(capacity, columns, depth, inner, fanout, total, at, far_in, boards_in, ring, *refs):
    edges, (far, picked, out, tail, gone) = refs[:-5], refs[-5:]
    del far_in
    boards = [boards_in[j] for j in range(columns)]
    boards = pack(
        capacity, columns, depth, inner, fanout, at[1], [ring], picked, out, boards, total // capacity - 1, capacity
    )
    for j in range(columns):
        tail[j, :SUB, :] = boards[j]
    value = edges[0][...]
    for part in edges[1:]:
        value = value + part[...]
    tail[:, SUB:, :] = value
    parts = out.shape[1] // capacity
    send(
        [
            (out.at[:, c * capacity:(c + 1) * capacity], far.at[:, (c + 1) * total - capacity:(c + 1) * total])
            for c in range(parts)
        ] + [(tail, far.at[:, parts * total:])],
        gone,
    )


def gather_sum(arrived, capacity, groups, total, parts):
    heads, cells = [], []
    for j in range(arrived.shape[0]):
        board = arrived[j, parts * total:parts * total + SUB, :]
        for g in groups:
            heads.append(read_labels(board, g * (capacity // SUB), capacity))
            first = g * capacity
            cells.append(beside(*[
                arrived[j, c * total + first:c * total + first + capacity, :] for c in range(parts)
            ]))
    head = stacked(*heads).astype(BF16)
    high, low = split(stacked(*cells))
    return mm_t(head, high) + mm_t(head, low)


def partial_kernel(capacity, depth, groups, far, *refs):
    outs, (boards, cells, here) = refs[:-3], refs[-3:]
    slots, parts = depth * capacity, outs[0].shape[1] // LANES
    pairs = [(far.at[:, parts * slots:parts * slots + SUB], boards)]
    for i, r in enumerate(groups):
        for c in range(parts):
            first = c * slots + r * capacity
            pairs.append((far.at[:, first:first + capacity], cells.at[i, c]))
    copies = [pltpu.make_async_copy(a, b, here.at[i]) for i, (a, b) in enumerate(pairs)]
    for copy in copies:
        copy.start()
    copies[0].wait()
    for i, (r, out) in enumerate(zip(groups, outs)):
        for copy in copies[1 + i * parts:1 + (i + 1) * parts]:
            copy.wait()
        heads, values = [], []
        for j in range(boards.shape[0]):
            heads.append(read_labels(boards[j], r * (capacity // SUB), capacity))
            values.append(beside(*[cells[i, c, j] for c in range(parts)]))
        head = stacked(*heads).astype(BF16)
        high, low = split(stacked(*values))
        out[...] = mm_t(head, high) + mm_t(head, low)


def edge_sums(proj, weight, label, tiles_x, tiles_y, logs, part):
    label = label.astype(jnp.int32)
    tile_x, tile_y = label // tiles_y, label % tiles_y
    place, other, size = (tile_y, tile_x, tiles_x) if part == 0 else (tile_x, tile_y, tiles_y)
    per = tiles_y if part == 0 else tiles_x
    blocks = weight.shape[0]
    proj = proj[:, part * LANES:(part + 1) * LANES]
    owner = lax.broadcasted_iota(jnp.int32, proj.shape, 1) // TS
    row = lax.broadcasted_iota(jnp.int32, (per, weight.shape[1]), 0)
    here = [place[n:n + 1] == row for n in range(blocks)]
    planes = len(logs)
    left, right = [], []
    for kind in range(2):
        gap = (size - 1 - other if kind == 0 else other).astype(F32)
        for z in range(planes):
            value = weight * jnp.exp(gap * (TS * logs[z]))
            left.append(stacked(*[jnp.where(here[n], value[n:n + 1], 0.0) for n in range(blocks)]))
            right.append(jnp.where(owner == kind * planes + z, proj, 0.0))
    return dot3(beside(*left), stacked(*right)).reshape(blocks, per, LANES)


def own_edges(proj, tiles_x, tiles_y, logs):
    lane = lax.broadcasted_iota(jnp.int32, (SUB, LANES), 1) // TS
    sub = lax.broadcasted_iota(jnp.int32, (SUB, LANES), 0)
    planes = len(logs)
    rate = jnp.zeros((SUB, LANES), F32)
    for z in range(planes):
        rate = jnp.where(lane % planes == z, TS * logs[z], rate)
    to_end = lane < planes
    near = jnp.exp(jnp.where(to_end, tiles_y - 1 - sub, sub).astype(F32) * rate)
    along_x, along_y = jnp.zeros((SUB, LANES), F32), []
    for i in range(tiles_x):
        rows = proj[i * tiles_y:(i + 1) * tiles_y]
        steps = jnp.where(to_end, tiles_x - 1 - i, i).astype(F32)
        along_x = along_x + rows[:, :LANES] * jnp.exp(steps * rate)
        along_y.append(jnp.sum(rows[:, LANES:] * near, axis=0, keepdims=True))
    return along_x[None], stacked(*along_y)[None]


def line_carries(ends, starts, across, first):
    forward, full, running = [], [], jnp.zeros_like(ends[0])
    for end, start in zip(ends, starts):
        forward.append(running)
        full.append(start + first * running)
        running = across * running + end
    backward, running = [], jnp.zeros_like(ends[0])
    for start in full[::-1]:
        backward.append(running)
        running = across * running + start
    return forward, backward[::-1]


def end_start(both, gain, back):
    half = both.shape[1] // 2
    end = both[:, :half]
    return end, gain[:half] * both[:, half:] - back[:half] * end


def edge_kernel(grid_x, depth, inner, planes, fanout, at, logs_in, target, table, lines, coef, both_x, ring, tiled,
                *refs):
    outs, carries = refs[:-1], refs[-1]
    _, cells_x, cells_y = target.shape
    tiles_x, tiles_y = cells_x // TS, cells_y // TS
    half = ring.shape[0] - 3 * SUB
    planes_a = half // cells_x
    logs = [logs_in[z] for z in range(planes)]
    names, tiles, shares = routing(ring, fanout)
    cells = [tile_columns(ring[:half, :], planes_a, tiles_x), tile_columns(tiled[...], planes - planes_a, tiles_x)]
    cells = beside(*cells)
    own_cells = tile_columns(swap_blocks(target[...].reshape(planes * cells_x, LANES)), planes, tiles_x)
    proj = dot3(stacked(cells, own_cells), table[...])
    own = own_edges(proj[cells.shape[0]:], tiles_x, tiles_y, logs)
    proj = proj[:cells.shape[0]]
    tile_count = names.shape[1]
    along = depth * inner
    blocks = grid_x * along
    wanted = lax.broadcasted_iota(jnp.int32, (blocks, tile_count), 0).astype(F32)
    _, weight, label = route_rows(names, tiles, shares, wanted)
    here = at[0] * along + at[1] * inner + at[2]
    edges = []
    for part in range(2):
        sums = edge_sums(proj, weight, label, tiles_x, tiles_y, logs, part)
        is_here = lax.broadcasted_iota(jnp.int32, sums.shape, 0) == here
        sums = jnp.where(is_here, own[part], 0.0) - sums
        edges.append(swap_blocks(sums.reshape(-1, LANES)).reshape(blocks, sums.shape[1] // SUB, SUB, LANES))
    gain, across_x, first_x, back_x, across_y, first_y, back_y = [coef[i][:, :1] for i in range(7)]

    ends, starts = zip(*[
        end_start(edges[0][p * along:(p + 1) * along, 0], gain, back_x) for p in range(grid_x)
    ])
    forward, backward = line_carries(ends, starts, across_x[:planes], first_x[:planes])
    for p in range(grid_x):
        rows = jnp.concatenate([forward[p], backward[p]], axis=1).reshape(depth, inner, SUB, LANES)
        carries[:, p * inner:(p + 1) * inner, :SUB, :] = rows

    side = jnp.concatenate([edges[1][:, i] for i in range(edges[1].shape[1])], axis=2)
    flat = side.reshape(blocks * SUB, cells_x)
    local = jnp.zeros_like(flat)
    for z in range(planes):
        local = local + dot3(masked(flat, planes, z), both_x[z])
    local = local.reshape(side.shape)
    ends = jnp.sum(side * lines[0], axis=2, keepdims=True)
    starts = jnp.sum(side * lines[1], axis=2, keepdims=True)
    forward, backward = line_carries(
        [ends[p * along:(p + 1) * along] for p in range(grid_x)],
        [starts[p * along:(p + 1) * along] for p in range(grid_x)],
        across_x,
        first_x,
    )
    smooth = [
        local[p * along:(p + 1) * along] + forward[p] * lines[2] + backward[p] * lines[3] for p in range(grid_x)
    ]
    smooth = jnp.stack(smooth)
    ends, starts = zip(*[end_start(smooth[:, q], gain, back_y) for q in range(along)])
    forward, backward = line_carries(ends, starts, across_y[:planes], first_y[:planes])
    for q in range(along):
        rows = jnp.concatenate([forward[q], backward[q]], axis=1)
        for p in range(grid_x):
            for i in range(cells_x // LANES):
                carries[q // inner, p * inner + q % inner, (1 + i) * SUB:(2 + i) * SUB, :] = (
                    rows[p, :, i * LANES:(i + 1) * LANES]
                )
    for o, out in enumerate(outs):
        out[...] = carries[turned_by(at[1], o, depth)]


def masked(rows, planes, z):
    row = lax.broadcasted_iota(jnp.int32, rows.shape, 0)
    return jnp.where(row % planes == z, rows, 0.0)


def outer(a, b):
    a_high, a_low = split(a)
    b_high, b_low = split(b)
    return mm_t(stacked(a_high, a_high, a_low), stacked(b_high, b_low, b_high))


def base_kernel(target, potential, both_x, both_y, out):
    for z in range(target.shape[0]):
        out[z] = potential[z] + dot3(dot3(both_x[z], target[z]), both_y[z])


def solve(pushed, before, both_x, both_y):
    return before - dot3(dot3(both_x, pushed), both_y)


def out_copies(near, far, gone, planes, first):
    return [
        pltpu.make_async_copy(near.at[z], far.at[first + z], gone.at[z]) for z in range(planes)
    ]


def near_kernel(capacity, depth, arrived, base_far, both_x, both_y, curve_x, curve_y, pushed_far, next_far, rest_out,
                pushed_out, next_out, pushed_gone, next_gone, base, base_here):
    del base_far
    fetched = pltpu.make_async_copy(next_far, base, base_here)
    fetched.start()
    planes, planes_a = base.shape[0], pushed_out.shape[0]
    cells_x = pushed_out.shape[1]
    total, parts = depth * capacity, 2 * planes_a
    first = parts * total + SUB
    carries = arrived[0, first:, :]
    for j in range(1, arrived.shape[0]):
        carries = carries + arrived[j, first:, :]
    carry_x = carries[:SUB]
    carry_y = beside(*[carries[i:i + SUB] for i in range(SUB, carries.shape[0], SUB)])
    total = gather_sum(arrived, capacity, list(range(depth)), total, parts)
    pushed_out[...] = swap_blocks(tile_rows(total, planes_a, cells_x // TS)).reshape(planes_a, cells_x, LANES)
    copies = out_copies(pushed_out, pushed_far, pushed_gone, planes_a, 0)
    copies += out_copies(next_out, next_far, next_gone, planes_a, 0)
    for copy in copies[:planes_a]:
        copy.start()
    fetched.wait()
    for z in range(planes):
        left = stacked(masked(curve_x[...], planes, z), masked(carry_y, planes, z))
        right = stacked(dot3(carry_x, both_y[z]), curve_y[...])
        before = base[z] + outer(left, right)
        if z < planes_a:
            next_out[z] = solve(pushed_out[z], before, both_x[z], both_y[z])
            copies[planes_a + z].start()
        else:
            rest_out[z - planes_a] = before
    for copy in copies:
        copy.wait()


def far_kernel(first, pushed_in, next_in, base, both_x, both_y, *refs):
    del pushed_in, next_in
    sums, (pushed_far, next_far, pushed_out, next_out, pushed_gone, next_gone) = refs[:-6], refs[-6:]
    count, cells_x, _ = pushed_out.shape
    total = sums[0][...]
    for part in sums[1:]:
        total = total + part[...]
    pushed_out[...] = swap_blocks(tile_rows(total, count, cells_x // TS)).reshape(count, cells_x, LANES)
    copies = out_copies(pushed_out, pushed_far, pushed_gone, count, first)
    copies += out_copies(next_out, next_far, next_gone, count, first)
    for copy in copies[:count]:
        copy.start()
    for z in range(count):
        next_out[z] = solve(pushed_out[z], base[z], both_x[first + z], both_y[first + z])
        copies[count + z].start()
    for copy in copies:
        copy.wait()


def call(name, body, out_shape, in_specs=None, scratch=(), wait=(), **extra):
    def run(*args):
        count, unread = len(args), len(wait)

        def kernel(*refs):
            body(*refs[:count], *refs[count + unread:])

        near = pl.BlockSpec(memory_space=pltpu.VMEM)
        specs = [near] * count if in_specs is None else list(in_specs)
        return pl.pallas_call(
            kernel,
            out_shape=out_shape,
            in_specs=specs + [pl.BlockSpec(memory_space=pl.ANY)] * unread,
            scratch_shapes=list(scratch),
            compiler_params=pltpu.CompilerParams(vmem_limit_bytes=VMEM_LIMIT),
            cost_estimate=pl.CostEstimate(
                flops=int(COST[name] * FLOPS_A_MICRO), bytes_accessed=0, transcendentals=0
            ),
            **extra,
        )(*args, *wait)

    return run


def table_kernel(planes, decay_in, logs_in, table, lines, coef, curve_x, curve_y, both_x, both_y):
    row = lax.broadcasted_iota(jnp.int32, (2 * planes, LANES), 0)
    decay, rate = jnp.zeros(row.shape, F32), jnp.zeros(row.shape, F32)
    for z in range(planes):
        decay = jnp.where(row % planes == z, decay_in[z], decay)
        rate = jnp.where(row % planes == z, logs_in[z], rate)
    gain = (1.0 - decay) / (1.0 + decay)
    coef[0] = gain
    for i, (curve, both) in enumerate(((curve_x, both_x), (curve_y, both_y))):
        length = curve.shape[1]
        across = jnp.exp(length * rate)
        coef[1 + 3 * i] = across
        coef[2 + 3 * i] = gain * decay * (1.0 - across * across)
        coef[3 + 3 * i] = gain * decay * across
        slope, width, turn = rate[:, :1], gain[:, :1], (gain * decay)[:, :1]
        place = lax.broadcasted_iota(jnp.int32, curve.shape, 1).astype(F32)
        risen = jnp.exp(place * slope) - jnp.exp((2.0 * length - place) * slope)
        fall = jnp.exp((length - place) * slope)
        bend = turn * risen
        curve[...] = jnp.where(lax.broadcasted_iota(jnp.int32, curve.shape, 0) < planes, bend, fall)
        if i == 0:
            lines[0] = jnp.exp((length - 1.0 - place) * slope)
            lines[1] = width * risen
            lines[2] = bend
            lines[3] = fall
        rows = lax.broadcasted_iota(jnp.int32, (length, length), 0).astype(F32)
        cols = lax.broadcasted_iota(jnp.int32, (length, length), 1).astype(F32)
        apart, down = jnp.abs(rows - cols), length - rows[:, :1]
        for z in range(planes):
            log = logs_in[z]
            both[z] = width[z:z + 1] * (jnp.exp(apart * log) - jnp.exp(down * log) * fall[z:z + 1])
    cells = TS * TS
    shape = (cells, table.shape[1])
    row, col = lax.broadcasted_iota(jnp.int32, shape, 0), lax.broadcasted_iota(jnp.int32, shape, 1)
    along_y, kind = col // (2 * planes * TS) == 1, col // (planes * TS) % 2
    owner, cell = col // TS % planes, col % TS
    at_x, at_y = row // TS, row % TS
    summed, kept = jnp.where(along_y, at_y, at_x), jnp.where(along_y, at_x, at_y)
    steps = jnp.where(kind == 0, TS - 1 - summed, summed).astype(F32)
    for z in range(planes):
        power = jnp.exp(steps * logs_in[z])
        table[z * cells:(z + 1) * cells, :] = jnp.where((owner == z) & (kept == cell), power, 0.0)


def per_device(source_mass, target_density, potential, dest_device, dest_tile, mass_counts, reach):
    planes, cells_x, cells_y = source_mass.shape
    tile_count, fanout = dest_device.shape[2:]
    tiles_x, tiles_y = cells_x // TS, cells_y // TS
    grid_x, depth, inner = lax.axis_size("gx"), lax.axis_size("z"), lax.axis_size("x")
    columns = grid_x * inner
    device_count = columns * depth
    capacity = max(2, 3 * fanout * tile_count // (2 * device_count))
    capacity = -(-capacity // SUB) * SUB
    slots = depth * capacity
    planes_a = planes // 2
    rest = planes - planes_a
    tile_cells = 2 * LANES
    at = jnp.stack([lax.axis_index("gx"), lax.axis_index("z"), lax.axis_index("x")])
    scalars, near = pl.BlockSpec(memory_space=pltpu.SMEM), pl.BlockSpec(memory_space=pltpu.VMEM)
    far = pl.BlockSpec(memory_space=pl.ANY)

    def array(*shape):
        return jax.ShapeDtypeStruct(shape, F32)

    def turn(x, axis, steps):
        size = lax.axis_size(axis)
        return lax.ppermute(x, axis, [(i, (i + steps) % size) for i in range(size)])

    routes = jnp.stack([x.reshape(tile_count, fanout).T for x in (dest_device, dest_tile, mass_counts)])
    ring, tiled = call(
        "ring", functools.partial(ring_kernel, planes_a),
        [array(planes_a * cells_x + 3 * SUB, LANES), array(rest * cells_x, LANES)],
    )(source_mass, routes.astype(F32))
    rings = [ring] + [None] * (depth - 1)
    for s in range(1, depth // 2 + 1):
        rings[s] = turn(rings[s - 1], "z", 1)
        if s < depth - s:
            rings[depth - s] = turn(rings[(depth - s + 1) % depth], "z", -1)

    packed_b = call(
        "start", functools.partial(start_kernel, capacity, columns, depth, inner, planes_a, fanout),
        array(columns, 2 * rest * slots + SUB, LANES),
        [scalars] + [near] * 2,
        [
            pltpu.VMEM((columns, 2 * rest * slots + SUB, LANES), F32),
            pltpu.SemaphoreType.DMA((CHUNKS if columns % CHUNKS == 0 else 1,)),
        ],
        out_specs=far,
    )(at, ring, tiled)
    arrived_b = lax.all_to_all(packed_b, ("gx", "x"), 0, 0, tiled=True)
    decay = 1.0 - 1.0 / reach
    logs = jnp.log(decay)
    eight = 2 * planes
    table, lines, coef, curve_x, curve_y, both_x, both_y = call(
        "table", functools.partial(table_kernel, planes),
        [
            array(planes * TS * TS, 4 * planes * TS), array(4, eight, cells_x), array(7, eight, LANES),
            array(eight, cells_x), array(eight, cells_y), array(planes, cells_x, cells_x),
            array(planes, cells_y, cells_y),
        ],
        [scalars] * 2,
        (),
        [ring],
    )(decay, logs)
    edge_rows = tiles_x + tiles_y
    edges = call(
        "edge", functools.partial(edge_kernel, grid_x, depth, inner, planes, fanout),
        [array(columns, edge_rows, LANES)] * depth,
        [scalars] * 2 + [near] * 7,
        [pltpu.VMEM((depth, columns, edge_rows, LANES), F32)],
        [rings[1], packed_b],
    )(at, logs, target_density, table, lines, coef, both_x, ring, tiled)
    edges = [edges[0]] + [turn(edges[o], "z", o) for o in range(1, depth)]
    sums = {}
    for groups in [[depth // 2], [r for r in range(depth) if r != depth // 2]]:
        parts = 2 * rest
        some = call(
            "partial", functools.partial(partial_kernel, capacity, depth, groups),
            [array(tile_count, rest * tile_cells)] * len(groups),
            [far],
            [
                pltpu.VMEM((columns, SUB, LANES), F32),
                pltpu.VMEM((len(groups), parts, columns, capacity, LANES), F32),
                pltpu.SemaphoreType.DMA((1 + len(groups) * parts,)),
            ],
        )(arrived_b)
        sums.update(zip(groups, some))
    moving = {r: sums[r] for r in range(depth)}
    for r in range(depth // 2, 0, -1):
        moving[r - 1] = turn(moving[r], "z", -1) if r == 1 else moving[r - 1] + turn(moving[r], "z", -1)
    moving = [sums[0], moving[0]]
    if depth > 2:
        more = sums[depth // 2 + 1]
        for r in range(depth // 2 + 1, depth):
            more = turn(more, "z", 1)
            if r < depth - 1:
                more = more + sums[r + 1]
        moving.append(more)
    last = depth // 2
    order = [s for s in range(depth) if s != last]
    parts = 2 * planes_a
    packed_a, boards = call(
        "early", functools.partial(early_kernel, capacity, columns, depth, inner, fanout, slots),
        [array(columns, parts * slots + SUB + edge_rows, LANES), array(columns, SUB, LANES)],
        [scalars] + [near] * len(order),
        [
            pltpu.VMEM((columns * capacity, tile_count), F32),
            pltpu.VMEM((columns, parts * (slots - capacity), LANES), F32),
            pltpu.SemaphoreType.DMA((parts,)),
        ],
        out_specs=[far, near],
    )(at, *[rings[s] for s in order])
    packed_a = call(
        "pack", functools.partial(forward_kernel, capacity, columns, depth, inner, fanout, slots),
        array(*packed_a.shape), [scalars, far] + [near] * (2 + len(edges)),
        [
            pltpu.VMEM((columns * capacity, tile_count), F32), pltpu.VMEM((columns, parts * capacity, LANES), F32),
            pltpu.VMEM((columns, SUB + edge_rows, LANES), F32), pltpu.SemaphoreType.DMA((parts + 1,)),
        ],
        out_specs=far, input_output_aliases={1: 0},
    )(at, packed_a, boards, rings[last], *edges)
    arrived_a = lax.all_to_all(packed_a, ("gx", "x"), 0, 0, tiled=True)
    base = call("base", base_kernel, array(*potential.shape), wait=[sums[0]])(
        target_density, potential, both_x, both_y
    )
    shapes = [array(*source_mass.shape), array(*potential.shape)]

    def staged(count):
        return [pltpu.VMEM((count, cells_x, cells_y), F32)] * 2 + [pltpu.SemaphoreType.DMA((count,))] * 2

    *outs, base = call(
        "near", functools.partial(near_kernel, capacity, depth), shapes + [array(rest, cells_x, cells_y)],
        [near, far] + [near] * 4, staged(planes_a) + [pltpu.VMEM(potential.shape, F32), pltpu.SemaphoreType.DMA],
        out_specs=[far, far, near], input_output_aliases={1: 1},
    )(arrived_a, base, both_x, both_y, curve_x, curve_y)
    outs = call(
        "far", functools.partial(far_kernel, planes_a), shapes, [far, far] + [near] * (3 + len(moving)),
        staged(rest), out_specs=[far, far], input_output_aliases={0: 0, 1: 1},
    )(*outs, base, both_x, both_y, *moving)
    return tuple(outs)


def solution(mesh):
    grid_x, grid_y = mesh.shape["gx"], mesh.shape["gy"]
    inner = grid_x // 2
    if inner < 1 or grid_y % inner:
        inner = 1
    depth = grid_y // inner
    split_mesh = Mesh(mesh.devices.reshape(grid_x, depth, inner), ("gx", "z", "x"))
    field = P(None, "gx", ("z", "x"))
    table = P("gx", ("z", "x"), None, None)
    return jax.shard_map(
        per_device,
        mesh=split_mesh,
        in_specs=(field, field, field, table, table, table, P()),
        out_specs=(field, field),
        check_vma=False,
    )
```

```python
import functools

import jax
import jax.numpy as jnp
from jax import lax
from jax.experimental import pallas as pl
from jax.experimental.pallas import tpu as pltpu
from jax.sharding import Mesh
from jax.sharding import PartitionSpec as P

TS = 16
MXU = 256
CHUNKS = 8
SUB = 8
LANES = 128
F32 = jnp.float32
BF16 = jnp.bfloat16
FLOPS_A_MICRO = 1_100_000_000
COST = {
    "ring": 0.8, "start": 2.5, "table": 20.0, "edge": 60.0, "partial": 1.4, "base": 1.0, "early": 1.8, "pack": 1.8,
    "near": 3.5, "far": 1.6,
}
VMEM_LIMIT = 20 * 1024 * 1024


def split(x):
    high = x.astype(BF16)
    return high, (x - high.astype(F32)).astype(BF16)


def mm(a, b):
    return jnp.dot(a, b, preferred_element_type=F32)


def mm_t(a, b):
    return lax.dot_general(a, b, (((0,), (0,)), ((), ())), preferred_element_type=F32)


def beside(*parts):
    return jnp.concatenate(parts, axis=1)


def stacked(*parts):
    return jnp.concatenate(parts, axis=0)


def dot3(a, b):
    a_high, a_low = split(a)
    b_high, b_low = split(b)
    deep, wide = a.shape[1], b.shape[1]
    if 2 * deep <= MXU and 2 * wide <= MXU:
        both = mm(beside(a_high, a_low), stacked(beside(b_high, b_low), beside(b_high, jnp.zeros_like(b_low))))
        return both[:, :wide] + both[:, wide:]
    if 2 * wide <= MXU:
        both = mm(a_high, beside(b_high, b_low))
        return both[:, :wide] + both[:, wide:] + mm(a_low, b_high)
    if 2 * deep <= MXU:
        return mm(beside(a_high, a_low), stacked(b_high, b_high)) + mm(a_high, b_low)
    rows = a.shape[0]
    both = mm(stacked(a_high, a_low), b_high)
    return both[:rows] + both[rows:] + mm(a_high, b_low)


def swap_blocks(x):
    rows = x.shape[0]
    x = x.reshape(rows // SUB, SUB, LANES)
    sub = lax.broadcasted_iota(jnp.int32, x.shape, 1)
    block = lax.broadcasted_iota(jnp.int32, x.shape, 2) // TS
    for k in (4, 2, 1):
        up = pltpu.roll(pltpu.roll(x, SUB - k, 1), TS * k, 2)
        down = up if 2 * k == SUB else pltpu.roll(pltpu.roll(x, k, 1), LANES - TS * k, 2)
        moved = jnp.where((sub & k) == 0, up, down)
        x = jnp.where((sub & k) == (block & k), x, moved)
    return x.reshape(rows, LANES)


def tile_columns(tiled, planes, tiles_x):
    grouped = tiled.reshape(planes, tiles_x, 2, SUB, LANES)
    columns = [grouped[z, :, h].reshape(tiles_x * SUB, LANES) for z in range(planes) for h in range(2)]
    return jnp.concatenate(columns, axis=1)


def tile_rows(columns, planes, tiles_x):
    parts = [
        columns[:, i * LANES:(i + 1) * LANES].reshape(1, tiles_x, 1, SUB, LANES) for i in range(2 * planes)
    ]
    planes_of = [jnp.concatenate(parts[2 * z:2 * z + 2], axis=2) for z in range(planes)]
    return jnp.concatenate(planes_of, axis=0).reshape(planes * tiles_x * TS, LANES)


def route_rows(names, tiles, shares, wanted):
    fanout, count = names.shape
    member = jnp.zeros(wanted.shape, F32)
    weight = jnp.zeros(wanted.shape, F32)
    label = jnp.zeros(wanted.shape, F32)
    for k in range(fanout):
        hit = names[k:k + 1, :] == wanted
        member = member + jnp.where(hit, 1.0, 0.0)
        weight = weight + jnp.where(hit, shares[k:k + 1, :], 0.0)
        label = label + jnp.where(hit, tiles[k:k + 1, :], 0.0)
    return member, weight, label


def ranked(member):
    count = member.shape[1]
    before = lax.broadcasted_iota(jnp.int32, (count, count), 0) < lax.broadcasted_iota(
        jnp.int32, (count, count), 1
    )
    rank = mm(member.astype(BF16), jnp.where(before, 1.0, 0.0).astype(BF16))
    return jnp.where(member > 0.0, rank, 2.0 * count)


def slots_of(rank, weight, label, capacity):
    slot = lax.broadcasted_iota(jnp.int32, (capacity, rank.shape[1]), 0).astype(F32)
    chosen = rank == slot
    return jnp.where(chosen, weight, 0.0), jnp.where(chosen, label, 0.0)


def in_all_lanes(rows):
    return mm(rows.astype(BF16), jnp.ones((rows.shape[1], LANES), BF16))


def place_labels(board, labels, first):
    lane = lax.broadcasted_iota(jnp.int32, board.shape, 1)
    for g in range(labels.shape[0] // SUB):
        board = jnp.where(lane == first + g, labels[g * SUB:(g + 1) * SUB], board)
    return board


def read_labels(board, first, capacity):
    lane = lax.broadcasted_iota(jnp.int32, (SUB, LANES), 1).astype(F32)
    rows = [
        jnp.where(board[:, first + g:first + g + 1] == lane, 1.0, 0.0) for g in range(capacity // SUB)
    ]
    return jnp.concatenate(rows, axis=0)


def ring_order(depth):
    return list(range(0, depth, 2)) + list(range(1, depth, 2))[::-1]


def seat_of(level, depth):
    return jnp.where(level % 2 == 0, level // 2, depth - (level + 1) // 2)


def level_of(seat, steps, depth):
    there = seat - steps
    there = jnp.where(there < 0, there + depth, there)
    return jnp.where(2 * there < depth, 2 * there, 2 * (depth - there) - 1)


def columns_wanted(shape, depth, inner, seat, steps):
    row = lax.broadcasted_iota(jnp.int32, shape, 0)
    column, steps = (row // depth, row % depth) if steps is None else (row, steps)
    level = level_of(seat, steps, depth)
    return (column // inner * (depth * inner) + level * inner + column % inner).astype(F32)


def ring_kernel(planes_a, source, routes, ring, tiled):
    planes, cells_x, _ = source.shape
    half = planes_a * cells_x
    fanout = routes.shape[1]
    ring[:half, :] = swap_blocks(source[:planes_a].reshape(half, LANES))
    ring[half:, :] = jnp.zeros((3 * SUB, LANES), F32)
    ring[half:half + fanout, :] = routes[0]
    ring[half + SUB:half + SUB + fanout, :] = routes[1]
    ring[half + 2 * SUB:half + 2 * SUB + fanout, :] = routes[2] / jnp.sum(routes[2], axis=0, keepdims=True)
    tiled[...] = swap_blocks(source[planes_a:].reshape(tiled.shape[0], LANES))


def start_kernel(capacity, columns, depth, inner, planes_a, fanout, at, ring, tiled, far, out, gone):
    cells_x = (ring.shape[0] - 3 * SUB) // planes_a
    rest = tiled.shape[0] // cells_x
    names, tiles, shares = routing(ring, fanout)
    wanted = columns_wanted((columns * depth, LANES), depth, inner, at[3], None)
    member, weight, label = route_rows(names, tiles, shares, wanted)
    rank = ranked(member)
    cells = tile_columns(tiled[...], rest, cells_x // TS)
    slots = depth * capacity
    step = columns // gone.shape[0]
    copies = []
    for first in range(0, columns, step):
        picked, named = [], []
        for n in range(first * depth, (first + step) * depth):
            rows, labels = slots_of(rank[n:n + 1], weight[n:n + 1], label[n:n + 1], capacity)
            picked.append(rows)
            named.append(labels)
        packed = dot3(stacked(*picked), cells)
        named = in_all_lanes(stacked(*named))
        put(out.at[first:first + step], packed.reshape(step, slots, packed.shape[1]))
        for j in range(step):
            board = jnp.zeros((SUB, LANES), F32)
            out[first + j, out.shape[1] - SUB:, :] = place_labels(board, named[j * slots:(j + 1) * slots], 0)
        there = slice(first, first + step)
        copies.append(pltpu.make_async_copy(out.at[there], far.at[there], gone.at[first // step]))
        copies[-1].start()
    for copy in copies:
        copy.wait()


def put(out, slots, first=0, size=None):
    count = slots.shape[1]
    size = count if size is None else size
    for c in range(slots.shape[2] // LANES):
        out[:, c * size + first:c * size + first + count, :] = slots[:, :, c * LANES:(c + 1) * LANES]


def routing(ring, fanout):
    first = ring.shape[0] - 3 * SUB
    return [ring[first + k * SUB:first + k * SUB + fanout, :] for k in range(3)]


def pack(capacity, columns, depth, inner, fanout, seat, rings, picked, pack_out, boards, first, size):
    wanted = columns_wanted((columns, LANES), depth, inner, seat, 0)
    for s, ring in enumerate(rings):
        half = ring.shape[0] - 3 * SUB
        member, weight, label = route_rows(*routing(ring, fanout), wanted)
        rank = ranked(member)
        named = []
        for j in range(columns):
            rows, labels = slots_of(rank[j:j + 1], weight[j:j + 1], label[j:j + 1], capacity)
            picked[j * capacity:(j + 1) * capacity, :] = rows
            named.append(labels)
        named = in_all_lanes(stacked(*named))
        for j in range(columns):
            labels = named[j * capacity:(j + 1) * capacity]
            boards[j] = place_labels(boards[j], labels, (first + s) * (capacity // SUB))
        planes = pack_out.shape[1] // size // 2
        cells = tile_columns(ring[:half, :], planes, half // planes // TS)
        packed = dot3(picked[...], cells)
        put(pack_out, packed.reshape(columns, capacity, packed.shape[1]), s * capacity, size)
    return boards


def send(pairs, gone):
    copies = [pltpu.make_async_copy(near, far, gone.at[i]) for i, (near, far) in enumerate(pairs)]
    for copy in copies:
        copy.start()
    for copy in copies:
        copy.wait()


def early_kernel(capacity, columns, depth, inner, fanout, total, at, *refs):
    rings, (far, boards_out, picked, out, gone) = refs[:-5], refs[-5:]
    size = len(rings) * capacity
    boards = [jnp.zeros((SUB, LANES), F32) for _ in range(columns)]
    boards = pack(capacity, columns, depth, inner, fanout, at[3], rings, picked, out, boards, 0, size)
    for j in range(columns):
        boards_out[j] = boards[j]
    send(
        [
            (out.at[:, c * size:(c + 1) * size], far.at[:, c * total:c * total + size])
            for c in range(out.shape[1] // size)
        ],
        gone,
    )


def forward_kernel(capacity, columns, depth, inner, fanout, total, at, far_in, boards_in, ring, *refs):
    edges, (far, picked, out, tail, gone) = refs[:-5], refs[-5:]
    del far_in
    boards = [boards_in[j] for j in range(columns)]
    boards = pack(
        capacity, columns, depth, inner, fanout, at[3], [ring], picked, out, boards, total // capacity - 1, capacity
    )
    for j in range(columns):
        tail[j, :SUB, :] = boards[j]
    value = edges[0][...]
    for part in edges[1:]:
        value = value + part[...]
    tail[:, SUB:, :] = value
    parts = out.shape[1] // capacity
    send(
        [
            (out.at[:, c * capacity:(c + 1) * capacity], far.at[:, (c + 1) * total - capacity:(c + 1) * total])
            for c in range(parts)
        ] + [(tail, far.at[:, parts * total:])],
        gone,
    )


def gather_sum(arrived, capacity, groups, total, parts):
    heads, cells = [], []
    for j in range(arrived.shape[0]):
        board = arrived[j, parts * total:parts * total + SUB, :]
        for g in groups:
            heads.append(read_labels(board, g * (capacity // SUB), capacity))
            first = g * capacity
            cells.append(beside(*[
                arrived[j, c * total + first:c * total + first + capacity, :] for c in range(parts)
            ]))
    head = stacked(*heads).astype(BF16)
    high, low = split(stacked(*cells))
    return mm_t(head, high) + mm_t(head, low)


def partial_kernel(capacity, depth, groups, far, *refs):
    outs, (boards, cells, here) = refs[:-3], refs[-3:]
    slots, parts = depth * capacity, outs[0].shape[1] // LANES
    pairs = [(far.at[:, parts * slots:parts * slots + SUB], boards)]
    for i, r in enumerate(groups):
        for c in range(parts):
            first = c * slots + r * capacity
            pairs.append((far.at[:, first:first + capacity], cells.at[i, c]))
    copies = [pltpu.make_async_copy(a, b, here.at[i]) for i, (a, b) in enumerate(pairs)]
    for copy in copies:
        copy.start()
    copies[0].wait()
    for i, (r, out) in enumerate(zip(groups, outs)):
        for copy in copies[1 + i * parts:1 + (i + 1) * parts]:
            copy.wait()
        heads, values = [], []
        for j in range(boards.shape[0]):
            heads.append(read_labels(boards[j], r * (capacity // SUB), capacity))
            values.append(beside(*[cells[i, c, j] for c in range(parts)]))
        head = stacked(*heads).astype(BF16)
        high, low = split(stacked(*values))
        out[...] = mm_t(head, high) + mm_t(head, low)


def edge_sums(proj, weight, label, tiles_x, tiles_y, logs, part):
    label = label.astype(jnp.int32)
    tile_x, tile_y = label // tiles_y, label % tiles_y
    place, other, size = (tile_y, tile_x, tiles_x) if part == 0 else (tile_x, tile_y, tiles_y)
    per = tiles_y if part == 0 else tiles_x
    blocks = weight.shape[0]
    proj = proj[:, part * LANES:(part + 1) * LANES]
    owner = lax.broadcasted_iota(jnp.int32, proj.shape, 1) // TS
    row = lax.broadcasted_iota(jnp.int32, (per, weight.shape[1]), 0)
    here = [place[n:n + 1] == row for n in range(blocks)]
    planes = len(logs)
    left, right = [], []
    for kind in range(2):
        gap = (size - 1 - other if kind == 0 else other).astype(F32)
        for z in range(planes):
            value = weight * jnp.exp(gap * (TS * logs[z]))
            left.append(stacked(*[jnp.where(here[n], value[n:n + 1], 0.0) for n in range(blocks)]))
            right.append(jnp.where(owner == kind * planes + z, proj, 0.0))
    return dot3(beside(*left), stacked(*right)).reshape(blocks, per, LANES)


def own_edges(proj, tiles_x, tiles_y, logs):
    lane = lax.broadcasted_iota(jnp.int32, (SUB, LANES), 1) // TS
    sub = lax.broadcasted_iota(jnp.int32, (SUB, LANES), 0)
    planes = len(logs)
    rate = jnp.zeros((SUB, LANES), F32)
    for z in range(planes):
        rate = jnp.where(lane % planes == z, TS * logs[z], rate)
    to_end = lane < planes
    near = jnp.exp(jnp.where(to_end, tiles_y - 1 - sub, sub).astype(F32) * rate)
    along_x, along_y = jnp.zeros((SUB, LANES), F32), []
    for i in range(tiles_x):
        rows = proj[i * tiles_y:(i + 1) * tiles_y]
        steps = jnp.where(to_end, tiles_x - 1 - i, i).astype(F32)
        along_x = along_x + rows[:, :LANES] * jnp.exp(steps * rate)
        along_y.append(jnp.sum(rows[:, LANES:] * near, axis=0, keepdims=True))
    return along_x[None], stacked(*along_y)[None]


def line_carries(ends, starts, across, first):
    forward, full, running = [], [], jnp.zeros_like(ends[0])
    for end, start in zip(ends, starts):
        forward.append(running)
        full.append(start + first * running)
        running = across * running + end
    backward, running = [], jnp.zeros_like(ends[0])
    for start in full[::-1]:
        backward.append(running)
        running = across * running + start
    return forward, backward[::-1]


def end_start(both, gain, back):
    half = both.shape[1] // 2
    end = both[:, :half]
    return end, gain[:half] * both[:, half:] - back[:half] * end


def edge_kernel(grid_x, depth, inner, planes, fanout, at, logs_in, target, table, lines, coef, both_x, ring, tiled,
                *refs):
    outs, carries = refs[:-1], refs[-1]
    _, cells_x, cells_y = target.shape
    tiles_x, tiles_y = cells_x // TS, cells_y // TS
    half = ring.shape[0] - 3 * SUB
    planes_a = half // cells_x
    logs = [logs_in[z] for z in range(planes)]
    names, tiles, shares = routing(ring, fanout)
    cells = [tile_columns(ring[:half, :], planes_a, tiles_x), tile_columns(tiled[...], planes - planes_a, tiles_x)]
    cells = beside(*cells)
    own_cells = tile_columns(swap_blocks(target[...].reshape(planes * cells_x, LANES)), planes, tiles_x)
    proj = dot3(stacked(cells, own_cells), table[...])
    own = own_edges(proj[cells.shape[0]:], tiles_x, tiles_y, logs)
    proj = proj[:cells.shape[0]]
    tile_count = names.shape[1]
    along = depth * inner
    blocks = grid_x * along
    wanted = lax.broadcasted_iota(jnp.int32, (blocks, tile_count), 0).astype(F32)
    _, weight, label = route_rows(names, tiles, shares, wanted)
    here = at[0] * along + at[1] * inner + at[2]
    edges = []
    for part in range(2):
        sums = edge_sums(proj, weight, label, tiles_x, tiles_y, logs, part)
        is_here = lax.broadcasted_iota(jnp.int32, sums.shape, 0) == here
        sums = jnp.where(is_here, own[part], 0.0) - sums
        edges.append(swap_blocks(sums.reshape(-1, LANES)).reshape(blocks, sums.shape[1] // SUB, SUB, LANES))
    gain, across_x, first_x, back_x, across_y, first_y, back_y = [coef[i][:, :1] for i in range(7)]

    ends, starts = zip(*[
        end_start(edges[0][p * along:(p + 1) * along, 0], gain, back_x) for p in range(grid_x)
    ])
    forward, backward = line_carries(ends, starts, across_x[:planes], first_x[:planes])
    for p in range(grid_x):
        rows = jnp.concatenate([forward[p], backward[p]], axis=1).reshape(depth, inner, SUB, LANES)
        carries[:, p * inner:(p + 1) * inner, :SUB, :] = rows

    side = jnp.concatenate([edges[1][:, i] for i in range(edges[1].shape[1])], axis=2)
    flat = side.reshape(blocks * SUB, cells_x)
    local = jnp.zeros_like(flat)
    for z in range(planes):
        local = local + dot3(masked(flat, planes, z), both_x[z])
    local = local.reshape(side.shape)
    ends = jnp.sum(side * lines[0], axis=2, keepdims=True)
    starts = jnp.sum(side * lines[1], axis=2, keepdims=True)
    forward, backward = line_carries(
        [ends[p * along:(p + 1) * along] for p in range(grid_x)],
        [starts[p * along:(p + 1) * along] for p in range(grid_x)],
        across_x,
        first_x,
    )
    smooth = [
        local[p * along:(p + 1) * along] + forward[p] * lines[2] + backward[p] * lines[3] for p in range(grid_x)
    ]
    smooth = jnp.stack(smooth)
    ends, starts = zip(*[end_start(smooth[:, q], gain, back_y) for q in range(along)])
    forward, backward = line_carries(ends, starts, across_y[:planes], first_y[:planes])
    for q in range(along):
        rows = jnp.concatenate([forward[q], backward[q]], axis=1)
        for p in range(grid_x):
            for i in range(cells_x // LANES):
                carries[q // inner, p * inner + q % inner, (1 + i) * SUB:(2 + i) * SUB, :] = (
                    rows[p, :, i * LANES:(i + 1) * LANES]
                )
    for o, out in enumerate(outs):
        out[...] = carries[lax.rem(at[1] + o, depth)]


def masked(rows, planes, z):
    row = lax.broadcasted_iota(jnp.int32, rows.shape, 0)
    return jnp.where(row % planes == z, rows, 0.0)


def outer(a, b):
    a_high, a_low = split(a)
    b_high, b_low = split(b)
    return mm_t(stacked(a_high, a_high, a_low), stacked(b_high, b_low, b_high))


def base_kernel(target, potential, both_x, both_y, out):
    for z in range(target.shape[0]):
        out[z] = potential[z] + dot3(dot3(both_x[z], target[z]), both_y[z])


def solve(pushed, before, both_x, both_y):
    return before - dot3(dot3(both_x, pushed), both_y)


def out_copies(near, far, gone, planes, first):
    return [
        pltpu.make_async_copy(near.at[z], far.at[first + z], gone.at[z]) for z in range(planes)
    ]


def near_kernel(capacity, depth, arrived, base_far, both_x, both_y, curve_x, curve_y, pushed_far, next_far, rest_out,
                pushed_out, next_out, pushed_gone, next_gone, base, base_here):
    del base_far
    fetched = pltpu.make_async_copy(next_far, base, base_here)
    fetched.start()
    planes, planes_a = base.shape[0], pushed_out.shape[0]
    cells_x = pushed_out.shape[1]
    total, parts = depth * capacity, 2 * planes_a
    first = parts * total + SUB
    carries = arrived[0, first:, :]
    for j in range(1, arrived.shape[0]):
        carries = carries + arrived[j, first:, :]
    carry_x = carries[:SUB]
    carry_y = beside(*[carries[i:i + SUB] for i in range(SUB, carries.shape[0], SUB)])
    total = gather_sum(arrived, capacity, list(range(depth)), total, parts)
    pushed_out[...] = swap_blocks(tile_rows(total, planes_a, cells_x // TS)).reshape(planes_a, cells_x, LANES)
    copies = out_copies(pushed_out, pushed_far, pushed_gone, planes_a, 0)
    copies += out_copies(next_out, next_far, next_gone, planes_a, 0)
    for copy in copies[:planes_a]:
        copy.start()
    fetched.wait()
    for z in range(planes):
        left = stacked(masked(curve_x[...], planes, z), masked(carry_y, planes, z))
        right = stacked(dot3(carry_x, both_y[z]), curve_y[...])
        before = base[z] + outer(left, right)
        if z < planes_a:
            next_out[z] = solve(pushed_out[z], before, both_x[z], both_y[z])
            copies[planes_a + z].start()
        else:
            rest_out[z - planes_a] = before
    for copy in copies:
        copy.wait()


def far_kernel(first, pushed_in, next_in, base, both_x, both_y, *refs):
    del pushed_in, next_in
    sums, (pushed_far, next_far, pushed_out, next_out, pushed_gone, next_gone) = refs[:-6], refs[-6:]
    count, cells_x, _ = pushed_out.shape
    total = sums[0][...]
    for part in sums[1:]:
        total = total + part[...]
    pushed_out[...] = swap_blocks(tile_rows(total, count, cells_x // TS)).reshape(count, cells_x, LANES)
    copies = out_copies(pushed_out, pushed_far, pushed_gone, count, first)
    copies += out_copies(next_out, next_far, next_gone, count, first)
    for copy in copies[:count]:
        copy.start()
    for z in range(count):
        next_out[z] = solve(pushed_out[z], base[z], both_x[first + z], both_y[first + z])
        copies[count + z].start()
    for copy in copies:
        copy.wait()


def call(name, body, out_shape, in_specs=None, scratch=(), wait=(), **extra):
    def run(*args):
        count, unread = len(args), len(wait)

        def kernel(*refs):
            body(*refs[:count], *refs[count + unread:])

        near = pl.BlockSpec(memory_space=pltpu.VMEM)
        specs = [near] * count if in_specs is None else list(in_specs)
        return pl.pallas_call(
            kernel,
            out_shape=out_shape,
            in_specs=specs + [pl.BlockSpec(memory_space=pl.ANY)] * unread,
            scratch_shapes=list(scratch),
            compiler_params=pltpu.CompilerParams(vmem_limit_bytes=VMEM_LIMIT),
            cost_estimate=pl.CostEstimate(
                flops=int(COST[name] * FLOPS_A_MICRO), bytes_accessed=0, transcendentals=0
            ),
            **extra,
        )(*args, *wait)

    return run


def table_kernel(planes, decay_in, logs_in, table, lines, coef, curve_x, curve_y, both_x, both_y):
    row = lax.broadcasted_iota(jnp.int32, (2 * planes, LANES), 0)
    decay, rate = jnp.zeros(row.shape, F32), jnp.zeros(row.shape, F32)
    for z in range(planes):
        decay = jnp.where(row % planes == z, decay_in[z], decay)
        rate = jnp.where(row % planes == z, logs_in[z], rate)
    gain = (1.0 - decay) / (1.0 + decay)
    coef[0] = gain
    for i, (curve, both) in enumerate(((curve_x, both_x), (curve_y, both_y))):
        length = curve.shape[1]
        across = jnp.exp(length * rate)
        coef[1 + 3 * i] = across
        coef[2 + 3 * i] = gain * decay * (1.0 - across * across)
        coef[3 + 3 * i] = gain * decay * across
        slope, width, turn = rate[:, :1], gain[:, :1], (gain * decay)[:, :1]
        place = lax.broadcasted_iota(jnp.int32, curve.shape, 1).astype(F32)
        risen = jnp.exp(place * slope) - jnp.exp((2.0 * length - place) * slope)
        fall = jnp.exp((length - place) * slope)
        bend = turn * risen
        curve[...] = jnp.where(lax.broadcasted_iota(jnp.int32, curve.shape, 0) < planes, bend, fall)
        if i == 0:
            lines[0] = jnp.exp((length - 1.0 - place) * slope)
            lines[1] = width * risen
            lines[2] = bend
            lines[3] = fall
        rows = lax.broadcasted_iota(jnp.int32, (length, length), 0).astype(F32)
        cols = lax.broadcasted_iota(jnp.int32, (length, length), 1).astype(F32)
        apart, down = jnp.abs(rows - cols), length - rows[:, :1]
        for z in range(planes):
            log = logs_in[z]
            both[z] = width[z:z + 1] * (jnp.exp(apart * log) - jnp.exp(down * log) * fall[z:z + 1])
    cells = TS * TS
    shape = (cells, table.shape[1])
    row, col = lax.broadcasted_iota(jnp.int32, shape, 0), lax.broadcasted_iota(jnp.int32, shape, 1)
    along_y, kind = col // (2 * planes * TS) == 1, col // (planes * TS) % 2
    owner, cell = col // TS % planes, col % TS
    at_x, at_y = row // TS, row % TS
    summed, kept = jnp.where(along_y, at_y, at_x), jnp.where(along_y, at_x, at_y)
    steps = jnp.where(kind == 0, TS - 1 - summed, summed).astype(F32)
    for z in range(planes):
        power = jnp.exp(steps * logs_in[z])
        table[z * cells:(z + 1) * cells, :] = jnp.where((owner == z) & (kept == cell), power, 0.0)


def per_device(source_mass, target_density, potential, dest_device, dest_tile, mass_counts, reach):
    planes, cells_x, cells_y = source_mass.shape
    tile_count, fanout = dest_device.shape[2:]
    tiles_x, tiles_y = cells_x // TS, cells_y // TS
    grid_x, depth, inner = lax.axis_size("gx"), lax.axis_size("z"), lax.axis_size("x")
    columns = grid_x * inner
    device_count = columns * depth
    capacity = max(2, 3 * fanout * tile_count // (2 * device_count))
    capacity = -(-capacity // SUB) * SUB
    slots = depth * capacity
    planes_a = planes // 2
    rest = planes - planes_a
    tile_cells = 2 * LANES
    level = lax.axis_index("z")
    at = jnp.stack([lax.axis_index("gx"), level, lax.axis_index("x"), seat_of(level, depth)])
    scalars, near = pl.BlockSpec(memory_space=pltpu.SMEM), pl.BlockSpec(memory_space=pltpu.VMEM)
    far = pl.BlockSpec(memory_space=pl.ANY)

    def array(*shape):
        return jax.ShapeDtypeStruct(shape, F32)

    seats = ring_order(depth)

    def turn(x, steps):
        return lax.ppermute(x, "z", [(seats[i], seats[(i + steps) % depth]) for i in range(depth)])

    def step(x, steps):
        return lax.ppermute(x, "z", [(i, (i + steps) % depth) for i in range(depth)])

    routes = jnp.stack([x.reshape(tile_count, fanout).T for x in (dest_device, dest_tile, mass_counts)])
    ring, tiled = call(
        "ring", functools.partial(ring_kernel, planes_a),
        [array(planes_a * cells_x + 3 * SUB, LANES), array(rest * cells_x, LANES)],
    )(source_mass, routes.astype(F32))
    rings = [ring] + [None] * (depth - 1)
    for s in range(1, depth // 2 + 1):
        rings[s] = step(rings[s - 1], 1)
        if s < depth - s:
            rings[depth - s] = step(rings[(depth - s + 1) % depth], -1)

    packed_b = call(
        "start", functools.partial(start_kernel, capacity, columns, depth, inner, planes_a, fanout),
        array(columns, 2 * rest * slots + SUB, LANES),
        [scalars] + [near] * 2,
        [
            pltpu.VMEM((columns, 2 * rest * slots + SUB, LANES), F32),
            pltpu.SemaphoreType.DMA((CHUNKS if columns % CHUNKS == 0 else 1,)),
        ],
        out_specs=far,
    )(at, ring, tiled)
    arrived_b = lax.all_to_all(packed_b, ("gx", "x"), 0, 0, tiled=True)
    decay = 1.0 - 1.0 / reach
    logs = jnp.log(decay)
    eight = 2 * planes
    table, lines, coef, curve_x, curve_y, both_x, both_y = call(
        "table", functools.partial(table_kernel, planes),
        [
            array(planes * TS * TS, 4 * planes * TS), array(4, eight, cells_x), array(7, eight, LANES),
            array(eight, cells_x), array(eight, cells_y), array(planes, cells_x, cells_x),
            array(planes, cells_y, cells_y),
        ],
        [scalars] * 2,
        (),
        [ring],
    )(decay, logs)
    edge_rows = tiles_x + tiles_y
    edges = call(
        "edge", functools.partial(edge_kernel, grid_x, depth, inner, planes, fanout),
        [array(columns, edge_rows, LANES)] * depth,
        [scalars] * 2 + [near] * 7,
        [pltpu.VMEM((depth, columns, edge_rows, LANES), F32)],
        [rings[1], packed_b],
    )(at, logs, target_density, table, lines, coef, both_x, ring, tiled)
    edges = [edges[0]] + [step(edges[o], o) for o in range(1, depth)]
    sums = {}
    for groups in [[depth // 2], [r for r in range(depth) if r != depth // 2]]:
        parts = 2 * rest
        some = call(
            "partial", functools.partial(partial_kernel, capacity, depth, groups),
            [array(tile_count, rest * tile_cells)] * len(groups),
            [far],
            [
                pltpu.VMEM((columns, SUB, LANES), F32),
                pltpu.VMEM((len(groups), parts, columns, capacity, LANES), F32),
                pltpu.SemaphoreType.DMA((1 + len(groups) * parts,)),
            ],
        )(arrived_b)
        sums.update(zip(groups, some))
    moving = {r: sums[r] for r in range(depth)}
    for r in range(depth // 2, 0, -1):
        moving[r - 1] = turn(moving[r], -1) if r == 1 else moving[r - 1] + turn(moving[r], -1)
    moving = [sums[0], moving[0]]
    if depth > 2:
        more = sums[depth // 2 + 1]
        for r in range(depth // 2 + 1, depth):
            more = turn(more, 1)
            if r < depth - 1:
                more = more + sums[r + 1]
        moving.append(more)
    last = depth // 2
    order = [s for s in range(depth) if s != last]
    parts = 2 * planes_a
    packed_a, boards = call(
        "early", functools.partial(early_kernel, capacity, columns, depth, inner, fanout, slots),
        [array(columns, parts * slots + SUB + edge_rows, LANES), array(columns, SUB, LANES)],
        [scalars] + [near] * len(order),
        [
            pltpu.VMEM((columns * capacity, tile_count), F32),
            pltpu.VMEM((columns, parts * (slots - capacity), LANES), F32),
            pltpu.SemaphoreType.DMA((parts,)),
        ],
        out_specs=[far, near],
    )(at, *[rings[s] for s in order])
    packed_a = call(
        "pack", functools.partial(forward_kernel, capacity, columns, depth, inner, fanout, slots),
        array(*packed_a.shape), [scalars, far] + [near] * (2 + len(edges)),
        [
            pltpu.VMEM((columns * capacity, tile_count), F32), pltpu.VMEM((columns, parts * capacity, LANES), F32),
            pltpu.VMEM((columns, SUB + edge_rows, LANES), F32), pltpu.SemaphoreType.DMA((parts + 1,)),
        ],
        out_specs=far, input_output_aliases={1: 0},
    )(at, packed_a, boards, rings[last], *edges)
    arrived_a = lax.all_to_all(packed_a, ("gx", "x"), 0, 0, tiled=True)
    base = call("base", base_kernel, array(*potential.shape), wait=[sums[0]])(
        target_density, potential, both_x, both_y
    )
    shapes = [array(*source_mass.shape), array(*potential.shape)]

    def staged(count):
        return [pltpu.VMEM((count, cells_x, cells_y), F32)] * 2 + [pltpu.SemaphoreType.DMA((count,))] * 2

    *outs, base = call(
        "near", functools.partial(near_kernel, capacity, depth), shapes + [array(rest, cells_x, cells_y)],
        [near, far] + [near] * 4, staged(planes_a) + [pltpu.VMEM(potential.shape, F32), pltpu.SemaphoreType.DMA],
        out_specs=[far, far, near], input_output_aliases={1: 1},
    )(arrived_a, base, both_x, both_y, curve_x, curve_y)
    outs = call(
        "far", functools.partial(far_kernel, planes_a), shapes, [far, far] + [near] * (3 + len(moving)),
        staged(rest), out_specs=[far, far], input_output_aliases={0: 0, 1: 1},
    )(*outs, base, both_x, both_y, *moving)
    return tuple(outs)


def solution(mesh):
    grid_x, grid_y = mesh.shape["gx"], mesh.shape["gy"]
    inner = grid_x // 2
    if inner < 1 or grid_y % inner:
        inner = 1
    depth = grid_y // inner
    split_mesh = Mesh(mesh.devices.reshape(grid_x, depth, inner), ("gx", "z", "x"))
    field = P(None, "gx", ("z", "x"))
    table = P("gx", ("z", "x"), None, None)
    return jax.shard_map(
        per_device,
        mesh=split_mesh,
        in_specs=(field, field, field, table, table, table, P()),
        out_specs=(field, field),
        check_vma=False,
    )
```
